32 devices in a mesh: gx: 8 (over z, x), yz: 4 (over y, core).
Axes of the slice: x: 2, y: 2, z: 4, core: 2. Of those that a mesh axis runs over, the one named last changes fastest.
Arguments:
- coarse_state: float32 [21, 48, 24, 384], P(None, 'gx', 'yz')
- fine_state: bfloat16 [128, 21, 512], P(('gx', 'yz')), may hold values from -6 to 6
- diffusion: float32 [21], replicated, may hold values from 0.005 to 0.04
- rate: float32 [21, 21], replicated, may hold values from -0.625 to 0.625
- box_pos: int32 [8, 4, 2], P('gx', 'yz'), may hold values from 0 to 63, as said below
- box_owner: int32 [8, 4, 2], P('gx', 'yz'), may hold values from 0 to 3, as said below
Outputs:
- coarse_next: float32 [21, 48, 24, 384], P(None, 'gx', 'yz')
- fine_next: bfloat16 [128, 21, 512], P(('gx', 'yz'))
The draws below stay inside these ranges and needn't reach their ends.
Inputs may be any that keep to these rules, and one draw needn't show every extreme that they name: `box_pos`: the 2 positions of one device are distinct. `box_owner`: the 2 boxes of one device go to distinct owners of its slab; in every slab some owner receives a box from every device of the slab.
All inputs are finite; a program needn't handle non-finite values.
Results may differ from the reference program's by a relative error of at most 0.0025.
Values may be sent and summed in bfloat16 or wider, within the bound.
No kernel may reach another device: no remote copies, remote signals or barrier semaphores. Data moves between devices by JAX's collectives and lax.ppermute only.
A program may use at most 64 MiB of HBM per device.

```python
import math
import jax
import jax.numpy as jnp
from jax import lax

S = 21
PZ = 64
CX = 6
NX = 48
NY = 24
NZ = 384
HB = 2
FC = 512
SLOTS = 128
N_GX = 8
N_YZ = 4


def draw_coarse_state(key, part):
    key = jax.random.fold_in(key, 5)
    first = jax.random.fold_in(key, 0)
    return jax.random.normal(first, (S, NX, NY, NZ), jnp.float32)


def draw_box_pos(key, part):
    key = jax.random.fold_in(key, 11)
    keys = jax.random.split(key, N_GX * N_YZ)
    picks = jax.vmap(lambda k: jax.random.permutation(k, PZ)[:HB])(keys)
    return picks.reshape(N_GX, N_YZ, HB).astype(jnp.int32)


def owner_row(key, hot):
    first, second = jax.random.split(key)
    others = (hot + 1 + jax.random.permutation(first, N_YZ - 1)[:HB - 1]) % N_YZ
    row = jnp.concatenate([hot[None], others.astype(jnp.int32)])
    return row[jax.random.permutation(second, HB)]


def draw_box_owner(key, part):
    key = jax.random.fold_in(key, 12)
    first, second = jax.random.split(key)
    hot = jax.random.randint(first, (N_GX,), 0, N_YZ).astype(jnp.int32)
    keys = jax.random.split(second, N_GX * N_YZ)
    hots = jnp.repeat(hot, N_YZ)
    rows = jax.vmap(owner_row)(keys, hots)
    return rows.reshape(N_GX, N_YZ, HB).astype(jnp.int32)


def steps_of(key, shape, cuts, low, largest):
    loudness = 1.0
    for axis_at, blocks in cuts:
        steps = jax.random.uniform(jax.random.fold_in(jax.random.fold_in(key, 6), axis_at), (blocks,), jnp.float32, low / len(cuts), largest / len(cuts))
        loudness = loudness * jnp.repeat(jnp.exp(steps), shape[axis_at] // blocks).reshape((-1,) + (1,) * (len(shape) - 1 - axis_at))
    return loudness


def gaussian(own_key, extent, width, bound, shards=(), kind=jnp.bfloat16):
    loudness = steps_of(own_key, extent, shards, -0.22, 0.18) if shards else 1.0
    values = jax.random.normal(own_key, extent, jnp.float32) * width * loudness
    return jnp.minimum(jnp.maximum(values, -bound), bound).astype(kind)


def setup_inputs(seed: int = 0) -> dict:
    streams_of = jax.random.split(jax.random.key(seed), 7)
    coarse_state = draw_coarse_state(jax.random.fold_in(streams_of[6], 71), 0)
    fine_state = gaussian(streams_of[1], (SLOTS, S, FC), 1.0, 6.0, ((0, 32),))
    diffusion = jnp.clip(jnp.exp(jax.random.uniform(streams_of[2], (S,), jnp.float32, math.log(0.005), math.log(0.04))), 0.005, 0.04)
    rate = gaussian(streams_of[3], (S, S), (4 * S) ** -0.5, 0.625, (), jnp.float32)
    box_pos = draw_box_pos(jax.random.fold_in(streams_of[6], 71), 0)
    box_owner = draw_box_owner(jax.random.fold_in(streams_of[6], 71), 0)
    return {"coarse_state": coarse_state, "fine_state": fine_state, "diffusion": diffusion, "rate": rate, "box_pos": box_pos, "box_owner": box_owner}


def react(rate, field):
    return jnp.einsum("st,txyz->sxyz", rate, field, precision=lax.Precision.HIGHEST)


def cycle_faces(patch):
    return jnp.stack([patch[:, 0, 1:-1, 1:-1], patch[:, -1, 1:-1, 1:-1], patch[:, 1:-1, 0, 1:-1], patch[:, 1:-1, -1, 1:-1], patch[:, 1:-1, 1:-1, 0], patch[:, 1:-1, 1:-1, -1]], axis=1)


def inner_faces(patch):
    return jnp.stack([patch[:, 1, 1:-1, 1:-1], patch[:, -2, 1:-1, 1:-1], patch[:, 1:-1, 1, 1:-1], patch[:, 1:-1, -2, 1:-1], patch[:, 1:-1, 1:-1, 1], patch[:, 1:-1, 1:-1, -2]], axis=1)


def widen(face):
    return jnp.repeat(jnp.repeat(face, 2, axis=1), 2, axis=2)


def fine_box(fine, ghost_old, ghost_new, diffusion, rate):
    species = fine.shape[0]
    half = ghost_old.shape[2]
    edge = 2 * half
    field = fine.reshape(species, edge, edge, edge)
    coef = diffusion[:, None, None, None]
    flux_sum = jnp.zeros_like(ghost_old)
    for sub in range(2):
        ghost = ghost_old if sub == 0 else 0.5 * (ghost_old + ghost_new)
        padded = jnp.pad(field, ((0, 0), (1, 1), (1, 1), (1, 1)))
        padded = padded.at[:, 0, 1:-1, 1:-1].set(widen(ghost[:, 0]))
        padded = padded.at[:, -1, 1:-1, 1:-1].set(widen(ghost[:, 1]))
        padded = padded.at[:, 1:-1, 0, 1:-1].set(widen(ghost[:, 2]))
        padded = padded.at[:, 1:-1, -1, 1:-1].set(widen(ghost[:, 3]))
        padded = padded.at[:, 1:-1, 1:-1, 0].set(widen(ghost[:, 4]))
        padded = padded.at[:, 1:-1, 1:-1, -1].set(widen(ghost[:, 5]))
        lap = padded[:, 2:, 1:-1, 1:-1] + padded[:, :-2, 1:-1, 1:-1]
        lap = lap + padded[:, 1:-1, 2:, 1:-1] + padded[:, 1:-1, :-2, 1:-1]
        lap = lap + padded[:, 1:-1, 1:-1, 2:] + padded[:, 1:-1, 1:-1, :-2] - 6.0 * field
        bounds = jnp.stack([field[:, 0], field[:, -1], field[:, :, 0], field[:, :, -1], field[:, :, :, 0], field[:, :, :, -1]], axis=1)
        pooled = bounds.reshape(species, 6, half, 2, half, 2).sum(axis=(3, 5))
        flux_sum = flux_sum + coef * (ghost - 0.25 * pooled)
        field = field + 2.0 * coef * lap + 0.5 * react(rate, field)
    average = field.reshape(species, half, 2, half, 2, half, 2).mean(axis=(2, 4, 6))
    return field.reshape(species, edge * edge * edge), flux_sum, average


def correct(patch_new, patch_old, flux_sum, average, diffusion):
    fix = diffusion[:, None, None, None] * (cycle_faces(patch_old) - inner_faces(patch_old)) - flux_sum
    out = patch_new.at[:, 0, 1:-1, 1:-1].add(fix[:, 0])
    out = out.at[:, -1, 1:-1, 1:-1].add(fix[:, 1])
    out = out.at[:, 1:-1, 0, 1:-1].add(fix[:, 2])
    out = out.at[:, 1:-1, -1, 1:-1].add(fix[:, 3])
    out = out.at[:, 1:-1, 1:-1, 0].add(fix[:, 4])
    out = out.at[:, 1:-1, 1:-1, -1].add(fix[:, 5])
    return out.at[:, 1:-1, 1:-1, 1:-1].set(average)


def reference(coarse_state, fine_state, diffusion, rate, box_pos, box_owner):
    coef = diffusion[:, None, None, None]
    lap = jnp.roll(coarse_state, 1, 1) + jnp.roll(coarse_state, -1, 1)
    lap = lap + jnp.roll(coarse_state, 1, 2) + jnp.roll(coarse_state, -1, 2)
    lap = lap + jnp.roll(coarse_state, 1, 3) + jnp.roll(coarse_state, -1, 3) - 6.0 * coarse_state
    advanced = coarse_state + coef * lap + react(rate, coarse_state)
    zero = jnp.zeros((), jnp.int32)

    def visit(carry, index):
        corrected, fine_out = carry
        slab = (index // (N_YZ * HB)).astype(jnp.int32)
        host = ((index // HB) % N_YZ).astype(jnp.int32)
        which = (index % HB).astype(jnp.int32)
        place = box_pos[slab, host, which].astype(jnp.int32)
        owner = box_owner[slab, host, which].astype(jnp.int32)
        corner = (zero, (slab * CX).astype(jnp.int32), (host * CX).astype(jnp.int32), (place * CX).astype(jnp.int32))
        old = lax.dynamic_slice(coarse_state, corner, (S, CX, CX, CX))
        new = lax.dynamic_slice(advanced, corner, (S, CX, CX, CX))
        slot = ((slab * N_YZ + owner) * N_YZ + host).astype(jnp.int32)
        fine = lax.dynamic_index_in_dim(fine_state, slot, 0, keepdims=False).astype(jnp.float32)
        field, flux_sum, average = fine_box(fine, cycle_faces(old), cycle_faces(new), diffusion, rate)
        corrected = lax.dynamic_update_slice(corrected, correct(new, old, flux_sum, average, diffusion), corner)
        fine_out = lax.dynamic_update_slice(fine_out, field.astype(jnp.bfloat16)[None], (slot, zero, zero))
        return (corrected, fine_out), None

    start = (advanced, jnp.zeros((SLOTS, S, FC), jnp.bfloat16))
    (coarse_next, fine_next), _ = lax.scan(visit, start, jnp.arange(N_GX * N_YZ * HB, dtype=jnp.int32))
    return coarse_next, fine_next
```

```python
import functools

import jax
import jax.numpy as jnp
import numpy as np
from jax import lax
from jax.experimental import pallas as pl
from jax.experimental.pallas import tpu as pltpu
from jax.sharding import PartitionSpec as P

F32 = jnp.float32
BF16 = jnp.bfloat16
LIMIT = 12 * 1024 * 1024
PATCH = 256
ORDER = 20_000_000


def padded(count, unit):
    return -(-count // unit) * unit


@functools.lru_cache(maxsize=None)
def tables(width, boxes):
    half = width - 2
    edge = 2 * half
    cells = width**3
    lanes = padded(cells, PATCH)
    fine = edge**3
    spread = np.zeros((lanes, fine), np.float32)
    average = np.zeros((fine, lanes), np.float32)
    halo = padded(boxes * 4 * half * half, 128)
    place = np.zeros((halo, lanes), np.float32)

    def cell(x, y, z):
        return (x * width + y) * width + z

    for number in range(6):
        axis, high = divmod(number, 2)
        others = [a for a in range(3) if a != axis]
        for r in range(half):
            for q in range(half):
                at = [0, 0, 0]
                at[axis] = width - 1 if high else 0
                at[others[0]] = r + 1
                at[others[1]] = q + 1
                here = cell(*at)
                for i in range(2):
                    for j in range(2):
                        pos = [0, 0, 0]
                        pos[axis] = edge - 1 if high else 0
                        pos[others[0]] = 2 * r + i
                        pos[others[1]] = 2 * q + j
                        spread[here, (pos[0] * edge + pos[1]) * edge + pos[2]] = 1.0
                if number < 4:
                    for box in range(boxes):
                        place[((box * 4 + number) * half + r) * half + q, here] = 1.0
    for x in range(edge):
        for y in range(edge):
            for z in range(edge):
                average[(x * edge + y) * edge + z, cell(x // 2 + 1, y // 2 + 1, z // 2 + 1)] = 0.125
    return dict(spread=spread, average=average, place=place, ghost=place @ spread)


def column(diffusion, stack):
    species = diffusion.shape[1]
    row = lax.broadcasted_iota(jnp.int32, (stack, species), 0)
    lane = lax.broadcasted_iota(jnp.int32, (stack, species), 1)
    return jnp.sum(jnp.where(row == lane, diffusion[...], 0.0), axis=1, keepdims=True)


def split(value):
    high = value.astype(BF16).astype(F32)
    return high, value - high


def parts(value):
    return jnp.concatenate(split(value), axis=0).astype(BF16)


def dot(a, b):
    return jnp.dot(a, b, preferred_element_type=F32)


def rows_dot(value, table):
    rows = value.shape[0]
    both = dot(parts(value), table)
    return both[:rows] + both[rows:]


GROUP = 5


def mixing(rate, scratch, stack, group):
    species = rate.shape[0]
    size = group * stack
    scratch[...] = jnp.zeros_like(scratch)
    high, low = split(rate[...])
    for b in range(group):
        at = b * stack
        for row, lane, part in ((at, at, high), (at, size + at, high), (size + at, at, low)):
            scratch[row : row + species, lane : lane + species] = part
    return scratch[: 2 * size, : 2 * size].astype(BF16)


def react(mix, fields):
    size = fields.shape[0]
    both = dot(mix, parts(fields))
    return both[:size] + both[size:]


def react_all(mix, fields):
    stack, depth = fields[0].shape
    made = [[] for _ in fields]

    def product(blocks):
        size = len(blocks[0])
        blank = [jnp.zeros_like(blocks[0][0])] * (GROUP - size)
        columns = [jnp.concatenate(block + blank, axis=0) for block in blocks]
        out = react(mix, jnp.concatenate(columns, axis=1))
        lanes = out.shape[1] // len(blocks)
        return [
            [out[b * stack : (b + 1) * stack, n * lanes : (n + 1) * lanes] for b in range(size)]
            for n in range(len(blocks))
        ]

    for lane in range(0, depth, 256):
        if lane + 256 <= depth:
            for at in range(0, len(fields), GROUP):
                block = [f[:, lane : lane + 256] for f in fields[at : at + GROUP]]
                for b, value in enumerate(product([block])[0]):
                    made[at + b].append(value)
        else:
            half = -(-len(fields) // 2)
            blocks = [[f[:, lane:] for f in part] for part in (fields[:half], fields[half:])]
            blocks[1] += [jnp.zeros_like(blocks[0][0])] * (half - len(blocks[1]))
            for n, values in enumerate(product(blocks)):
                for b, value in enumerate(values):
                    if n * half + b < len(fields):
                        made[n * half + b].append(value)
    return [jnp.concatenate(value, axis=1) for value in made]


def lanes_of(stack, lanes=128):
    return lax.broadcasted_iota(jnp.int32, (stack, lanes), 1)


def tiles_of(stack, depth, start, width):
    lane = lanes_of(stack)
    masks = []
    for t in range(depth // 128):
        along = lane + (t * 128 - start)
        masks.append((along >= 0) & (along < width))
    return masks


def fold(value, masks):
    out = value[:, :128]
    for t in range(1, len(masks)):
        out = jnp.where(masks[t], value[:, t * 128 : (t + 1) * 128], out)
    return out


def turn(value, by):
    return pltpu.roll(value, by & 127, 1)


def neighbour(me, count, even_up):
    step = jnp.where((me % 2 == 0) == even_up, 1, count - 1)
    return lax.rem(me + step, count)


def upper():
    return (lax.axis_index("yz") >= lax.axis_size("yz") // 2).astype(jnp.int32)


def layer_rows(width, species, groups=0):
    return padded((width + groups) * species, 16)


def blocks_of(width, species, nz, cells):
    pieces = cells // 128
    across = nz // 128
    places = [((width + n // across) * species, n % across * 128) for n in range(2 * pieces)]
    return places[:pieces], places[pieces:]


def pack_x_kernel(c, fine, first, near_slot, far_slot, own, *refs):
    others, (layer, tmp, held, rows, sem, fine_sem) = refs[:-6], refs[-6:]
    nx, width = c.shape[:2]
    species, count, _ = fine.shape
    stack = padded(species, 8)
    slots = pltpu.make_async_copy(fine, held, fine_sem)
    slots.start()
    copy = pltpu.make_async_copy(c.at[upper() * (nx - 1)], layer, sem)
    copy.start()
    slots.wait()
    step = rows.shape[1] // stack
    pieces = rows.shape[0]
    for s in range(species):
        value = held[s].astype(F32)
        for q in range(pieces):
            rows[q, s * step : s * step + count] = value[:, q * 128 : (q + 1) * 128]

    def slot(at):
        taken = [rows[q, pl.ds(at, species, stride=step), :] for q in range(pieces)]
        return jnp.concatenate(taken, axis=1)

    me = lax.axis_index("yz")
    own[...] = slot(me).astype(BF16)
    for k, out in enumerate(others):
        out[...] = slot(lax.rem(me + 2 + k, count)).astype(out.dtype)
    near_slot[...] = slot(neighbour(me, count, True))
    far_slot[...] = slot(neighbour(me, count, False))
    tmp[width * species :] = jnp.zeros((tmp.shape[0] - width * species, tmp.shape[1]), F32)
    copy.wait()
    for r in range(width):
        tmp[r * species : (r + 1) * species] = layer[r]
    first[...] = tmp[...].astype(BF16)


def pack_x(c, fine, forward):
    nx, ny, species, nz = c.shape
    count, cells = fine.shape[1:]
    stack = padded(species, 8)
    vmem = pl.BlockSpec(memory_space=pltpu.VMEM)
    rows = layer_rows(ny, species)
    outs = [jax.ShapeDtypeStruct((rows, nz), BF16)]
    outs += [jax.ShapeDtypeStruct((species, cells), F32)] * 2
    outs += [jax.ShapeDtypeStruct((species, cells), BF16)]
    kind = F32 if forward else BF16
    outs += [jax.ShapeDtypeStruct((species, cells), kind)] * max(count - 3, 0)
    return pl.pallas_call(
        pack_x_kernel,
        in_specs=[pl.BlockSpec(memory_space=pltpu.HBM)] * 2,
        out_specs=[vmem] * len(outs),
        out_shape=outs,
        scratch_shapes=[
            pltpu.VMEM((ny, species, nz), F32),
            pltpu.VMEM((rows, nz), F32),
            pltpu.VMEM(fine.shape, BF16),
            pltpu.VMEM((cells // 128, stack * padded(count, 8), 128), F32),
            pltpu.SemaphoreType.DMA,
            pltpu.SemaphoreType.DMA,
        ],
        compiler_params=pltpu.CompilerParams(vmem_limit_bytes=LIMIT),
        name="pack_x",
    )(
        pltpu.with_memory_space_constraint(c, pltpu.HBM),
        pltpu.with_memory_space_constraint(fine, pltpu.HBM),
    )


def pack_layer(columns, tmp, species):
    for r, value in enumerate(columns):
        tmp[r * species : (r + 1) * species] = value
    below = len(columns) * species
    tmp[below:] = jnp.zeros((tmp.shape[0] - below, tmp.shape[1]), F32)


def pack_slot(value, places, tmp):
    for q, (row, lane) in enumerate(places):
        tmp[row : row + value.shape[0], lane : lane + 128] = value[:, q * 128 : (q + 1) * 128]


def pack_near_kernel(c, slot, *refs):
    second, (out, tmp) = refs[:-2], refs[-2:]
    nx, ny, species, nz = c.shape
    y = jnp.where(lax.axis_index("yz") % 2 == 0, ny - 1, 0)
    pack_layer([c[r, y] for r in range(nx)], tmp, species)
    places = blocks_of(nx, species, nz, slot.shape[1])
    pack_slot(slot[...], places[0], tmp)
    for value in second:
        pack_slot(value[...], places[1], tmp)
    out[...] = tmp[...].astype(BF16)


def pack_far_kernel(c, slot, *refs):
    passed, (out, x_out, tmp, x_tmp) = refs[:-4], refs[-4:]
    nx, ny, species, nz = c.shape
    y = jnp.where(lax.axis_index("yz") % 2 == 0, 0, ny - 1)
    pack_layer([c[r, y] for r in range(nx)], tmp, species)
    places = blocks_of(nx, species, nz, slot.shape[1])
    pack_slot(slot[...], places[0], tmp)
    for ref in passed:
        tmp[nx * species :] = jnp.where(
            passes(tmp.shape[0] - nx * species, nz, places[1], nx * species, species),
            ref[...].astype(F32)[nx * species :],
            tmp[nx * species :],
        )
    out[...] = tmp[...].astype(BF16)
    x = (1 - upper()) * (nx - 1)
    pack_layer([c[x, r] for r in range(ny)], x_tmp, species)
    x_out[...] = x_tmp[...].astype(BF16)


def passes(rows, lanes, places, base, species):
    row = lax.broadcasted_iota(jnp.int32, (rows, lanes), 0)
    lane = lax.broadcasted_iota(jnp.int32, (rows, lanes), 1)
    mask = row < 0
    for at, start in places:
        here = (row >= at - base) & (row < at - base + species)
        mask = mask | (here & (lane >= start) & (lane < start + 128))
    return mask


def pack_y(kernel, name, c, slot, second, groups, extra):
    nx, ny, species, nz = c.shape
    vmem = pl.BlockSpec(memory_space=pltpu.VMEM)
    shapes = [(layer_rows(nx, species, groups), nz)]
    if extra:
        shapes.append((layer_rows(ny, species), nz))
    return pl.pallas_call(
        kernel,
        in_specs=[vmem] * (2 + len(second)),
        out_specs=[vmem] * len(shapes),
        out_shape=[jax.ShapeDtypeStruct(shape, BF16) for shape in shapes],
        scratch_shapes=[pltpu.VMEM(shape, F32) for shape in shapes],
        compiler_params=pltpu.CompilerParams(vmem_limit_bytes=LIMIT),
        name=name,
    )(c, slot, *second)


def coarse_kernel(
    pos, c, rate, coef, spread, ghost, after, adv, old, new, mix, spread16, ghost16, columns, scratch
):
    count, stack, nz = adv.shape
    boxes = pos.shape[1]
    width = c.shape[0]
    mix[...] = mixing(rate, scratch, stack, 2)
    mixed = mixing(rate, scratch, stack, GROUP)
    spread16[...] = spread[...].astype(BF16)
    ghost16[...] = ghost[...].astype(BF16)
    for k in range(count):
        columns[k, c.shape[2] :] = jnp.zeros((stack - c.shape[2], nz), F32)
        columns[k, : c.shape[2]] = c[k // width, k % width]
    diff = column(coef, stack)
    lane = lanes_of(stack)
    starts = [pos[0, i] * width for i in range(boxes)]
    masks = [tiles_of(stack, nz, start, width) for start in starts]
    tiles = old.shape[1] // 128
    zero = jnp.zeros((stack, 128), F32)
    gathered = [[[zero] * tiles for _ in range(2)] for _ in range(boxes)]
    for first in range(0, count, 2 * GROUP):
        some = range(first, min(first + 2 * GROUP, count))
        made = react_all(mixed, [columns[k] for k in some])
        for k in some:
            x, y = k // width, k % width
            mine = columns[k]
            lap = pltpu.roll(mine, 1, 1) + pltpu.roll(mine, nz - 1, 1) - 6.0 * mine
            if x > 0:
                lap = lap + columns[k - width]
            if x < width - 1:
                lap = lap + columns[k + width]
            if y > 0:
                lap = lap + columns[k - 1]
            if y < width - 1:
                lap = lap + columns[k + 1]
            value = mine + diff * lap + made[k - first]
            adv[k] = value
            if x in (0, width - 1) and y in (0, width - 1):
                continue
            for i in range(boxes):
                for n, source in enumerate((mine, value)):
                    moved = turn(fold(source, masks[i]), k * width - starts[i])
                    for t in range(tiles):
                        low, high = k * width - t * 128, (k + 1) * width - t * 128
                        if high > 0 and low < 128:
                            here = (lane >= low) & (lane < high)
                            gathered[i][n][t] = jnp.where(here, moved, gathered[i][n][t])
    for i in range(boxes):
        for out, parts_of in zip((old, new), gathered[i]):
            for t in range(tiles):
                out[i * stack : (i + 1) * stack, t * 128 : (t + 1) * 128] = parts_of[t]


def coarse_part(pos, c, rate, coef, table, stack, after):
    nx, ny, species, nz = c.shape
    boxes = pos.shape[1]
    lanes = padded(nx**3, PATCH)
    vmem = pl.BlockSpec(memory_space=pltpu.VMEM)
    small = jax.ShapeDtypeStruct((boxes * stack, lanes), F32)
    size = padded(2 * GROUP * stack, 128)
    return pl.pallas_call(
        coarse_kernel,
        in_specs=[vmem] * 6 + [pl.BlockSpec(memory_space=pl.ANY)],
        out_specs=[vmem] * 6,
        out_shape=[
            jax.ShapeDtypeStruct((nx * ny, stack, nz), F32),
            small,
            small,
            jax.ShapeDtypeStruct((4 * stack, 4 * stack), BF16),
            jax.ShapeDtypeStruct(table["spread"].shape, BF16),
            jax.ShapeDtypeStruct(table["ghost"].shape, BF16),
        ],
        scratch_shapes=[
            pltpu.VMEM((nx * ny, stack, nz), F32),
            pltpu.VMEM((size, size), F32),
        ],
        compiler_params=pltpu.CompilerParams(vmem_limit_bytes=LIMIT),
        cost_estimate=pl.CostEstimate(
            flops=800 * c.size, bytes_accessed=12 * c.size, transcendentals=0
        ),
        name="coarse_part",
    )(pos, c, rate, coef, jnp.asarray(table["spread"]), jnp.asarray(table["ghost"]), after)


def by_box(total, boxes, half):
    each = 4 * half * half
    lane = lax.broadcasted_iota(jnp.int32, total.shape, 1)
    rows = [
        jnp.where((lane >= i * each) & (lane < (i + 1) * each), total, 0.0) for i in range(boxes)
    ]
    return jnp.concatenate(rows, axis=0)


def gather_faces(pos, layers, faces, half, stack, species, nz, total):
    lane = lanes_of(stack)
    for ref, face in zip(layers, faces):
        for i in range(pos.shape[1]):
            start = pos[0, i] * (half + 2) + 1
            masks = tiles_of(stack, nz, start, half)
            for r in range(half):
                base = ((i * 4 + face) * half + r) * half
                at = (r + 1) * species
                moved = turn(fold(ref[at : at + stack], masks), base - start)
                tiles = []
                for t in range(total.shape[1] // 128):
                    along = lane + (t * 128 - base)
                    here = (along >= 0) & (along < half)
                    tiles.append(jnp.where(here, moved, total[:, t * 128 : (t + 1) * 128]))
                total = tiles[0] if len(tiles) == 1 else jnp.concatenate(tiles, axis=1)
    return total


def x_faces_kernel(pos, owner, first, own, after, *refs, count, half):
    others, (from_x, field, wide) = refs[:-3], refs[-3:]
    stack = from_x.shape[0]
    species = own.shape[0]
    nz = first.shape[1]
    wide[...] = first[...].astype(F32)
    zero = jnp.zeros(from_x.shape, F32)
    from_x[...] = gather_faces(pos, [wide], [1 - upper()], half, stack, species, nz, zero)
    me = lax.axis_index("yz")
    direct = [ref[...].astype(F32) for ref in (own, *others)]
    for i in range(pos.shape[1]):
        back = lax.rem(me - owner[0, i] + count, count)
        value = direct[0]
        for k in range(len(others)):
            value = jnp.where(back == k + 2, direct[k + 1], value)
        edge = species // 8 * 8
        field[i * stack + edge : (i + 1) * stack] = jnp.zeros((stack - edge, value.shape[1]), F32)
        field[i * stack : i * stack + species] = value


def x_faces(pos, owner, first, own, after, others, half, stack, count):
    vmem = pl.BlockSpec(memory_space=pltpu.VMEM)
    boxes = pos.shape[1]
    lanes = padded(boxes * 4 * half * half, 128)
    return pl.pallas_call(
        functools.partial(x_faces_kernel, count=count, half=half),
        in_specs=[vmem] * 4 + [pl.BlockSpec(memory_space=pl.ANY)] + [vmem] * len(others),
        out_specs=[vmem] * 2,
        out_shape=[
            jax.ShapeDtypeStruct((stack, lanes), F32),
            jax.ShapeDtypeStruct((boxes * stack, own.shape[1]), F32),
        ],
        scratch_shapes=[pltpu.VMEM(first.shape, F32)],
        compiler_params=pltpu.CompilerParams(vmem_limit_bytes=LIMIT),
        cost_estimate=pl.CostEstimate(flops=10**9, bytes_accessed=ORDER, transcendentals=0),
        name="x_faces",
    )(pos, owner, first, own, after, *others)


def fine_kernel(pos, owner, x_second, near, far, start, *refs, count, edge):
    old, new, mix, coef, spread, ghost, from_x = refs[:7]
    packets = refs[7 : 7 + count]
    fix, kept, final, field, wide, x_wide = refs[7 + count :]
    species = packets[0].shape[0]
    stack = from_x.shape[0]
    boxes = final.shape[0] // stack
    cells = final.shape[1]
    me = lax.axis_index("yz")
    mixed = mix[...]

    def reaction(value):
        pairs = [value[at : at + 2 * stack] for at in range(0, boxes * stack, 2 * stack)]
        return jnp.concatenate([react(mixed, pair) for pair in pairs], axis=0)

    nz = near.shape[1]
    half = edge // 2
    wide[0] = near[...].astype(F32)
    wide[1] = far[...].astype(F32)
    first_at, second_at = blocks_of(half + 2, species, nz, cells)
    near_at, far_at = neighbour(me, count, True), neighbour(me, count, False)
    sources = [(near_at, 0, first_at), (far_at, 1, first_at)]
    if count == 4:
        sources.append((lax.rem(me + 2, count), 1, second_at))
    for i in range(boxes):
        for q in range(cells // 128):
            mine = (slice(i * stack, (i + 1) * stack), slice(q * 128, (q + 1) * 128))
            part = start[mine]
            for source, n, places in sources:
                row, at = places[q]
                sent = wide[n, row : row + stack, at : at + 128]
                part = jnp.where(owner[0, i] == source, sent, part)
            field[mine] = part
    diff = jnp.concatenate([column(coef, stack)] * boxes, axis=0)
    old_v, new_v = old[...], new[...]
    sums = old_v + new_v
    spread_v = spread[...]
    both = rows_dot(jnp.concatenate([old_v, sums], axis=0), spread_v)
    ghost0, ghost1 = both[: boxes * stack], both[boxes * stack :]
    index = lax.broadcasted_iota(jnp.int32, (1, cells), 1)
    at = (index // (edge * edge), index // edge % edge, index % edge)
    step = (edge * edge, edge, 1)

    def inside(value):
        lap = -6.0 * value
        for axis in range(3):
            before = pltpu.roll(value, step[axis], 1)
            after = pltpu.roll(value, cells - step[axis], 1)
            lap = lap + jnp.where(at[axis] == 0, 0.0, before)
            lap = lap + jnp.where(at[axis] == edge - 1, 0.0, after)
        return lap

    first = field[...]
    second = first + 2.0 * diff * (inside(first) + ghost0) + 0.5 * reaction(first)
    base = second + diff * (2.0 * inside(second) + ghost1) + 0.5 * reaction(second)
    odd = me % 2
    x_wide[...] = x_second[...].astype(F32)
    layers = (x_wide, wide.at[0], wide.at[1])
    faces = (upper(), 3 - odd, 2 + odd)
    total = gather_faces(pos, layers, faces, half, stack, species, nz, from_x[...])
    kept[...] = total
    stacked = by_box(total, boxes, half).astype(BF16)
    value = base + diff * diff * dot(stacked, ghost[...])
    final[...] = value
    for k, out in enumerate(packets):
        dest = partner(me, k, count)
        packet = jnp.zeros((species, cells), F32)
        for i in range(boxes):
            packet = jnp.where(owner[0, i] == dest, value[i * stack : i * stack + species], packet)
        out[...] = packet.astype(BF16)
    pooled = lax.dot_general(
        parts(first + second), spread_v, (((1,), (1,)), ((), ())), preferred_element_type=F32
    )
    pooled = 0.25 * (pooled[: boxes * stack] + pooled[boxes * stack :])
    width = edge // 2 + 2
    lanes = old.shape[1]
    lane = lax.broadcasted_iota(jnp.int32, (1, lanes), 1)
    at = (lane // (width * width), lane // width % width, lane % width)
    step = (width * width, width, 1)
    inner = [(a >= 1) & (a <= width - 2) for a in at]
    rest = pooled - 0.5 * sums
    result = jnp.zeros_like(old_v)
    for axis in range(3):
        sides = inner[(axis + 1) % 3] & inner[(axis + 2) % 3]
        for edge_at, shift in ((0, lanes - step[axis]), (width - 1, step[axis])):
            mask = sides & (at[axis] == edge_at)
            fixed = rest - pltpu.roll(old_v, shift, 1)
            result = jnp.where(mask, fixed, result)
    fix[...] = diff * result


def fine_part(pos, owner, second, near, far, start, old, new, mix, coef, spread, ghost, from_x, edge, count):
    boxes = owner.shape[1]
    stack = from_x.shape[0]
    cells = start.shape[1]
    vmem = pl.BlockSpec(memory_space=pltpu.VMEM)
    return pl.pallas_call(
        functools.partial(fine_kernel, count=count, edge=edge),
        in_specs=[vmem] * 13,
        out_specs=[vmem] * (count + 3),
        out_shape=[jax.ShapeDtypeStruct((coef.shape[1], cells), BF16)] * count
        + [
            jax.ShapeDtypeStruct((boxes * stack, old.shape[1]), F32),
            jax.ShapeDtypeStruct(from_x.shape, F32),
            jax.ShapeDtypeStruct((boxes * stack, cells), F32),
        ],
        scratch_shapes=[
            pltpu.VMEM((boxes * stack, cells), F32),
            pltpu.VMEM((2, *near.shape), F32),
            pltpu.VMEM(second.shape, F32),
        ],
        compiler_params=pltpu.CompilerParams(vmem_limit_bytes=LIMIT),
        name="fine_part",
    )(
        pos,
        owner,
        second,
        near,
        far,
        start,
        old,
        new,
        mix,
        coef,
        spread,
        ghost,
        from_x,
    )


def delta_of(field, kept, fix, coef, average, place, half, stack):
    boxes = field.shape[0] // stack
    diffs = jnp.concatenate([column(coef, stack)] * boxes, axis=0)
    stacked = by_box(kept[...], boxes, half).astype(BF16)
    halo = dot(stacked, place[...].astype(BF16))
    means = rows_dot(field[...], average[...].astype(BF16))
    return fix[...] - 0.5 * diffs * diffs * halo + means


def correct_kernel(
    pos, adv, x_first, x_second, near, far, coef, field, kept, fix, average, place, out, block, wide, sems, half
):
    count, stack, nz = adv.shape
    species = block.shape[2]
    width = half + 2
    delta = delta_of(field, kept, fix, coef, average, place, half, stack)
    diff = column(coef, stack)
    even = lax.axis_index("yz") % 2 == 0
    rows = x_first.shape[0]
    first_v, second_v = x_first[...].astype(F32), x_second[...].astype(F32)
    near_v, far_v = near[:rows].astype(F32), far[:rows].astype(F32)
    up = upper() == 1
    wide[0, :rows] = jnp.where(up, first_v, second_v)
    wide[1, :rows] = jnp.where(up, second_v, first_v)
    wide[2, :rows] = jnp.where(even, far_v, near_v)
    wide[3, :rows] = jnp.where(even, near_v, far_v)
    boxes = delta.shape[0] // stack
    starts = [pos[0, i] * width for i in range(boxes)]
    cycle = [tiles_of(stack, nz, start, width) for start in starts]
    inside = [tiles_of(stack, nz, start + 1, half) for start in starts]
    lane = lanes_of(stack)
    copies = []
    for k in range(count):
        x, y = k // width, k % width
        value = adv[k]
        for there, at, n in (
            (x == 0, y, 0),
            (x == width - 1, y, 1),
            (y == 0, x, 2),
            (y == width - 1, x, 3),
        ):
            if there:
                value = value + diff * wide[n, at * species : at * species + stack]
        if x not in (0, width - 1) or y not in (0, width - 1):
            tiles = [value[:, t * 128 : (t + 1) * 128] for t in range(nz // 128)]
            covers = 0 < x < width - 1 and 0 < y < width - 1
            for i in range(boxes):
                mine = delta[i * stack : (i + 1) * stack]
                t = k * width // 128
                part = mine[:, t * 128 : (t + 1) * 128]
                if (k + 1) * width > (t + 1) * 128:
                    after = mine[:, (t + 1) * 128 : (t + 2) * 128]
                    part = jnp.where(lane < (k + 1) * width - (t + 1) * 128, after, part)
                moved = turn(part, starts[i] - k * width)
                for t in range(nz // 128):
                    if covers:
                        tiles[t] = jnp.where(inside[i][t], 0.0, tiles[t])
                    tiles[t] = tiles[t] + jnp.where(cycle[i][t], moved, 0.0)
            value = jnp.concatenate(tiles, axis=1)
        block[x, y] = value[:species]
        if y == width - 1:
            copies.append(pltpu.make_async_copy(block.at[x], out.at[x], sems.at[x]))
            copies[-1].start()
    for copy in copies:
        copy.wait()


def correct(pos, adv, halos, coef, field, kept, fix, table, half):
    _, stack, nz = adv.shape
    width = half + 2
    species = coef.shape[1]
    vmem = pl.BlockSpec(memory_space=pltpu.VMEM)
    return pl.pallas_call(
        functools.partial(correct_kernel, half=half),
        in_specs=[vmem] * 12,
        out_specs=pl.BlockSpec(memory_space=pltpu.HBM),
        out_shape=jax.ShapeDtypeStruct((width, width, species, nz), F32),
        scratch_shapes=[
            pltpu.VMEM((width, width, species, nz), F32),
            pltpu.VMEM((4, halos[0].shape[0] + stack, nz), F32),
            pltpu.SemaphoreType.DMA((width,)),
        ],
        compiler_params=pltpu.CompilerParams(vmem_limit_bytes=LIMIT),
        cost_estimate=pl.CostEstimate(
            flops=20 * adv.size, bytes_accessed=12 * adv.size, transcendentals=0
        ),
        name="coarse_correct",
    )(
        pos,
        adv,
        *halos,
        coef,
        field,
        kept,
        fix,
        jnp.asarray(table["average"]),
        jnp.asarray(table["place"]),
    )


def ring(axis, by):
    count = lax.axis_size(axis)
    return [(i, (i + by) % count) for i in range(count)]


def mutual(axis, by):
    count = lax.axis_size(axis)
    one_way = [(i, (i + by) % count) for i in range(0, count, 2)]
    return one_way + [(j, i) for i, j in one_way]


def slabs(by):
    slabs_count, count = lax.axis_size("gx"), lax.axis_size("yz")
    pairs = []
    for g in range(slabs_count):
        for j in range(count):
            to = (g + (by if j < count // 2 else -by)) % slabs_count
            pairs.append((g * count + j, to * count + j))
    return pairs


def partner(me, k, count):
    return me ^ k if count & (count - 1) == 0 else lax.rem(me + k, count)


def origin(me, source, count):
    return me ^ source if count & (count - 1) == 0 else lax.rem(me - source + count, count)


def local(coarse_state, fine_state, diffusion, rate, box_pos, box_owner):
    species, width = coarse_state.shape[:2]
    half = width - 2
    stack = padded(species, 8)
    count = lax.axis_size("yz")
    me = lax.axis_index("yz")
    pos, owner = box_pos[0], box_owner[0]
    table = tables(width, pos.shape[1])
    coef = diffusion[None]
    c = jnp.transpose(coarse_state, (1, 2, 0, 3))

    fine = jnp.transpose(fine_state, (1, 0, 2))
    forward = count == 4
    forward = count == 4
    groups = -(-(2 if forward else 1) * fine.shape[2] // c.shape[3])
    x_first, near_slot, far_slot, own, *others = pack_x(c, fine, forward)
    relayed = others if forward else []
    (near,) = pack_y(pack_near_kernel, "pack_near", c, near_slot, relayed, groups, False)
    near = lax.ppermute(near, "yz", mutual("yz", 1))
    relayed = [near] if forward else []
    far, x_second = pack_y(pack_far_kernel, "pack_far", c, far_slot, relayed, groups, True)
    halos = [
        lax.ppermute(x_first, ("gx", "yz"), slabs(-1)),
        lax.ppermute(x_second, ("gx", "yz"), slabs(1)),
        near,
        lax.ppermute(far, "yz", mutual("yz", -1)),
    ]
    if forward:
        others = []
    others = [lax.ppermute(slot, "yz", ring("yz", 2 + k)) for k, slot in enumerate(others)]

    adv, old, new, mix, spread, ghost = coarse_part(
        pos, c, rate, coef, table, stack, far
    )
    from_x, start = x_faces(pos, owner, halos[0], own, old, others, half, stack, count)
    made = fine_part(
        pos, owner, *halos[1:], start, old, new, mix, coef, spread, ghost, from_x, 2 * half, count
    )
    packets, (fix, kept, field) = made[:count], made[count:]

    def swap(value, k):
        even = count & (count - 1) == 0
        pairs = [(i, i ^ k if even else (i + k) % count) for i in range(count)]
        return lax.ppermute(value, "yz", pairs)

    back = [packets[0]] + [swap(packets[k], k) for k in range(1, count)]
    coarse_next = correct(pos, adv, halos, coef, field, kept, fix, table, half)

    source = lax.broadcasted_iota(jnp.int32, (count, 1, 1), 0)
    turn = origin(me, source, count)
    fine_next = jnp.broadcast_to(back[0][None], (count,) + back[0].shape)
    for k in range(1, count):
        fine_next = jnp.where(turn == k, back[k][None], fine_next)
    return jnp.transpose(coarse_next, (2, 0, 1, 3)), fine_next


def solution(mesh):
    in_specs = (
        P(None, "gx", "yz", None),
        P(("gx", "yz"), None, None),
        P(),
        P(),
        P("gx", "yz", None),
        P("gx", "yz", None),
    )
    out_specs = (P(None, "gx", "yz", None), P(("gx", "yz"), None, None))
    return jax.shard_map(local, mesh=mesh, in_specs=in_specs, out_specs=out_specs, check_vma=False)
```

```python
import functools

import jax
import jax.numpy as jnp
import numpy as np
from jax import lax
from jax.experimental import pallas as pl
from jax.experimental.pallas import tpu as pltpu
from jax.sharding import PartitionSpec as P

F32 = jnp.float32
BF16 = jnp.bfloat16
LIMIT = 12 * 1024 * 1024
PATCH = 256
ORDER = 20_000_000


def padded(count, unit):
    return -(-count // unit) * unit


@functools.lru_cache(maxsize=None)
def tables(width, boxes):
    half = width - 2
    edge = 2 * half
    cells = width**3
    lanes = padded(cells, PATCH)
    fine = edge**3
    spread = np.zeros((lanes, fine), np.float32)
    average = np.zeros((fine, lanes), np.float32)
    halo = padded(boxes * 4 * half * half, 128)
    place = np.zeros((halo, lanes), np.float32)

    def cell(x, y, z):
        return (x * width + y) * width + z

    for number in range(6):
        axis, high = divmod(number, 2)
        others = [a for a in range(3) if a != axis]
        for r in range(half):
            for q in range(half):
                at = [0, 0, 0]
                at[axis] = width - 1 if high else 0
                at[others[0]] = r + 1
                at[others[1]] = q + 1
                here = cell(*at)
                for i in range(2):
                    for j in range(2):
                        pos = [0, 0, 0]
                        pos[axis] = edge - 1 if high else 0
                        pos[others[0]] = 2 * r + i
                        pos[others[1]] = 2 * q + j
                        spread[here, (pos[0] * edge + pos[1]) * edge + pos[2]] = 1.0
                if number < 4:
                    for box in range(boxes):
                        place[((box * 4 + number) * half + r) * half + q, here] = 1.0
    for x in range(edge):
        for y in range(edge):
            for z in range(edge):
                average[(x * edge + y) * edge + z, cell(x // 2 + 1, y // 2 + 1, z // 2 + 1)] = 0.125
    return dict(spread=spread, average=average, place=place, ghost=place @ spread)


def column(diffusion, stack):
    species = diffusion.shape[1]
    row = lax.broadcasted_iota(jnp.int32, (stack, species), 0)
    lane = lax.broadcasted_iota(jnp.int32, (stack, species), 1)
    return jnp.sum(jnp.where(row == lane, diffusion[...], 0.0), axis=1, keepdims=True)


def split(value):
    high = value.astype(BF16).astype(F32)
    return high, value - high


def parts(value):
    return jnp.concatenate(split(value), axis=0).astype(BF16)


def dot(a, b):
    return jnp.dot(a, b, preferred_element_type=F32)


def rows_dot(value, table):
    rows = value.shape[0]
    both = dot(parts(value), table)
    return both[:rows] + both[rows:]


GROUP = 5


def mixing(rate, scratch, stack, group):
    species = rate.shape[0]
    size = group * stack
    scratch[...] = jnp.zeros_like(scratch)
    high, low = split(rate[...])
    for b in range(group):
        at = b * stack
        for row, lane, part in ((at, at, high), (at, size + at, high), (size + at, at, low)):
            scratch[row : row + species, lane : lane + species] = part
    return scratch[: 2 * size, : 2 * size].astype(BF16)


def react(mix, fields):
    size = fields.shape[0]
    both = dot(mix, parts(fields))
    return both[:size] + both[size:]


def react_all(mix, fields):
    stack, depth = fields[0].shape
    made = [[] for _ in fields]

    def product(blocks):
        size = len(blocks[0])
        blank = [jnp.zeros_like(blocks[0][0])] * (GROUP - size)
        columns = [jnp.concatenate(block + blank, axis=0) for block in blocks]
        out = react(mix, jnp.concatenate(columns, axis=1))
        lanes = out.shape[1] // len(blocks)
        return [
            [out[b * stack : (b + 1) * stack, n * lanes : (n + 1) * lanes] for b in range(size)]
            for n in range(len(blocks))
        ]

    for lane in range(0, depth, 256):
        if lane + 256 <= depth:
            for at in range(0, len(fields), GROUP):
                block = [f[:, lane : lane + 256] for f in fields[at : at + GROUP]]
                for b, value in enumerate(product([block])[0]):
                    made[at + b].append(value)
        else:
            half = -(-len(fields) // 2)
            blocks = [[f[:, lane:] for f in part] for part in (fields[:half], fields[half:])]
            blocks[1] += [jnp.zeros_like(blocks[0][0])] * (half - len(blocks[1]))
            for n, values in enumerate(product(blocks)):
                for b, value in enumerate(values):
                    if n * half + b < len(fields):
                        made[n * half + b].append(value)
    return [jnp.concatenate(value, axis=1) for value in made]


def lanes_of(stack, lanes=128):
    return lax.broadcasted_iota(jnp.int32, (stack, lanes), 1)


def tiles_of(stack, depth, start, width):
    lane = lanes_of(stack)
    masks = []
    for t in range(depth // 128):
        along = lane + (t * 128 - start)
        masks.append((along >= 0) & (along < width))
    return masks


def fold(value, masks):
    out = value[:, :128]
    for t in range(1, len(masks)):
        out = jnp.where(masks[t], value[:, t * 128 : (t + 1) * 128], out)
    return out


def turn(value, by):
    return pltpu.roll(value, by & 127, 1)


def neighbour(me, count, even_up):
    step = jnp.where((me % 2 == 0) == even_up, 1, count - 1)
    return lax.rem(me + step, count)


def layer_rows(width, species, groups=0):
    return padded((width + groups) * species, 16)


def blocks_of(width, species, nz, pieces):
    across = nz // 128
    return [((width + n // across) * species, n % across * 128) for n in range(pieces)]


def pack_layer(columns, tmp, species):
    for r, value in enumerate(columns):
        tmp[r * species : (r + 1) * species] = value
    below = len(columns) * species
    tmp[below:] = jnp.zeros((tmp.shape[0] - below, tmp.shape[1]), F32)


def pack_y_kernel(c, fine, near, far, own, *refs):
    others, (layer, tmp, held, rows, sems, fine_sem) = refs[:-6], refs[-6:]
    nx, ny, species, nz = c.shape
    count = fine.shape[1]
    stack = padded(species, 8)
    me = lax.axis_index("yz")
    slots = pltpu.make_async_copy(fine, held, fine_sem)
    slots.start()
    copies = []
    for n, y in enumerate((jnp.where(me % 2 == 0, ny - 1, 0), jnp.where(me % 2 == 0, 0, ny - 1))):
        copies.append(pltpu.make_async_copy(c.at[:, y], layer.at[n], sems.at[n]))
        copies[-1].start()
    slots.wait()
    step = rows.shape[1] // stack
    pieces = rows.shape[0]
    for s in range(species):
        value = held[s].astype(F32)
        for q in range(pieces):
            rows[q, s * step : s * step + count] = value[:, q * 128 : (q + 1) * 128]

    def slot(at):
        return [rows[q, pl.ds(at, species, stride=step), :] for q in range(pieces)]

    own[...] = jnp.concatenate(slot(me), axis=1).astype(BF16)
    for k, out in enumerate(others):
        out[...] = jnp.concatenate(slot(lax.rem(me + 2 + k, count)), axis=1).astype(BF16)
    for n, out in enumerate((far, near)):
        n = 1 - n
        copies[n].wait()
        pack_layer([layer[n, r] for r in range(nx)], tmp, species)
        places = blocks_of(nx, species, nz, pieces)
        for (row, lane), piece in zip(places, slot(neighbour(me, count, n == 0))):
            tmp[row : row + species, lane : lane + 128] = piece
        out[...] = tmp[...].astype(BF16)


def pack_y(c, fine):
    nx, ny, species, nz = c.shape
    count, cells = fine.shape[1:]
    stack = padded(species, 8)
    vmem = pl.BlockSpec(memory_space=pltpu.VMEM)
    rows = layer_rows(nx, species, -(-cells // nz))
    outs = [jax.ShapeDtypeStruct((rows, nz), BF16)] * 2
    outs += [jax.ShapeDtypeStruct((species, cells), BF16)] * (1 + max(count - 3, 0))
    return pl.pallas_call(
        pack_y_kernel,
        in_specs=[pl.BlockSpec(memory_space=pltpu.HBM)] * 2,
        out_specs=[vmem] * len(outs),
        out_shape=outs,
        scratch_shapes=[
            pltpu.VMEM((2, nx, species, nz), F32),
            pltpu.VMEM((rows, nz), F32),
            pltpu.VMEM(fine.shape, BF16),
            pltpu.VMEM((cells // 128, stack * padded(count, 8), 128), F32),
            pltpu.SemaphoreType.DMA((2,)),
            pltpu.SemaphoreType.DMA,
        ],
        compiler_params=pltpu.CompilerParams(vmem_limit_bytes=LIMIT),
        name="pack_y",
    )(
        pltpu.with_memory_space_constraint(c, pltpu.HBM),
        pltpu.with_memory_space_constraint(fine, pltpu.HBM),
    )


def pack_x_kernel(c, after, out, tmp, x):
    nx, ny, species, _ = c.shape
    pack_layer([c[x, r] for r in range(ny)], tmp, species)
    out[...] = tmp[...].astype(BF16)


def pack_x(c, after, x):
    nx, ny, species, nz = c.shape
    vmem = pl.BlockSpec(memory_space=pltpu.VMEM)
    shape = (layer_rows(ny, species), nz)
    return pl.pallas_call(
        functools.partial(pack_x_kernel, x=x),
        in_specs=[vmem, pl.BlockSpec(memory_space=pl.ANY)],
        out_specs=vmem,
        out_shape=jax.ShapeDtypeStruct(shape, BF16),
        scratch_shapes=[pltpu.VMEM(shape, F32)],
        compiler_params=pltpu.CompilerParams(vmem_limit_bytes=LIMIT),
        name="pack_x",
    )(c, after)


def coarse_kernel(
    pos, c, rate, coef, spread, ghost, after, adv, old, new, mix, spread16, ghost16, columns, scratch
):
    count, stack, nz = adv.shape
    boxes = pos.shape[1]
    width = c.shape[0]
    mix[...] = mixing(rate, scratch, stack, 2)
    mixed = mixing(rate, scratch, stack, GROUP)
    spread16[...] = spread[...].astype(BF16)
    ghost16[...] = ghost[...].astype(BF16)
    for k in range(count):
        columns[k, c.shape[2] :] = jnp.zeros((stack - c.shape[2], nz), F32)
        columns[k, : c.shape[2]] = c[k // width, k % width]
    diff = column(coef, stack)
    for first in range(0, count, 2 * GROUP):
        some = range(first, min(first + 2 * GROUP, count))
        made = react_all(mixed, [columns[k] for k in some])
        for k in some:
            x, y = k // width, k % width
            mine = columns[k]
            lap = pltpu.roll(mine, 1, 1) + pltpu.roll(mine, nz - 1, 1) - 6.0 * mine
            if x > 0:
                lap = lap + columns[k - width]
            if x < width - 1:
                lap = lap + columns[k + width]
            if y > 0:
                lap = lap + columns[k - 1]
            if y < width - 1:
                lap = lap + columns[k + 1]
            value = mine + diff * lap + made[k - first]
            adv[k] = value
    lanes = old.shape[1]
    cell = lanes_of(stack, lanes) // width
    for i in range(boxes):
        lane = pos[0, i] * width
        start = pl.multiple_of(jnp.minimum(lane // 128, nz // 128 - 2) * 128, 128)
        offset = lane - start
        for source, out in ((columns, old), (adv, new)):
            total = jnp.zeros((stack, lanes), F32)
            for k in range(count):
                if k // width in (0, width - 1) and k % width in (0, width - 1):
                    continue
                part = source[k, :, pl.ds(start, PATCH)]
                moved = pltpu.roll(part, (k * width - offset) & (PATCH - 1), 1)
                total = jnp.where(cell == k, moved, total)
            out[i * stack : (i + 1) * stack] = total


def coarse_part(pos, c, rate, coef, table, stack, after):
    nx, ny, species, nz = c.shape
    boxes = pos.shape[1]
    lanes = padded(nx**3, PATCH)
    vmem = pl.BlockSpec(memory_space=pltpu.VMEM)
    small = jax.ShapeDtypeStruct((boxes * stack, lanes), F32)
    size = padded(2 * GROUP * stack, 128)
    return pl.pallas_call(
        coarse_kernel,
        in_specs=[vmem] * 6 + [pl.BlockSpec(memory_space=pl.ANY)],
        out_specs=[vmem] * 6,
        out_shape=[
            jax.ShapeDtypeStruct((nx * ny, stack, nz), F32),
            small,
            small,
            jax.ShapeDtypeStruct((4 * stack, 4 * stack), BF16),
            jax.ShapeDtypeStruct(table["spread"].shape, BF16),
            jax.ShapeDtypeStruct(table["ghost"].shape, BF16),
        ],
        scratch_shapes=[
            pltpu.VMEM((nx * ny, stack, nz), F32),
            pltpu.VMEM((size, size), F32),
        ],
        compiler_params=pltpu.CompilerParams(vmem_limit_bytes=LIMIT),
        cost_estimate=pl.CostEstimate(
            flops=800 * c.size, bytes_accessed=12 * c.size, transcendentals=0
        ),
        name="coarse_part",
    )(pos, c, rate, coef, jnp.asarray(table["spread"]), jnp.asarray(table["ghost"]), after)


def by_box(total, boxes, half):
    each = 4 * half * half
    lane = lax.broadcasted_iota(jnp.int32, total.shape, 1)
    rows = [
        jnp.where((lane >= i * each) & (lane < (i + 1) * each), total, 0.0) for i in range(boxes)
    ]
    return jnp.concatenate(rows, axis=0)


def gather_faces(pos, layers, faces, half, stack, species, nz, total):
    lane = lanes_of(stack)
    for ref, face in zip(layers, faces):
        for i in range(pos.shape[1]):
            start = pos[0, i] * (half + 2) + 1
            masks = tiles_of(stack, nz, start, half)
            for r in range(half):
                base = ((i * 4 + face) * half + r) * half
                at = (r + 1) * species
                moved = turn(fold(ref[at : at + stack], masks), base - start)
                tiles = []
                for t in range(total.shape[1] // 128):
                    along = lane + (t * 128 - base)
                    here = (along >= 0) & (along < half)
                    tiles.append(jnp.where(here, moved, total[:, t * 128 : (t + 1) * 128]))
                total = tiles[0] if len(tiles) == 1 else jnp.concatenate(tiles, axis=1)
    return total


def y_faces_kernel(pos, owner, near, far, x_low, own, after, *refs):
    others, (from_y, start, wide, x_wide) = refs[:-4], refs[-4:]
    stack = from_y.shape[0]
    species, cells = own.shape
    nz = near.shape[1]
    boxes = pos.shape[1]
    width = (near.shape[0] // species) - (-(-cells // nz))
    half = width - 2
    wide[0] = near[...].astype(F32)
    wide[1] = far[...].astype(F32)
    x_wide[...] = x_low[...].astype(F32)
    me, count = lax.axis_index("yz"), lax.axis_size("yz")
    odd = me % 2
    zero = jnp.zeros(from_y.shape, F32)
    layers = (wide.at[0], wide.at[1], x_wide)
    from_y[...] = gather_faces(pos, layers, (3 - odd, 2 + odd, 0), half, stack, species, nz, zero)
    direct = [ref[...].astype(F32) for ref in (own, *others)]
    places = blocks_of(width, species, nz, cells // 128)
    edge = species // 8 * 8
    for i in range(boxes):
        by_near = owner[0, i] == neighbour(me, count, True)
        by_far = owner[0, i] == neighbour(me, count, False)
        at = i * stack
        start[at + edge : at + stack] = jnp.zeros((stack - edge, cells), F32)
        back = lax.rem(me - owner[0, i] + count, count)
        value = direct[0]
        for k in range(len(others)):
            value = jnp.where(back == k + 2, direct[k + 1], value)
        for q, (row, lane) in enumerate(places):
            part = value[:, q * 128 : (q + 1) * 128]
            sent = [wide[n, row : row + species, lane : lane + 128] for n in range(2)]
            part = jnp.where(by_far, sent[1], jnp.where(by_near, sent[0], part))
            start[at : at + species, q * 128 : (q + 1) * 128] = part


def y_faces(pos, owner, near, far, x_low, own, after, others, half, stack):
    vmem = pl.BlockSpec(memory_space=pltpu.VMEM)
    boxes = pos.shape[1]
    lanes = padded(boxes * 4 * half * half, 128)
    return pl.pallas_call(
        y_faces_kernel,
        in_specs=[vmem] * 6 + [pl.BlockSpec(memory_space=pl.ANY)] + [vmem] * len(others),
        out_specs=[vmem] * 2,
        out_shape=[
            jax.ShapeDtypeStruct((stack, lanes), F32),
            jax.ShapeDtypeStruct((boxes * stack, own.shape[1]), F32),
        ],
        scratch_shapes=[pltpu.VMEM((2, *near.shape), F32), pltpu.VMEM(x_low.shape, F32)],
        compiler_params=pltpu.CompilerParams(vmem_limit_bytes=LIMIT),
        cost_estimate=pl.CostEstimate(flops=10**9, bytes_accessed=ORDER, transcendentals=0),
        name="y_faces",
    )(pos, owner, near, far, x_low, own, after, *others)


def fine_kernel(pos, owner, x_high, field, *refs, count, edge):
    old, new, mix, coef, spread, ghost, from_y = refs[:7]
    packets = refs[7 : 7 + count]
    fix, kept, final, wide = refs[7 + count :]
    species = packets[0].shape[0]
    stack = from_y.shape[0]
    boxes = final.shape[0] // stack
    cells = final.shape[1]
    me = lax.axis_index("yz")
    mixed = mix[...]

    def reaction(value):
        pairs = [value[at : at + 2 * stack] for at in range(0, boxes * stack, 2 * stack)]
        return jnp.concatenate([react(mixed, pair) for pair in pairs], axis=0)

    nz = x_high.shape[1]
    half = edge // 2
    wide[...] = x_high[...].astype(F32)
    diff = jnp.concatenate([column(coef, stack)] * boxes, axis=0)
    old_v, new_v = old[...], new[...]
    sums = old_v + new_v
    spread_v = spread[...]
    both = rows_dot(jnp.concatenate([old_v, sums], axis=0), spread_v)
    ghost0, ghost1 = both[: boxes * stack], both[boxes * stack :]
    index = lax.broadcasted_iota(jnp.int32, (1, cells), 1)
    at = (index // (edge * edge), index // edge % edge, index % edge)
    step = (edge * edge, edge, 1)

    def inside(value):
        lap = -6.0 * value
        for axis in range(3):
            before = pltpu.roll(value, step[axis], 1)
            after = pltpu.roll(value, cells - step[axis], 1)
            lap = lap + jnp.where(at[axis] == 0, 0.0, before)
            lap = lap + jnp.where(at[axis] == edge - 1, 0.0, after)
        return lap

    first = field[...]
    second = first + 2.0 * diff * (inside(first) + ghost0) + 0.5 * reaction(first)
    base = second + diff * (2.0 * inside(second) + ghost1) + 0.5 * reaction(second)
    total = gather_faces(pos, [wide], [1], half, stack, species, nz, from_y[...])
    kept[...] = total
    stacked = by_box(total, boxes, half).astype(BF16)
    value = base + diff * diff * dot(stacked, ghost[...])
    final[...] = value
    for k, out in enumerate(packets):
        dest = partner(me, k, count)
        packet = jnp.zeros((species, cells), F32)
        for i in range(boxes):
            packet = jnp.where(owner[0, i] == dest, value[i * stack : i * stack + species], packet)
        out[...] = packet.astype(BF16)
    pooled = lax.dot_general(
        parts(first + second), spread_v, (((1,), (1,)), ((), ())), preferred_element_type=F32
    )
    pooled = 0.25 * (pooled[: boxes * stack] + pooled[boxes * stack :])
    width = edge // 2 + 2
    lanes = old.shape[1]
    lane = lax.broadcasted_iota(jnp.int32, (1, lanes), 1)
    at = (lane // (width * width), lane // width % width, lane % width)
    step = (width * width, width, 1)
    inner = [(a >= 1) & (a <= width - 2) for a in at]
    rest = pooled - 0.5 * sums
    result = jnp.zeros_like(old_v)
    for axis in range(3):
        sides = inner[(axis + 1) % 3] & inner[(axis + 2) % 3]
        for edge_at, shift in ((0, lanes - step[axis]), (width - 1, step[axis])):
            mask = sides & (at[axis] == edge_at)
            fixed = rest - pltpu.roll(old_v, shift, 1)
            result = jnp.where(mask, fixed, result)
    fix[...] = diff * result


def fine_part(pos, owner, high, start, old, new, mix, coef, spread, ghost, from_y, count, edge):
    boxes = owner.shape[1]
    stack = from_y.shape[0]
    cells = start.shape[1]
    vmem = pl.BlockSpec(memory_space=pltpu.VMEM)
    return pl.pallas_call(
        functools.partial(fine_kernel, count=count, edge=edge),
        in_specs=[vmem] * 11,
        out_specs=[vmem] * (count + 3),
        out_shape=[jax.ShapeDtypeStruct((coef.shape[1], cells), BF16)] * count
        + [
            jax.ShapeDtypeStruct((boxes * stack, old.shape[1]), F32),
            jax.ShapeDtypeStruct(from_y.shape, F32),
            jax.ShapeDtypeStruct((boxes * stack, cells), F32),
        ],
        scratch_shapes=[
            pltpu.VMEM(high.shape, F32),
        ],
        compiler_params=pltpu.CompilerParams(vmem_limit_bytes=LIMIT),
        name="fine_part",
    )(pos, owner, high, start, old, new, mix, coef, spread, ghost, from_y)


def delta_of(field, kept, fix, coef, average, place, half, stack):
    boxes = field.shape[0] // stack
    diffs = jnp.concatenate([column(coef, stack)] * boxes, axis=0)
    stacked = by_box(kept[...], boxes, half).astype(BF16)
    halo = dot(stacked, place[...].astype(BF16))
    means = rows_dot(field[...], average[...].astype(BF16))
    return fix[...] - 0.5 * diffs * diffs * halo + means


def correct_kernel(
    pos, adv, x_first, x_second, near, far, coef, field, kept, fix, average, place, out, block, wide, sems, half
):
    count, stack, nz = adv.shape
    species = block.shape[2]
    width = half + 2
    delta = delta_of(field, kept, fix, coef, average, place, half, stack)
    diff = column(coef, stack)
    even = lax.axis_index("yz") % 2 == 0
    rows = x_first.shape[0]
    near_v, far_v = near[:rows].astype(F32), far[:rows].astype(F32)
    wide[0, :rows] = x_first[...].astype(F32)
    wide[1, : x_second.shape[0]] = x_second[...].astype(F32)
    wide[2, :rows] = jnp.where(even, far_v, near_v)
    wide[3, :rows] = jnp.where(even, near_v, far_v)
    boxes = delta.shape[0] // stack
    starts = [pos[0, i] * width for i in range(boxes)]
    cycle = [tiles_of(stack, nz, start, width) for start in starts]
    inside = [tiles_of(stack, nz, start + 1, half) for start in starts]
    lane = lanes_of(stack)
    copies = []
    for k in range(count):
        x, y = k // width, k % width
        value = adv[k]
        for there, at, n in (
            (x == 0, y, 0),
            (x == width - 1, y, 1),
            (y == 0, x, 2),
            (y == width - 1, x, 3),
        ):
            if there:
                value = value + diff * wide[n, at * species : at * species + stack]
        if x not in (0, width - 1) or y not in (0, width - 1):
            tiles = [value[:, t * 128 : (t + 1) * 128] for t in range(nz // 128)]
            covers = 0 < x < width - 1 and 0 < y < width - 1
            for i in range(boxes):
                mine = delta[i * stack : (i + 1) * stack]
                t = k * width // 128
                part = mine[:, t * 128 : (t + 1) * 128]
                if (k + 1) * width > (t + 1) * 128:
                    after = mine[:, (t + 1) * 128 : (t + 2) * 128]
                    part = jnp.where(lane < (k + 1) * width - (t + 1) * 128, after, part)
                moved = turn(part, starts[i] - k * width)
                for t in range(nz // 128):
                    if covers:
                        tiles[t] = jnp.where(inside[i][t], 0.0, tiles[t])
                    tiles[t] = tiles[t] + jnp.where(cycle[i][t], moved, 0.0)
            value = jnp.concatenate(tiles, axis=1)
        block[x, y] = value[:species]
        if y == width - 1:
            copies.append(pltpu.make_async_copy(block.at[x], out.at[x], sems.at[x]))
            copies[-1].start()
    for copy in copies:
        copy.wait()


def correct(pos, adv, halos, coef, field, kept, fix, table, half):
    _, stack, nz = adv.shape
    width = half + 2
    species = coef.shape[1]
    vmem = pl.BlockSpec(memory_space=pltpu.VMEM)
    return pl.pallas_call(
        functools.partial(correct_kernel, half=half),
        in_specs=[vmem] * 12,
        out_specs=pl.BlockSpec(memory_space=pltpu.HBM),
        out_shape=jax.ShapeDtypeStruct((width, width, species, nz), F32),
        scratch_shapes=[
            pltpu.VMEM((width, width, species, nz), F32),
            pltpu.VMEM((4, halos[0].shape[0] + stack, nz), F32),
            pltpu.SemaphoreType.DMA((width,)),
        ],
        compiler_params=pltpu.CompilerParams(vmem_limit_bytes=LIMIT),
        cost_estimate=pl.CostEstimate(
            flops=20 * adv.size, bytes_accessed=12 * adv.size, transcendentals=0
        ),
        name="coarse_correct",
    )(
        pos,
        adv,
        *halos,
        coef,
        field,
        kept,
        fix,
        jnp.asarray(table["average"]),
        jnp.asarray(table["place"]),
    )


def ring(axis, by):
    count = lax.axis_size(axis)
    return [(i, (i + by) % count) for i in range(count)]


def mutual(axis, by):
    count = lax.axis_size(axis)
    one_way = [(i, (i + by) % count) for i in range(0, count, 2)]
    return one_way + [(j, i) for i, j in one_way]


def partner(me, k, count):
    return me ^ k if count & (count - 1) == 0 else lax.rem(me + k, count)


def origin(me, source, count):
    return me ^ source if count & (count - 1) == 0 else lax.rem(me - source + count, count)


def local(coarse_state, fine_state, diffusion, rate, box_pos, box_owner):
    species, width = coarse_state.shape[:2]
    half = width - 2
    stack = padded(species, 8)
    count = lax.axis_size("yz")
    me = lax.axis_index("yz")
    pos, owner = box_pos[0], box_owner[0]
    table = tables(width, pos.shape[1])
    coef = diffusion[None]
    c = jnp.transpose(coarse_state, (1, 2, 0, 3))

    fine = jnp.transpose(fine_state, (1, 0, 2))
    near, far, own, *others = pack_y(c, fine)
    x_high = pack_x(c, own, c.shape[0] - 1)
    x_low = pack_x(c, x_high, 0)
    halos = [
        lax.ppermute(x_high, "gx", ring("gx", 1)),
        lax.ppermute(x_low, "gx", ring("gx", -1)),
        lax.ppermute(near, "yz", mutual("yz", 1)),
        lax.ppermute(far, "yz", mutual("yz", -1)),
    ]
    others = [lax.ppermute(slot, "yz", ring("yz", 2 + k)) for k, slot in enumerate(others)]

    adv, old, new, mix, spread, ghost = coarse_part(
        pos, c, rate, coef, table, stack, x_low
    )
    from_y, start = y_faces(
        pos, owner, *halos[2:], halos[0], own, old, others, half, stack
    )
    made = fine_part(
        pos, owner, halos[1], start, old, new, mix, coef, spread, ghost, from_y, count, 2 * half
    )
    packets, (fix, kept, field) = made[:count], made[count:]

    def swap(value, k):
        even = count & (count - 1) == 0
        pairs = [(i, i ^ k if even else (i + k) % count) for i in range(count)]
        return lax.ppermute(value, "yz", pairs)

    back = [swap(packets[k], k) for k in range(count - 1, 0, -1)][::-1]
    back = [packets[0]] + back
    coarse_next = correct(pos, adv, halos, coef, field, kept, fix, table, half)

    source = lax.broadcasted_iota(jnp.int32, (count, 1, 1), 0)
    turn = origin(me, source, count)
    fine_next = jnp.broadcast_to(back[0][None], (count,) + back[0].shape)
    for k in range(1, count):
        fine_next = jnp.where(turn == k, back[k][None], fine_next)
    return jnp.transpose(coarse_next, (2, 0, 1, 3)), fine_next


def solution(mesh):
    in_specs = (
        P(None, "gx", "yz", None),
        P(("gx", "yz"), None, None),
        P(),
        P(),
        P("gx", "yz", None),
        P("gx", "yz", None),
    )
    out_specs = (P(None, "gx", "yz", None), P(("gx", "yz"), None, None))
    return jax.shard_map(local, mesh=mesh, in_specs=in_specs, out_specs=out_specs, check_vma=False)
```

```python
import functools

import jax
import jax.numpy as jnp
import numpy as np
from jax import lax
from jax.experimental import pallas as pl
from jax.experimental.pallas import tpu as pltpu
from jax.sharding import PartitionSpec as P

F32 = jnp.float32
BF16 = jnp.bfloat16
LIMIT = 12 * 1024 * 1024
PATCH = 256
ORDER = 20_000_000


def padded(count, unit):
    return -(-count // unit) * unit


@functools.lru_cache(maxsize=None)
def tables(width, boxes):
    half = width - 2
    edge = 2 * half
    cells = width**3
    lanes = padded(cells, PATCH)
    fine = edge**3
    spread = np.zeros((lanes, fine), np.float32)
    average = np.zeros((fine, lanes), np.float32)
    halo = padded(boxes * 4 * half * half, 128)
    place = np.zeros((halo, lanes), np.float32)

    def cell(x, y, z):
        return (x * width + y) * width + z

    for number in range(6):
        axis, high = divmod(number, 2)
        others = [a for a in range(3) if a != axis]
        for r in range(half):
            for q in range(half):
                at = [0, 0, 0]
                at[axis] = width - 1 if high else 0
                at[others[0]] = r + 1
                at[others[1]] = q + 1
                here = cell(*at)
                for i in range(2):
                    for j in range(2):
                        pos = [0, 0, 0]
                        pos[axis] = edge - 1 if high else 0
                        pos[others[0]] = 2 * r + i
                        pos[others[1]] = 2 * q + j
                        spread[here, (pos[0] * edge + pos[1]) * edge + pos[2]] = 1.0
                if number < 4:
                    for box in range(boxes):
                        place[((box * 4 + number) * half + r) * half + q, here] = 1.0
    for x in range(edge):
        for y in range(edge):
            for z in range(edge):
                average[(x * edge + y) * edge + z, cell(x // 2 + 1, y // 2 + 1, z // 2 + 1)] = 0.125
    return dict(spread=spread, average=average, place=place, ghost=place @ spread)


def column(diffusion, stack):
    species = diffusion.shape[1]
    row = lax.broadcasted_iota(jnp.int32, (stack, species), 0)
    lane = lax.broadcasted_iota(jnp.int32, (stack, species), 1)
    return jnp.sum(jnp.where(row == lane, diffusion[...], 0.0), axis=1, keepdims=True)


def split(value):
    high = value.astype(BF16).astype(F32)
    return high, value - high


def parts(value):
    return jnp.concatenate(split(value), axis=0).astype(BF16)


def dot(a, b):
    return jnp.dot(a, b, preferred_element_type=F32)


def rows_dot(value, table):
    rows = value.shape[0]
    both = dot(parts(value), table)
    return both[:rows] + both[rows:]


GROUP = 5


def mixing(rate, scratch, stack, group):
    species = rate.shape[0]
    size = group * stack
    scratch[...] = jnp.zeros_like(scratch)
    high, low = split(rate[...])
    for b in range(group):
        at = b * stack
        for row, lane, part in ((at, at, high), (at, size + at, high), (size + at, at, low)):
            scratch[row : row + species, lane : lane + species] = part
    return scratch[: 2 * size, : 2 * size].astype(BF16)


def react(mix, fields):
    size = fields.shape[0]
    both = dot(mix, parts(fields))
    return both[:size] + both[size:]


def react_all(mix, fields):
    stack, depth = fields[0].shape
    made = [[] for _ in fields]

    def product(blocks):
        size = len(blocks[0])
        blank = [jnp.zeros_like(blocks[0][0])] * (GROUP - size)
        columns = [jnp.concatenate(block + blank, axis=0) for block in blocks]
        out = react(mix, jnp.concatenate(columns, axis=1))
        lanes = out.shape[1] // len(blocks)
        return [
            [out[b * stack : (b + 1) * stack, n * lanes : (n + 1) * lanes] for b in range(size)]
            for n in range(len(blocks))
        ]

    for lane in range(0, depth, 256):
        if lane + 256 <= depth:
            for at in range(0, len(fields), GROUP):
                block = [f[:, lane : lane + 256] for f in fields[at : at + GROUP]]
                for b, value in enumerate(product([block])[0]):
                    made[at + b].append(value)
        else:
            half = -(-len(fields) // 2)
            blocks = [[f[:, lane:] for f in part] for part in (fields[:half], fields[half:])]
            blocks[1] += [jnp.zeros_like(blocks[0][0])] * (half - len(blocks[1]))
            for n, values in enumerate(product(blocks)):
                for b, value in enumerate(values):
                    if n * half + b < len(fields):
                        made[n * half + b].append(value)
    return [jnp.concatenate(value, axis=1) for value in made]


def lanes_of(stack, lanes=128):
    return lax.broadcasted_iota(jnp.int32, (stack, lanes), 1)


def tiles_of(stack, depth, start, width):
    lane = lanes_of(stack)
    masks = []
    for t in range(depth // 128):
        along = lane + (t * 128 - start)
        masks.append((along >= 0) & (along < width))
    return masks


def fold(value, masks):
    out = value[:, :128]
    for t in range(1, len(masks)):
        out = jnp.where(masks[t], value[:, t * 128 : (t + 1) * 128], out)
    return out


def turn(value, by):
    return pltpu.roll(value, by & 127, 1)


def neighbour(me, count, even_up):
    step = jnp.where((me % 2 == 0) == even_up, 1, count - 1)
    return lax.rem(me + step, count)


def layer_rows(width, species, groups=0):
    return padded((width + groups) * species, 16)


def blocks_of(width, species, nz, pieces, slot=0):
    across = nz // 128
    numbers = range(slot * pieces, (slot + 1) * pieces)
    return [((width + n // across) * species, n % across * 128) for n in numbers]


def pack_layer(columns, tmp, species):
    for r, value in enumerate(columns):
        tmp[r * species : (r + 1) * species] = value
    below = len(columns) * species
    tmp[below:] = jnp.zeros((tmp.shape[0] - below, tmp.shape[1]), F32)


def pack_y_kernel(c, fine, near, far, own, *refs):
    others, (layer, tmp, held, rows, sems, fine_sem) = refs[:-6], refs[-6:]
    nx, ny, species, nz = c.shape
    count = fine.shape[1]
    stack = padded(species, 8)
    me = lax.axis_index("yz")
    slots = pltpu.make_async_copy(fine, held, fine_sem)
    slots.start()
    copies = []
    for n, y in enumerate((jnp.where(me % 2 == 0, ny - 1, 0), jnp.where(me % 2 == 0, 0, ny - 1))):
        copies.append(pltpu.make_async_copy(c.at[:, y], layer.at[n], sems.at[n]))
        copies[-1].start()
    slots.wait()
    step = rows.shape[1] // stack
    pieces = rows.shape[0]
    for s in range(species):
        value = held[s].astype(F32)
        for q in range(pieces):
            rows[q, s * step : s * step + count] = value[:, q * 128 : (q + 1) * 128]

    def slot(at):
        return [rows[q, pl.ds(at, species, stride=step), :] for q in range(pieces)]

    own[...] = jnp.concatenate(slot(me), axis=1).astype(BF16)
    for k, out in enumerate(others):
        out[...] = jnp.concatenate(slot(lax.rem(me + 2 + k, count)), axis=1).astype(BF16)
    for n, out in enumerate((far, near)):
        n = 1 - n
        copies[n].wait()
        pack_layer([layer[n, r] for r in range(nx)], tmp, species)
        sent = [slot(neighbour(me, count, n == 0))]
        if n == 0 and relays(count):
            sent.append(slot(lax.rem(me + 2, count)))
        for m, value in enumerate(sent):
            for (row, lane), piece in zip(blocks_of(nx, species, nz, pieces, m), value):
                tmp[row : row + species, lane : lane + 128] = piece
        out[...] = tmp[: out.shape[0]].astype(BF16)


def pack_y(c, fine):
    nx, ny, species, nz = c.shape
    count, cells = fine.shape[1:]
    stack = padded(species, 8)
    vmem = pl.BlockSpec(memory_space=pltpu.VMEM)
    far_rows = layer_rows(nx, species, -(-cells // nz))
    rows = layer_rows(nx, species, -(-2 * cells // nz)) if relays(count) else far_rows
    outs = [jax.ShapeDtypeStruct((n, nz), BF16) for n in (rows, far_rows)]
    direct = 0 if relays(count) else max(count - 3, 0)
    outs += [jax.ShapeDtypeStruct((species, cells), BF16)] * (1 + direct)
    return pl.pallas_call(
        pack_y_kernel,
        in_specs=[pl.BlockSpec(memory_space=pltpu.HBM)] * 2,
        out_specs=[vmem] * len(outs),
        out_shape=outs,
        scratch_shapes=[
            pltpu.VMEM((2, nx, species, nz), F32),
            pltpu.VMEM((rows, nz), F32),
            pltpu.VMEM(fine.shape, BF16),
            pltpu.VMEM((cells // 128, stack * padded(count, 8), 128), F32),
            pltpu.SemaphoreType.DMA((2,)),
            pltpu.SemaphoreType.DMA,
        ],
        compiler_params=pltpu.CompilerParams(vmem_limit_bytes=LIMIT),
        name="pack_y",
    )(
        pltpu.with_memory_space_constraint(c, pltpu.HBM),
        pltpu.with_memory_space_constraint(fine, pltpu.HBM),
    )


def relays(count):
    return count == 4


def relay_kernel(near, after, out, wide, width):
    species, cells = out.shape
    wide[...] = near[...].astype(F32)
    places = blocks_of(width, species, near.shape[1], cells // 128, 1)
    pieces = [wide[row : row + species, lane : lane + 128] for row, lane in places]
    out[...] = jnp.concatenate(pieces, axis=1).astype(BF16)


def relay(near, after, width, species, cells):
    vmem = pl.BlockSpec(memory_space=pltpu.VMEM)
    return pl.pallas_call(
        functools.partial(relay_kernel, width=width),
        in_specs=[vmem, pl.BlockSpec(memory_space=pl.ANY)],
        out_specs=vmem,
        out_shape=jax.ShapeDtypeStruct((species, cells), BF16),
        scratch_shapes=[pltpu.VMEM(near.shape, F32)],
        compiler_params=pltpu.CompilerParams(vmem_limit_bytes=LIMIT),
        name="relay",
    )(near, after)


def pack_x_kernel(c, after, out, tmp, x):
    nx, ny, species, _ = c.shape
    pack_layer([c[x, r] for r in range(ny)], tmp, species)
    out[...] = tmp[...].astype(BF16)


def pack_x(c, after, x):
    nx, ny, species, nz = c.shape
    vmem = pl.BlockSpec(memory_space=pltpu.VMEM)
    shape = (layer_rows(ny, species), nz)
    return pl.pallas_call(
        functools.partial(pack_x_kernel, x=x),
        in_specs=[vmem, pl.BlockSpec(memory_space=pl.ANY)],
        out_specs=vmem,
        out_shape=jax.ShapeDtypeStruct(shape, BF16),
        scratch_shapes=[pltpu.VMEM(shape, F32)],
        compiler_params=pltpu.CompilerParams(vmem_limit_bytes=LIMIT),
        name="pack_x",
    )(c, after)


def coarse_kernel(
    pos, c, rate, coef, spread, ghost, after, adv, old, new, mix, spread16, ghost16, columns, scratch
):
    count, stack, nz = adv.shape
    boxes = pos.shape[1]
    width = c.shape[0]
    mix[...] = mixing(rate, scratch, stack, 2)
    mixed = mixing(rate, scratch, stack, GROUP)
    spread16[...] = spread[...].astype(BF16)
    ghost16[...] = ghost[...].astype(BF16)
    for k in range(count):
        columns[k, c.shape[2] :] = jnp.zeros((stack - c.shape[2], nz), F32)
        columns[k, : c.shape[2]] = c[k // width, k % width]
    diff = column(coef, stack)
    for first in range(0, count, 2 * GROUP):
        some = range(first, min(first + 2 * GROUP, count))
        made = react_all(mixed, [columns[k] for k in some])
        for k in some:
            x, y = k // width, k % width
            mine = columns[k]
            lap = pltpu.roll(mine, 1, 1) + pltpu.roll(mine, nz - 1, 1) - 6.0 * mine
            if x > 0:
                lap = lap + columns[k - width]
            if x < width - 1:
                lap = lap + columns[k + width]
            if y > 0:
                lap = lap + columns[k - 1]
            if y < width - 1:
                lap = lap + columns[k + 1]
            value = mine + diff * lap + made[k - first]
            adv[k] = value
    lanes = old.shape[1]
    cell = lanes_of(stack, lanes) // width
    for i in range(boxes):
        lane = pos[0, i] * width
        start = pl.multiple_of(jnp.minimum(lane // 128, nz // 128 - 2) * 128, 128)
        offset = lane - start
        for source, out in ((columns, old), (adv, new)):
            total = jnp.zeros((stack, lanes), F32)
            for k in range(count):
                if k // width in (0, width - 1) and k % width in (0, width - 1):
                    continue
                part = source[k, :, pl.ds(start, PATCH)]
                moved = pltpu.roll(part, (k * width - offset) & (PATCH - 1), 1)
                total = jnp.where(cell == k, moved, total)
            out[i * stack : (i + 1) * stack] = total


def coarse_part(pos, c, rate, coef, table, stack, after):
    nx, ny, species, nz = c.shape
    boxes = pos.shape[1]
    lanes = padded(nx**3, PATCH)
    vmem = pl.BlockSpec(memory_space=pltpu.VMEM)
    small = jax.ShapeDtypeStruct((boxes * stack, lanes), F32)
    size = padded(2 * GROUP * stack, 128)
    return pl.pallas_call(
        coarse_kernel,
        in_specs=[vmem] * 6 + [pl.BlockSpec(memory_space=pl.ANY)],
        out_specs=[vmem] * 6,
        out_shape=[
            jax.ShapeDtypeStruct((nx * ny, stack, nz), F32),
            small,
            small,
            jax.ShapeDtypeStruct((4 * stack, 4 * stack), BF16),
            jax.ShapeDtypeStruct(table["spread"].shape, BF16),
            jax.ShapeDtypeStruct(table["ghost"].shape, BF16),
        ],
        scratch_shapes=[
            pltpu.VMEM((nx * ny, stack, nz), F32),
            pltpu.VMEM((size, size), F32),
        ],
        compiler_params=pltpu.CompilerParams(vmem_limit_bytes=LIMIT),
        cost_estimate=pl.CostEstimate(
            flops=800 * c.size, bytes_accessed=12 * c.size, transcendentals=0
        ),
        name="coarse_part",
    )(pos, c, rate, coef, jnp.asarray(table["spread"]), jnp.asarray(table["ghost"]), after)


def by_box(total, boxes, half):
    each = 4 * half * half
    lane = lax.broadcasted_iota(jnp.int32, total.shape, 1)
    rows = [
        jnp.where((lane >= i * each) & (lane < (i + 1) * each), total, 0.0) for i in range(boxes)
    ]
    return jnp.concatenate(rows, axis=0)


def gather_faces(pos, layers, faces, half, stack, species, nz, total):
    lane = lanes_of(stack)
    for ref, face in zip(layers, faces):
        for i in range(pos.shape[1]):
            start = pos[0, i] * (half + 2) + 1
            masks = tiles_of(stack, nz, start, half)
            for r in range(half):
                base = ((i * 4 + face) * half + r) * half
                at = (r + 1) * species
                moved = turn(fold(ref[at : at + stack], masks), base - start)
                tiles = []
                for t in range(total.shape[1] // 128):
                    along = lane + (t * 128 - base)
                    here = (along >= 0) & (along < half)
                    tiles.append(jnp.where(here, moved, total[:, t * 128 : (t + 1) * 128]))
                total = tiles[0] if len(tiles) == 1 else jnp.concatenate(tiles, axis=1)
    return total


def y_faces_kernel(pos, owner, near, far, own, after, from_y, start, wide):
    stack = from_y.shape[0]
    species, cells = own.shape
    nz = near.shape[1]
    boxes = pos.shape[1]
    width = far.shape[0] // species - -(-cells // nz)
    half = width - 2
    wide[0] = near[...].astype(F32)
    wide[1, : far.shape[0]] = far[...].astype(F32)
    me, count = lax.axis_index("yz"), lax.axis_size("yz")
    odd = me % 2
    zero = jnp.zeros(from_y.shape, F32)
    layers = (wide.at[0], wide.at[1])
    from_y[...] = gather_faces(pos, layers, (3 - odd, 2 + odd), half, stack, species, nz, zero)
    direct = own[...].astype(F32)
    places = blocks_of(width, species, nz, cells // 128)
    edge = species // 8 * 8
    for i in range(boxes):
        by_near = owner[0, i] == neighbour(me, count, True)
        by_far = owner[0, i] == neighbour(me, count, False)
        at = i * stack
        start[at + edge : at + stack] = jnp.zeros((stack - edge, cells), F32)
        for q, (row, lane) in enumerate(places):
            part = direct[:, q * 128 : (q + 1) * 128]
            sent = [wide[n, row : row + species, lane : lane + 128] for n in range(2)]
            part = jnp.where(by_far, sent[1], jnp.where(by_near, sent[0], part))
            start[at : at + species, q * 128 : (q + 1) * 128] = part


def y_faces(pos, owner, near, far, own, after, half, stack):
    vmem = pl.BlockSpec(memory_space=pltpu.VMEM)
    boxes = pos.shape[1]
    lanes = padded(boxes * 4 * half * half, 128)
    return pl.pallas_call(
        y_faces_kernel,
        in_specs=[vmem] * 5 + [pl.BlockSpec(memory_space=pl.ANY)],
        out_specs=[vmem] * 2,
        out_shape=[
            jax.ShapeDtypeStruct((stack, lanes), F32),
            jax.ShapeDtypeStruct((boxes * stack, own.shape[1]), F32),
        ],
        scratch_shapes=[pltpu.VMEM((2, *near.shape), F32)],
        compiler_params=pltpu.CompilerParams(vmem_limit_bytes=LIMIT),
        cost_estimate=pl.CostEstimate(flops=10**9, bytes_accessed=ORDER, transcendentals=0),
        name="y_faces",
    )(pos, owner, near, far, own, after)


def fine_kernel(pos, owner, x_low, x_high, start, *refs, count, edge):
    others, refs = refs[: count - 3], refs[count - 3 :]
    old, new, mix, coef, spread, ghost, from_y = refs[:7]
    packets = refs[7 : 7 + count]
    fix, kept, final, field, wide = refs[7 + count :]
    species = packets[0].shape[0]
    stack = from_y.shape[0]
    boxes = final.shape[0] // stack
    cells = final.shape[1]
    me = lax.axis_index("yz")
    mixed = mix[...]

    def reaction(value):
        pairs = [value[at : at + 2 * stack] for at in range(0, boxes * stack, 2 * stack)]
        return jnp.concatenate([react(mixed, pair) for pair in pairs], axis=0)

    nz = x_low.shape[1]
    half = edge // 2
    wide[0, : x_low.shape[0]] = x_low[...].astype(F32)
    wide[1, : x_high.shape[0]] = x_high[...].astype(F32)
    sent = [ref[...].astype(F32) for ref in others]
    for i in range(boxes):
        at = i * stack
        field[at : at + stack] = start[at : at + stack]
        back = lax.rem(me - owner[0, i] + count, count)
        value = start[at : at + species]
        for k in range(len(sent)):
            value = jnp.where(back == k + 2, sent[k], value)
        field[at : at + species] = value
    diff = jnp.concatenate([column(coef, stack)] * boxes, axis=0)
    old_v, new_v = old[...], new[...]
    sums = old_v + new_v
    spread_v = spread[...]
    both = rows_dot(jnp.concatenate([old_v, sums], axis=0), spread_v)
    ghost0, ghost1 = both[: boxes * stack], both[boxes * stack :]
    index = lax.broadcasted_iota(jnp.int32, (1, cells), 1)
    at = (index // (edge * edge), index // edge % edge, index % edge)
    step = (edge * edge, edge, 1)

    def inside(value):
        lap = -6.0 * value
        for axis in range(3):
            before = pltpu.roll(value, step[axis], 1)
            after = pltpu.roll(value, cells - step[axis], 1)
            lap = lap + jnp.where(at[axis] == 0, 0.0, before)
            lap = lap + jnp.where(at[axis] == edge - 1, 0.0, after)
        return lap

    first = field[...]
    second = first + 2.0 * diff * (inside(first) + ghost0) + 0.5 * reaction(first)
    base = second + diff * (2.0 * inside(second) + ghost1) + 0.5 * reaction(second)
    layers = (wide.at[0], wide.at[1])
    total = gather_faces(pos, layers, (0, 1), half, stack, species, nz, from_y[...])
    kept[...] = total
    stacked = by_box(total, boxes, half).astype(BF16)
    value = base + diff * diff * dot(stacked, ghost[...])
    final[...] = value
    for k, out in enumerate(packets):
        dest = partner(me, k, count)
        packet = jnp.zeros((species, cells), F32)
        for i in range(boxes):
            packet = jnp.where(owner[0, i] == dest, value[i * stack : i * stack + species], packet)
        out[...] = packet.astype(BF16)
    pooled = lax.dot_general(
        parts(first + second), spread_v, (((1,), (1,)), ((), ())), preferred_element_type=F32
    )
    pooled = 0.25 * (pooled[: boxes * stack] + pooled[boxes * stack :])
    width = edge // 2 + 2
    lanes = old.shape[1]
    lane = lax.broadcasted_iota(jnp.int32, (1, lanes), 1)
    at = (lane // (width * width), lane // width % width, lane % width)
    step = (width * width, width, 1)
    inner = [(a >= 1) & (a <= width - 2) for a in at]
    rest = pooled - 0.5 * sums
    result = jnp.zeros_like(old_v)
    for axis in range(3):
        sides = inner[(axis + 1) % 3] & inner[(axis + 2) % 3]
        for edge_at, shift in ((0, lanes - step[axis]), (width - 1, step[axis])):
            mask = sides & (at[axis] == edge_at)
            fixed = rest - pltpu.roll(old_v, shift, 1)
            result = jnp.where(mask, fixed, result)
    fix[...] = diff * result


def fine_part(pos, owner, low, high, start, others, old, new, mix, coef, spread, ghost, from_y, edge):
    boxes = owner.shape[1]
    count = len(others) + 3
    stack = from_y.shape[0]
    cells = start.shape[1]
    vmem = pl.BlockSpec(memory_space=pltpu.VMEM)
    return pl.pallas_call(
        functools.partial(fine_kernel, count=count, edge=edge),
        in_specs=[vmem] * (count + 9),
        out_specs=[vmem] * (count + 3),
        out_shape=[jax.ShapeDtypeStruct((coef.shape[1], cells), BF16)] * count
        + [
            jax.ShapeDtypeStruct((boxes * stack, old.shape[1]), F32),
            jax.ShapeDtypeStruct(from_y.shape, F32),
            jax.ShapeDtypeStruct((boxes * stack, cells), F32),
        ],
        scratch_shapes=[
            pltpu.VMEM((boxes * stack, cells), F32),
            pltpu.VMEM((2, *low.shape), F32),
        ],
        compiler_params=pltpu.CompilerParams(vmem_limit_bytes=LIMIT),
        name="fine_part",
    )(pos, owner, low, high, start, *others, old, new, mix, coef, spread, ghost, from_y)


def delta_of(field, kept, fix, coef, average, place, half, stack):
    boxes = field.shape[0] // stack
    diffs = jnp.concatenate([column(coef, stack)] * boxes, axis=0)
    stacked = by_box(kept[...], boxes, half).astype(BF16)
    halo = dot(stacked, place[...].astype(BF16))
    means = rows_dot(field[...], average[...].astype(BF16))
    return fix[...] - 0.5 * diffs * diffs * halo + means


def correct_kernel(
    pos, adv, x_first, x_second, near, far, coef, field, kept, fix, average, place, out, block, wide, sems, half
):
    count, stack, nz = adv.shape
    species = block.shape[2]
    width = half + 2
    delta = delta_of(field, kept, fix, coef, average, place, half, stack)
    diff = column(coef, stack)
    even = lax.axis_index("yz") % 2 == 0
    rows = x_first.shape[0]
    near_v, far_v = near[:rows].astype(F32), far[:rows].astype(F32)
    wide[0, :rows] = x_first[...].astype(F32)
    wide[1, : x_second.shape[0]] = x_second[...].astype(F32)
    wide[2, :rows] = jnp.where(even, far_v, near_v)
    wide[3, :rows] = jnp.where(even, near_v, far_v)
    boxes = delta.shape[0] // stack
    starts = [pos[0, i] * width for i in range(boxes)]
    cycle = [tiles_of(stack, nz, start, width) for start in starts]
    inside = [tiles_of(stack, nz, start + 1, half) for start in starts]
    lane = lanes_of(stack)
    copies = []
    for k in range(count):
        x, y = k // width, k % width
        value = adv[k]
        for there, at, n in (
            (x == 0, y, 0),
            (x == width - 1, y, 1),
            (y == 0, x, 2),
            (y == width - 1, x, 3),
        ):
            if there:
                value = value + diff * wide[n, at * species : at * species + stack]
        if x not in (0, width - 1) or y not in (0, width - 1):
            tiles = [value[:, t * 128 : (t + 1) * 128] for t in range(nz // 128)]
            covers = 0 < x < width - 1 and 0 < y < width - 1
            for i in range(boxes):
                mine = delta[i * stack : (i + 1) * stack]
                t = k * width // 128
                part = mine[:, t * 128 : (t + 1) * 128]
                if (k + 1) * width > (t + 1) * 128:
                    after = mine[:, (t + 1) * 128 : (t + 2) * 128]
                    part = jnp.where(lane < (k + 1) * width - (t + 1) * 128, after, part)
                moved = turn(part, starts[i] - k * width)
                for t in range(nz // 128):
                    if covers:
                        tiles[t] = jnp.where(inside[i][t], 0.0, tiles[t])
                    tiles[t] = tiles[t] + jnp.where(cycle[i][t], moved, 0.0)
            value = jnp.concatenate(tiles, axis=1)
        block[x, y] = value[:species]
        if y == width - 1:
            copies.append(pltpu.make_async_copy(block.at[x], out.at[x], sems.at[x]))
            copies[-1].start()
    for copy in copies:
        copy.wait()


def correct(pos, adv, halos, coef, field, kept, fix, table, half):
    _, stack, nz = adv.shape
    width = half + 2
    species = coef.shape[1]
    vmem = pl.BlockSpec(memory_space=pltpu.VMEM)
    return pl.pallas_call(
        functools.partial(correct_kernel, half=half),
        in_specs=[vmem] * 12,
        out_specs=pl.BlockSpec(memory_space=pltpu.HBM),
        out_shape=jax.ShapeDtypeStruct((width, width, species, nz), F32),
        scratch_shapes=[
            pltpu.VMEM((width, width, species, nz), F32),
            pltpu.VMEM((4, halos[0].shape[0] + stack, nz), F32),
            pltpu.SemaphoreType.DMA((width,)),
        ],
        compiler_params=pltpu.CompilerParams(vmem_limit_bytes=LIMIT),
        cost_estimate=pl.CostEstimate(
            flops=20 * adv.size, bytes_accessed=12 * adv.size, transcendentals=0
        ),
        name="coarse_correct",
    )(
        pos,
        adv,
        *halos,
        coef,
        field,
        kept,
        fix,
        jnp.asarray(table["average"]),
        jnp.asarray(table["place"]),
    )


def unpack_kernel(*refs):
    packets, (out, rows) = refs[:-2], refs[-2:]
    species, cells = packets[0].shape
    count = len(packets)
    step = rows.shape[1] // padded(species, 8)
    me = lax.axis_index("yz")
    for n, packet in enumerate(packets):
        source = origin(me, (count - n) % count, count)
        value = packet[...].astype(F32)
        for q in range(cells // 128):
            rows[q, pl.ds(source, species, stride=step), :] = value[:, q * 128 : (q + 1) * 128]
    for s in range(species):
        pieces = [rows[q, s * step : s * step + count] for q in range(cells // 128)]
        out[s] = jnp.concatenate(pieces, axis=1).astype(BF16)


def unpack(packets):
    species, cells = packets[0].shape
    count = len(packets)
    vmem = pl.BlockSpec(memory_space=pltpu.VMEM)
    rows = padded(species, 8) * padded(count, 8)
    return pl.pallas_call(
        unpack_kernel,
        in_specs=[vmem] * count,
        out_specs=vmem,
        out_shape=jax.ShapeDtypeStruct((species, count, cells), BF16),
        scratch_shapes=[pltpu.VMEM((cells // 128, rows, 128), F32)],
        compiler_params=pltpu.CompilerParams(vmem_limit_bytes=LIMIT),
        name="unpack",
    )(packets[0], *packets[:0:-1])


def ring(axis, by):
    count = lax.axis_size(axis)
    return [(i, (i + by) % count) for i in range(count)]


def mutual(axis, by):
    count = lax.axis_size(axis)
    one_way = [(i, (i + by) % count) for i in range(0, count, 2)]
    return one_way + [(j, i) for i, j in one_way]


def partner(me, k, count):
    return me ^ k if count & (count - 1) == 0 else lax.rem(me + k, count)


def origin(me, source, count):
    return me ^ source if count & (count - 1) == 0 else lax.rem(me - source + count, count)


def local(coarse_state, fine_state, diffusion, rate, box_pos, box_owner):
    species, width = coarse_state.shape[:2]
    half = width - 2
    stack = padded(species, 8)
    count = lax.axis_size("yz")
    me = lax.axis_index("yz")
    pos, owner = box_pos[0], box_owner[0]
    table = tables(width, pos.shape[1])
    coef = diffusion[None]
    c = jnp.transpose(coarse_state, (1, 2, 0, 3))

    fine = jnp.transpose(fine_state, (1, 0, 2))
    near, far, own, *others = pack_y(c, fine)
    x_high = pack_x(c, own, c.shape[0] - 1)
    x_low = pack_x(c, x_high, 0)
    halos = [
        lax.ppermute(x_high, "gx", ring("gx", 1)),
        lax.ppermute(x_low, "gx", ring("gx", -1)),
        lax.ppermute(near, "yz", mutual("yz", 1)),
        lax.ppermute(far, "yz", mutual("yz", -1)),
    ]
    if relays(count):
        after = passed = relay(halos[2], x_low, width, *own.shape)
        others = [lax.ppermute(passed, "yz", mutual("yz", -1))]
    else:
        after = x_low
        others = [lax.ppermute(slot, "yz", ring("yz", 2 + k)) for k, slot in enumerate(others)]

    adv, old, new, mix, spread, ghost = coarse_part(
        pos, c, rate, coef, table, stack, after
    )
    from_y, start = y_faces(pos, owner, *halos[2:], own, old, half, stack)
    made = fine_part(
        pos, owner, *halos[:2], start, others, old, new, mix, coef, spread, ghost, from_y, 2 * half
    )
    packets, (fix, kept, field) = made[:count], made[count:]

    def swap(value, k):
        even = count & (count - 1) == 0
        pairs = [(i, i ^ k if even else (i + k) % count) for i in range(count)]
        return lax.ppermute(value, "yz", pairs)

    back = [packets[0]] + [swap(packets[k], k) for k in range(1, count)]
    coarse_next = correct(pos, adv, halos, coef, field, kept, fix, table, half)

    fine_next = jnp.transpose(unpack(back), (1, 0, 2))
    return jnp.transpose(coarse_next, (2, 0, 1, 3)), fine_next


def solution(mesh):
    in_specs = (
        P(None, "gx", "yz", None),
        P(("gx", "yz"), None, None),
        P(),
        P(),
        P("gx", "yz", None),
        P("gx", "yz", None),
    )
    out_specs = (P(None, "gx", "yz", None), P(("gx", "yz"), None, None))
    return jax.shard_map(local, mesh=mesh, in_specs=in_specs, out_specs=out_specs, check_vma=False)
```

```python
import functools

import jax
import jax.numpy as jnp
import numpy as np
from jax import lax
from jax.experimental import pallas as pl
from jax.experimental.pallas import tpu as pltpu
from jax.sharding import PartitionSpec as P

F32 = jnp.float32
BF16 = jnp.bfloat16
LIMIT = 12 * 1024 * 1024
PATCH = 256
ORDER = 20_000_000


def padded(count, unit):
    return -(-count // unit) * unit


@functools.lru_cache(maxsize=None)
def tables(width, boxes):
    half = width - 2
    edge = 2 * half
    cells = width**3
    lanes = padded(cells, PATCH)
    fine = edge**3
    spread = np.zeros((lanes, fine), np.float32)
    average = np.zeros((fine, lanes), np.float32)
    halo = padded(boxes * 4 * half * half, 128)
    place = np.zeros((halo, lanes), np.float32)

    def cell(x, y, z):
        return (x * width + y) * width + z

    for number in range(6):
        axis, high = divmod(number, 2)
        others = [a for a in range(3) if a != axis]
        for r in range(half):
            for q in range(half):
                at = [0, 0, 0]
                at[axis] = width - 1 if high else 0
                at[others[0]] = r + 1
                at[others[1]] = q + 1
                here = cell(*at)
                for i in range(2):
                    for j in range(2):
                        pos = [0, 0, 0]
                        pos[axis] = edge - 1 if high else 0
                        pos[others[0]] = 2 * r + i
                        pos[others[1]] = 2 * q + j
                        spread[here, (pos[0] * edge + pos[1]) * edge + pos[2]] = 1.0
                if number < 4:
                    for box in range(boxes):
                        place[((box * 4 + number) * half + r) * half + q, here] = 1.0
    for x in range(edge):
        for y in range(edge):
            for z in range(edge):
                average[(x * edge + y) * edge + z, cell(x // 2 + 1, y // 2 + 1, z // 2 + 1)] = 0.125
    return dict(spread=spread, average=average, place=place, ghost=place @ spread)


def column(diffusion, stack):
    species = diffusion.shape[1]
    row = lax.broadcasted_iota(jnp.int32, (stack, species), 0)
    lane = lax.broadcasted_iota(jnp.int32, (stack, species), 1)
    return jnp.sum(jnp.where(row == lane, diffusion[...], 0.0), axis=1, keepdims=True)


def split(value):
    high = value.astype(BF16).astype(F32)
    return high, value - high


def parts(value):
    return jnp.concatenate(split(value), axis=0).astype(BF16)


def dot(a, b):
    return jnp.dot(a, b, preferred_element_type=F32)


def rows_dot(value, table):
    rows = value.shape[0]
    both = dot(parts(value), table)
    return both[:rows] + both[rows:]


GROUP = 5


def mixing(rate, scratch, stack, group):
    species = rate.shape[0]
    size = group * stack
    scratch[...] = jnp.zeros_like(scratch)
    high, low = split(rate[...])
    for b in range(group):
        at = b * stack
        for row, lane, part in ((at, at, high), (at, size + at, high), (size + at, at, low)):
            scratch[row : row + species, lane : lane + species] = part
    return scratch[: 2 * size, : 2 * size].astype(BF16)


def react(mix, fields):
    size = fields.shape[0]
    both = dot(mix, parts(fields))
    return both[:size] + both[size:]


def react_all(mix, fields):
    stack, depth = fields[0].shape
    made = [[] for _ in fields]

    def product(blocks):
        size = len(blocks[0])
        blank = [jnp.zeros_like(blocks[0][0])] * (GROUP - size)
        columns = [jnp.concatenate(block + blank, axis=0) for block in blocks]
        out = react(mix, jnp.concatenate(columns, axis=1))
        lanes = out.shape[1] // len(blocks)
        return [
            [out[b * stack : (b + 1) * stack, n * lanes : (n + 1) * lanes] for b in range(size)]
            for n in range(len(blocks))
        ]

    for lane in range(0, depth, 256):
        if lane + 256 <= depth:
            for at in range(0, len(fields), GROUP):
                block = [f[:, lane : lane + 256] for f in fields[at : at + GROUP]]
                for b, value in enumerate(product([block])[0]):
                    made[at + b].append(value)
        else:
            half = -(-len(fields) // 2)
            blocks = [[f[:, lane:] for f in part] for part in (fields[:half], fields[half:])]
            blocks[1] += [jnp.zeros_like(blocks[0][0])] * (half - len(blocks[1]))
            for n, values in enumerate(product(blocks)):
                for b, value in enumerate(values):
                    if n * half + b < len(fields):
                        made[n * half + b].append(value)
    return [jnp.concatenate(value, axis=1) for value in made]


def lanes_of(stack, lanes=128):
    return lax.broadcasted_iota(jnp.int32, (stack, lanes), 1)


def tiles_of(stack, depth, start, width):
    lane = lanes_of(stack)
    masks = []
    for t in range(depth // 128):
        along = lane + (t * 128 - start)
        masks.append((along >= 0) & (along < width))
    return masks


def fold(value, masks):
    out = value[:, :128]
    for t in range(1, len(masks)):
        out = jnp.where(masks[t], value[:, t * 128 : (t + 1) * 128], out)
    return out


def turn(value, by):
    return pltpu.roll(value, by & 127, 1)


def neighbour(me, count, even_up):
    step = jnp.where((me % 2 == 0) == even_up, 1, count - 1)
    return lax.rem(me + step, count)


def layer_rows(width, species, groups=0):
    return padded((width + groups) * species, 16)


def blocks_of(width, species, nz, pieces, slot=0):
    across = nz // 128
    numbers = range(slot * pieces, (slot + 1) * pieces)
    return [((width + n // across) * species, n % across * 128) for n in numbers]


def pack_layer(columns, tmp, species):
    for r, value in enumerate(columns):
        tmp[r * species : (r + 1) * species] = value
    below = len(columns) * species
    tmp[below:] = jnp.zeros((tmp.shape[0] - below, tmp.shape[1]), F32)


def pack_y_kernel(c, fine, near, far, own, *refs):
    others, (layer, tmp, held, rows, sems, fine_sem) = refs[:-6], refs[-6:]
    nx, ny, species, nz = c.shape
    count = fine.shape[1]
    stack = padded(species, 8)
    me = lax.axis_index("yz")
    slots = pltpu.make_async_copy(fine, held, fine_sem)
    slots.start()
    copies = []
    for n, y in enumerate((jnp.where(me % 2 == 0, ny - 1, 0), jnp.where(me % 2 == 0, 0, ny - 1))):
        copies.append(pltpu.make_async_copy(c.at[:, y], layer.at[n], sems.at[n]))
        copies[-1].start()
    slots.wait()
    step = rows.shape[1] // stack
    pieces = rows.shape[0]
    for s in range(species):
        value = held[s].astype(F32)
        for q in range(pieces):
            rows[q, s * step : s * step + count] = value[:, q * 128 : (q + 1) * 128]

    def slot(at):
        return [rows[q, pl.ds(at, species, stride=step), :] for q in range(pieces)]

    own[...] = jnp.concatenate(slot(me), axis=1).astype(BF16)
    for k, out in enumerate(others):
        out[...] = jnp.concatenate(slot(lax.rem(me + 2 + k, count)), axis=1).astype(BF16)
    for n, out in enumerate((far, near)):
        n = 1 - n
        copies[n].wait()
        pack_layer([layer[n, r] for r in range(nx)], tmp, species)
        sent = [slot(neighbour(me, count, n == 0))]
        if n == 0 and relays(count):
            sent.append(slot(lax.rem(me + 2, count)))
        for m, value in enumerate(sent):
            for (row, lane), piece in zip(blocks_of(nx, species, nz, pieces, m), value):
                tmp[row : row + species, lane : lane + 128] = piece
        out[...] = tmp[: out.shape[0]].astype(BF16)


def pack_y(c, fine):
    nx, ny, species, nz = c.shape
    count, cells = fine.shape[1:]
    stack = padded(species, 8)
    vmem = pl.BlockSpec(memory_space=pltpu.VMEM)
    far_rows = layer_rows(nx, species, -(-cells // nz))
    rows = layer_rows(nx, species, -(-2 * cells // nz)) if relays(count) else far_rows
    outs = [jax.ShapeDtypeStruct((n, nz), BF16) for n in (rows, far_rows)]
    direct = 0 if relays(count) else max(count - 3, 0)
    outs += [jax.ShapeDtypeStruct((species, cells), BF16)] * (1 + direct)
    return pl.pallas_call(
        pack_y_kernel,
        in_specs=[pl.BlockSpec(memory_space=pltpu.HBM)] * 2,
        out_specs=[vmem] * len(outs),
        out_shape=outs,
        scratch_shapes=[
            pltpu.VMEM((2, nx, species, nz), F32),
            pltpu.VMEM((rows, nz), F32),
            pltpu.VMEM(fine.shape, BF16),
            pltpu.VMEM((cells // 128, stack * padded(count, 8), 128), F32),
            pltpu.SemaphoreType.DMA((2,)),
            pltpu.SemaphoreType.DMA,
        ],
        compiler_params=pltpu.CompilerParams(vmem_limit_bytes=LIMIT),
        name="pack_y",
    )(
        pltpu.with_memory_space_constraint(c, pltpu.HBM),
        pltpu.with_memory_space_constraint(fine, pltpu.HBM),
    )


def relays(count):
    return count == 4


def relay_kernel(near, after, out, wide, width):
    species, cells = out.shape
    wide[...] = near[...].astype(F32)
    places = blocks_of(width, species, near.shape[1], cells // 128, 1)
    pieces = [wide[row : row + species, lane : lane + 128] for row, lane in places]
    out[...] = jnp.concatenate(pieces, axis=1).astype(BF16)


def relay(near, after, width, species, cells):
    vmem = pl.BlockSpec(memory_space=pltpu.VMEM)
    return pl.pallas_call(
        functools.partial(relay_kernel, width=width),
        in_specs=[vmem, pl.BlockSpec(memory_space=pl.ANY)],
        out_specs=vmem,
        out_shape=jax.ShapeDtypeStruct((species, cells), BF16),
        scratch_shapes=[pltpu.VMEM(near.shape, F32)],
        compiler_params=pltpu.CompilerParams(vmem_limit_bytes=LIMIT),
        name="relay",
    )(near, after)


def pack_x_kernel(c, after, out, tmp, x):
    nx, ny, species, _ = c.shape
    pack_layer([c[x, r] for r in range(ny)], tmp, species)
    out[...] = tmp[...].astype(BF16)


def pack_x(c, after, x):
    nx, ny, species, nz = c.shape
    vmem = pl.BlockSpec(memory_space=pltpu.VMEM)
    shape = (layer_rows(ny, species), nz)
    return pl.pallas_call(
        functools.partial(pack_x_kernel, x=x),
        in_specs=[vmem, pl.BlockSpec(memory_space=pl.ANY)],
        out_specs=vmem,
        out_shape=jax.ShapeDtypeStruct(shape, BF16),
        scratch_shapes=[pltpu.VMEM(shape, F32)],
        compiler_params=pltpu.CompilerParams(vmem_limit_bytes=LIMIT),
        name="pack_x",
    )(c, after)


def coarse_kernel(
    pos, c, rate, coef, spread, ghost, after, adv, old, new, mix, spread16, ghost16, columns, scratch
):
    count, stack, nz = adv.shape
    boxes = pos.shape[1]
    width = c.shape[0]
    mix[...] = mixing(rate, scratch, stack, 2)
    mixed = mixing(rate, scratch, stack, GROUP)
    spread16[...] = spread[...].astype(BF16)
    ghost16[...] = ghost[...].astype(BF16)
    for k in range(count):
        columns[k, c.shape[2] :] = jnp.zeros((stack - c.shape[2], nz), F32)
        columns[k, : c.shape[2]] = c[k // width, k % width]
    diff = column(coef, stack)
    for first in range(0, count, 2 * GROUP):
        some = range(first, min(first + 2 * GROUP, count))
        made = react_all(mixed, [columns[k] for k in some])
        for k in some:
            x, y = k // width, k % width
            mine = columns[k]
            lap = pltpu.roll(mine, 1, 1) + pltpu.roll(mine, nz - 1, 1) - 6.0 * mine
            if x > 0:
                lap = lap + columns[k - width]
            if x < width - 1:
                lap = lap + columns[k + width]
            if y > 0:
                lap = lap + columns[k - 1]
            if y < width - 1:
                lap = lap + columns[k + 1]
            value = mine + diff * lap + made[k - first]
            adv[k] = value
    lanes = old.shape[1]
    cell = lanes_of(stack, lanes) // width
    for i in range(boxes):
        lane = pos[0, i] * width
        start = pl.multiple_of(jnp.minimum(lane // 128, nz // 128 - 2) * 128, 128)
        offset = lane - start
        for source, out in ((columns, old), (adv, new)):
            total = jnp.zeros((stack, lanes), F32)
            for k in range(count):
                if k // width in (0, width - 1) and k % width in (0, width - 1):
                    continue
                part = source[k, :, pl.ds(start, PATCH)]
                moved = pltpu.roll(part, (k * width - offset) & (PATCH - 1), 1)
                total = jnp.where(cell == k, moved, total)
            out[i * stack : (i + 1) * stack] = total


def coarse_part(pos, c, rate, coef, table, stack, after):
    nx, ny, species, nz = c.shape
    boxes = pos.shape[1]
    lanes = padded(nx**3, PATCH)
    vmem = pl.BlockSpec(memory_space=pltpu.VMEM)
    small = jax.ShapeDtypeStruct((boxes * stack, lanes), F32)
    size = padded(2 * GROUP * stack, 128)
    return pl.pallas_call(
        coarse_kernel,
        in_specs=[vmem] * 6 + [pl.BlockSpec(memory_space=pl.ANY)],
        out_specs=[vmem] * 6,
        out_shape=[
            jax.ShapeDtypeStruct((nx * ny, stack, nz), F32),
            small,
            small,
            jax.ShapeDtypeStruct((4 * stack, 4 * stack), BF16),
            jax.ShapeDtypeStruct(table["spread"].shape, BF16),
            jax.ShapeDtypeStruct(table["ghost"].shape, BF16),
        ],
        scratch_shapes=[
            pltpu.VMEM((nx * ny, stack, nz), F32),
            pltpu.VMEM((size, size), F32),
        ],
        compiler_params=pltpu.CompilerParams(vmem_limit_bytes=LIMIT),
        cost_estimate=pl.CostEstimate(
            flops=800 * c.size, bytes_accessed=12 * c.size, transcendentals=0
        ),
        name="coarse_part",
    )(pos, c, rate, coef, jnp.asarray(table["spread"]), jnp.asarray(table["ghost"]), after)


def by_box(total, boxes, half):
    each = 4 * half * half
    lane = lax.broadcasted_iota(jnp.int32, total.shape, 1)
    rows = [
        jnp.where((lane >= i * each) & (lane < (i + 1) * each), total, 0.0) for i in range(boxes)
    ]
    return jnp.concatenate(rows, axis=0)


def gather_faces(pos, layers, faces, half, stack, species, nz, total):
    lane = lanes_of(stack)
    for ref, face in zip(layers, faces):
        for i in range(pos.shape[1]):
            start = pos[0, i] * (half + 2) + 1
            masks = tiles_of(stack, nz, start, half)
            for r in range(half):
                base = ((i * 4 + face) * half + r) * half
                at = (r + 1) * species
                moved = turn(fold(ref[at : at + stack], masks), base - start)
                tiles = []
                for t in range(total.shape[1] // 128):
                    along = lane + (t * 128 - base)
                    here = (along >= 0) & (along < half)
                    tiles.append(jnp.where(here, moved, total[:, t * 128 : (t + 1) * 128]))
                total = tiles[0] if len(tiles) == 1 else jnp.concatenate(tiles, axis=1)
    return total


def y_faces_kernel(pos, owner, near, far, own, after, from_y, start, wide):
    stack = from_y.shape[0]
    species, cells = own.shape
    nz = near.shape[1]
    boxes = pos.shape[1]
    width = far.shape[0] // species - -(-cells // nz)
    half = width - 2
    wide[0] = near[...].astype(F32)
    wide[1, : far.shape[0]] = far[...].astype(F32)
    me, count = lax.axis_index("yz"), lax.axis_size("yz")
    odd = me % 2
    zero = jnp.zeros(from_y.shape, F32)
    layers = (wide.at[0], wide.at[1])
    from_y[...] = gather_faces(pos, layers, (3 - odd, 2 + odd), half, stack, species, nz, zero)
    direct = own[...].astype(F32)
    places = blocks_of(width, species, nz, cells // 128)
    edge = species // 8 * 8
    for i in range(boxes):
        by_near = owner[0, i] == neighbour(me, count, True)
        by_far = owner[0, i] == neighbour(me, count, False)
        at = i * stack
        start[at + edge : at + stack] = jnp.zeros((stack - edge, cells), F32)
        for q, (row, lane) in enumerate(places):
            part = direct[:, q * 128 : (q + 1) * 128]
            sent = [wide[n, row : row + species, lane : lane + 128] for n in range(2)]
            part = jnp.where(by_far, sent[1], jnp.where(by_near, sent[0], part))
            start[at : at + species, q * 128 : (q + 1) * 128] = part


def y_faces(pos, owner, near, far, own, after, half, stack):
    vmem = pl.BlockSpec(memory_space=pltpu.VMEM)
    boxes = pos.shape[1]
    lanes = padded(boxes * 4 * half * half, 128)
    return pl.pallas_call(
        y_faces_kernel,
        in_specs=[vmem] * 5 + [pl.BlockSpec(memory_space=pl.ANY)],
        out_specs=[vmem] * 2,
        out_shape=[
            jax.ShapeDtypeStruct((stack, lanes), F32),
            jax.ShapeDtypeStruct((boxes * stack, own.shape[1]), F32),
        ],
        scratch_shapes=[pltpu.VMEM((2, *near.shape), F32)],
        compiler_params=pltpu.CompilerParams(vmem_limit_bytes=LIMIT),
        cost_estimate=pl.CostEstimate(flops=10**9, bytes_accessed=ORDER, transcendentals=0),
        name="y_faces",
    )(pos, owner, near, far, own, after)


def fine_kernel(pos, owner, x_low, x_high, start, *refs, count, edge):
    others, refs = refs[: count - 3], refs[count - 3 :]
    old, new, mix, coef, spread, ghost, from_y = refs[:7]
    packets = refs[7 : 7 + count]
    fix, kept, final, field, wide = refs[7 + count :]
    species = packets[0].shape[0]
    stack = from_y.shape[0]
    boxes = final.shape[0] // stack
    cells = final.shape[1]
    me = lax.axis_index("yz")
    mixed = mix[...]

    def reaction(value):
        pairs = [value[at : at + 2 * stack] for at in range(0, boxes * stack, 2 * stack)]
        return jnp.concatenate([react(mixed, pair) for pair in pairs], axis=0)

    nz = x_low.shape[1]
    half = edge // 2
    wide[0, : x_low.shape[0]] = x_low[...].astype(F32)
    wide[1, : x_high.shape[0]] = x_high[...].astype(F32)
    sent = [ref[...].astype(F32) for ref in others]
    for i in range(boxes):
        at = i * stack
        field[at : at + stack] = start[at : at + stack]
        back = lax.rem(me - owner[0, i] + count, count)
        value = start[at : at + species]
        for k in range(len(sent)):
            value = jnp.where(back == k + 2, sent[k], value)
        field[at : at + species] = value
    diff = jnp.concatenate([column(coef, stack)] * boxes, axis=0)
    old_v, new_v = old[...], new[...]
    sums = old_v + new_v
    spread_v = spread[...]
    both = rows_dot(jnp.concatenate([old_v, sums], axis=0), spread_v)
    ghost0, ghost1 = both[: boxes * stack], both[boxes * stack :]
    index = lax.broadcasted_iota(jnp.int32, (1, cells), 1)
    at = (index // (edge * edge), index // edge % edge, index % edge)
    step = (edge * edge, edge, 1)

    def inside(value):
        lap = -6.0 * value
        for axis in range(3):
            before = pltpu.roll(value, step[axis], 1)
            after = pltpu.roll(value, cells - step[axis], 1)
            lap = lap + jnp.where(at[axis] == 0, 0.0, before)
            lap = lap + jnp.where(at[axis] == edge - 1, 0.0, after)
        return lap

    first = field[...]
    second = first + 2.0 * diff * (inside(first) + ghost0) + 0.5 * reaction(first)
    base = second + diff * (2.0 * inside(second) + ghost1) + 0.5 * reaction(second)
    layers = (wide.at[0], wide.at[1])
    total = gather_faces(pos, layers, (0, 1), half, stack, species, nz, from_y[...])
    kept[...] = total
    stacked = by_box(total, boxes, half).astype(BF16)
    value = base + diff * diff * dot(stacked, ghost[...])
    final[...] = value
    for k, out in enumerate(packets):
        dest = partner(me, k, count)
        packet = jnp.zeros((species, cells), F32)
        for i in range(boxes):
            packet = jnp.where(owner[0, i] == dest, value[i * stack : i * stack + species], packet)
        out[...] = packet.astype(BF16)
    pooled = lax.dot_general(
        parts(first + second), spread_v, (((1,), (1,)), ((), ())), preferred_element_type=F32
    )
    pooled = 0.25 * (pooled[: boxes * stack] + pooled[boxes * stack :])
    width = edge // 2 + 2
    lanes = old.shape[1]
    lane = lax.broadcasted_iota(jnp.int32, (1, lanes), 1)
    at = (lane // (width * width), lane // width % width, lane % width)
    step = (width * width, width, 1)
    inner = [(a >= 1) & (a <= width - 2) for a in at]
    rest = pooled - 0.5 * sums
    result = jnp.zeros_like(old_v)
    for axis in range(3):
        sides = inner[(axis + 1) % 3] & inner[(axis + 2) % 3]
        for edge_at, shift in ((0, lanes - step[axis]), (width - 1, step[axis])):
            mask = sides & (at[axis] == edge_at)
            fixed = rest - pltpu.roll(old_v, shift, 1)
            result = jnp.where(mask, fixed, result)
    fix[...] = diff * result


def fine_part(pos, owner, low, high, start, others, old, new, mix, coef, spread, ghost, from_y, edge):
    boxes = owner.shape[1]
    count = len(others) + 3
    stack = from_y.shape[0]
    cells = start.shape[1]
    vmem = pl.BlockSpec(memory_space=pltpu.VMEM)
    return pl.pallas_call(
        functools.partial(fine_kernel, count=count, edge=edge),
        in_specs=[vmem] * (count + 9),
        out_specs=[vmem] * (count + 3),
        out_shape=[jax.ShapeDtypeStruct((coef.shape[1], cells), BF16)] * count
        + [
            jax.ShapeDtypeStruct((boxes * stack, old.shape[1]), F32),
            jax.ShapeDtypeStruct(from_y.shape, F32),
            jax.ShapeDtypeStruct((boxes * stack, cells), F32),
        ],
        scratch_shapes=[
            pltpu.VMEM((boxes * stack, cells), F32),
            pltpu.VMEM((2, *low.shape), F32),
        ],
        compiler_params=pltpu.CompilerParams(vmem_limit_bytes=LIMIT),
        name="fine_part",
    )(pos, owner, low, high, start, *others, old, new, mix, coef, spread, ghost, from_y)


def delta_of(field, kept, fix, coef, average, place, half, stack):
    boxes = field.shape[0] // stack
    diffs = jnp.concatenate([column(coef, stack)] * boxes, axis=0)
    stacked = by_box(kept[...], boxes, half).astype(BF16)
    halo = dot(stacked, place[...].astype(BF16))
    means = rows_dot(field[...], average[...].astype(BF16))
    return fix[...] - 0.5 * diffs * diffs * halo + means


def correct_kernel(
    pos, adv, x_first, x_second, near, far, coef, field, kept, fix, average, place, out, block, wide, sems, half
):
    count, stack, nz = adv.shape
    species = block.shape[2]
    width = half + 2
    delta = delta_of(field, kept, fix, coef, average, place, half, stack)
    diff = column(coef, stack)
    even = lax.axis_index("yz") % 2 == 0
    rows = x_first.shape[0]
    near_v, far_v = near[:rows].astype(F32), far[:rows].astype(F32)
    wide[0, :rows] = x_first[...].astype(F32)
    wide[1, : x_second.shape[0]] = x_second[...].astype(F32)
    wide[2, :rows] = jnp.where(even, far_v, near_v)
    wide[3, :rows] = jnp.where(even, near_v, far_v)
    boxes = delta.shape[0] // stack
    starts = [pos[0, i] * width for i in range(boxes)]
    cycle = [tiles_of(stack, nz, start, width) for start in starts]
    inside = [tiles_of(stack, nz, start + 1, half) for start in starts]
    lane = lanes_of(stack)
    copies = []
    for k in range(count):
        x, y = k // width, k % width
        value = adv[k]
        for there, at, n in (
            (x == 0, y, 0),
            (x == width - 1, y, 1),
            (y == 0, x, 2),
            (y == width - 1, x, 3),
        ):
            if there:
                value = value + diff * wide[n, at * species : at * species + stack]
        if x not in (0, width - 1) or y not in (0, width - 1):
            tiles = [value[:, t * 128 : (t + 1) * 128] for t in range(nz // 128)]
            covers = 0 < x < width - 1 and 0 < y < width - 1
            for i in range(boxes):
                mine = delta[i * stack : (i + 1) * stack]
                t = k * width // 128
                part = mine[:, t * 128 : (t + 1) * 128]
                if (k + 1) * width > (t + 1) * 128:
                    after = mine[:, (t + 1) * 128 : (t + 2) * 128]
                    part = jnp.where(lane < (k + 1) * width - (t + 1) * 128, after, part)
                moved = turn(part, starts[i] - k * width)
                for t in range(nz // 128):
                    if covers:
                        tiles[t] = jnp.where(inside[i][t], 0.0, tiles[t])
                    tiles[t] = tiles[t] + jnp.where(cycle[i][t], moved, 0.0)
            value = jnp.concatenate(tiles, axis=1)
        block[x, y] = value[:species]
        if y == width - 1:
            copies.append(pltpu.make_async_copy(block.at[x], out.at[x], sems.at[x]))
            copies[-1].start()
    for copy in copies:
        copy.wait()


def correct(pos, adv, halos, coef, field, kept, fix, table, half):
    _, stack, nz = adv.shape
    width = half + 2
    species = coef.shape[1]
    vmem = pl.BlockSpec(memory_space=pltpu.VMEM)
    return pl.pallas_call(
        functools.partial(correct_kernel, half=half),
        in_specs=[vmem] * 12,
        out_specs=pl.BlockSpec(memory_space=pltpu.HBM),
        out_shape=jax.ShapeDtypeStruct((width, width, species, nz), F32),
        scratch_shapes=[
            pltpu.VMEM((width, width, species, nz), F32),
            pltpu.VMEM((4, halos[0].shape[0] + stack, nz), F32),
            pltpu.SemaphoreType.DMA((width,)),
        ],
        compiler_params=pltpu.CompilerParams(vmem_limit_bytes=LIMIT),
        cost_estimate=pl.CostEstimate(
            flops=20 * adv.size, bytes_accessed=12 * adv.size, transcendentals=0
        ),
        name="coarse_correct",
    )(
        pos,
        adv,
        *halos,
        coef,
        field,
        kept,
        fix,
        jnp.asarray(table["average"]),
        jnp.asarray(table["place"]),
    )


def return_order(count):
    return [0, 2, 3, 1] if count == 4 else list(range(count))


def unpack_kernel(*refs):
    packets, (out, rows) = refs[:-2], refs[-2:]
    species, cells = packets[0].shape
    count = len(packets)
    step = rows.shape[1] // padded(species, 8)
    me = lax.axis_index("yz")
    for k, packet in zip(return_order(count), packets):
        source = origin(me, k, count)
        value = packet[...].astype(F32)
        for q in range(cells // 128):
            rows[q, pl.ds(source, species, stride=step), :] = value[:, q * 128 : (q + 1) * 128]
    for s in range(species):
        pieces = [rows[q, s * step : s * step + count] for q in range(cells // 128)]
        out[s] = jnp.concatenate(pieces, axis=1).astype(BF16)


def unpack(packets):
    species, cells = packets[0].shape
    count = len(packets)
    vmem = pl.BlockSpec(memory_space=pltpu.VMEM)
    rows = padded(species, 8) * padded(count, 8)
    return pl.pallas_call(
        unpack_kernel,
        in_specs=[vmem] * count,
        out_specs=vmem,
        out_shape=jax.ShapeDtypeStruct((species, count, cells), BF16),
        scratch_shapes=[pltpu.VMEM((cells // 128, rows, 128), F32)],
        compiler_params=pltpu.CompilerParams(vmem_limit_bytes=LIMIT),
        name="unpack",
    )(*[packets[k] for k in return_order(count)])


def ring(axis, by):
    count = lax.axis_size(axis)
    return [(i, (i + by) % count) for i in range(count)]


def mutual(axis, by):
    count = lax.axis_size(axis)
    one_way = [(i, (i + by) % count) for i in range(0, count, 2)]
    return one_way + [(j, i) for i, j in one_way]


def partner(me, k, count):
    return me ^ k if count & (count - 1) == 0 else lax.rem(me + k, count)


def origin(me, source, count):
    return me ^ source if count & (count - 1) == 0 else lax.rem(me - source + count, count)


def local(coarse_state, fine_state, diffusion, rate, box_pos, box_owner):
    species, width = coarse_state.shape[:2]
    half = width - 2
    stack = padded(species, 8)
    count = lax.axis_size("yz")
    me = lax.axis_index("yz")
    pos, owner = box_pos[0], box_owner[0]
    table = tables(width, pos.shape[1])
    coef = diffusion[None]
    c = jnp.transpose(coarse_state, (1, 2, 0, 3))

    fine = jnp.transpose(fine_state, (1, 0, 2))
    near, far, own, *others = pack_y(c, fine)
    x_high = pack_x(c, own, c.shape[0] - 1)
    x_low = pack_x(c, x_high, 0)
    halos = [
        lax.ppermute(x_high, "gx", ring("gx", 1)),
        lax.ppermute(x_low, "gx", ring("gx", -1)),
        lax.ppermute(near, "yz", mutual("yz", 1)),
        lax.ppermute(far, "yz", mutual("yz", -1)),
    ]
    if relays(count):
        after = passed = relay(halos[2], x_low, width, *own.shape)
        others = [lax.ppermute(passed, "yz", mutual("yz", -1))]
    else:
        after = x_low
        others = [lax.ppermute(slot, "yz", ring("yz", 2 + k)) for k, slot in enumerate(others)]

    adv, old, new, mix, spread, ghost = coarse_part(
        pos, c, rate, coef, table, stack, after
    )
    from_y, start = y_faces(pos, owner, *halos[2:], own, old, half, stack)
    made = fine_part(
        pos, owner, *halos[:2], start, others, old, new, mix, coef, spread, ghost, from_y, 2 * half
    )
    packets, (fix, kept, field) = made[:count], made[count:]

    def swap(value, k):
        even = count & (count - 1) == 0
        pairs = [(i, i ^ k if even else (i + k) % count) for i in range(count)]
        return lax.ppermute(value, "yz", pairs)

    back = [packets[0]] + [swap(packets[k], k) for k in range(1, count)]
    coarse_next = correct(pos, adv, halos, coef, field, kept, fix, table, half)

    fine_next = jnp.transpose(unpack(back), (1, 0, 2))
    return jnp.transpose(coarse_next, (2, 0, 1, 3)), fine_next


def solution(mesh):
    in_specs = (
        P(None, "gx", "yz", None),
        P(("gx", "yz"), None, None),
        P(),
        P(),
        P("gx", "yz", None),
        P("gx", "yz", None),
    )
    out_specs = (P(None, "gx", "yz", None), P(("gx", "yz"), None, None))
    return jax.shard_map(local, mesh=mesh, in_specs=in_specs, out_specs=out_specs, check_vma=False)
```

```python
import functools

import jax
import jax.numpy as jnp
import numpy as np
from jax import lax
from jax.experimental import pallas as pl
from jax.experimental.pallas import tpu as pltpu
from jax.sharding import PartitionSpec as P

F32 = jnp.float32
BF16 = jnp.bfloat16
LIMIT = 12 * 1024 * 1024
PATCH = 256
ORDER = 20_000_000


def padded(count, unit):
    return -(-count // unit) * unit


@functools.lru_cache(maxsize=None)
def tables(width, boxes):
    half = width - 2
    edge = 2 * half
    cells = width**3
    lanes = padded(cells, PATCH)
    fine = edge**3
    spread = np.zeros((lanes, fine), np.float32)
    average = np.zeros((fine, lanes), np.float32)
    halo = padded(boxes * 4 * half * half, 128)
    place = np.zeros((halo, lanes), np.float32)

    def cell(x, y, z):
        return (x * width + y) * width + z

    for number in range(6):
        axis, high = divmod(number, 2)
        others = [a for a in range(3) if a != axis]
        for r in range(half):
            for q in range(half):
                at = [0, 0, 0]
                at[axis] = width - 1 if high else 0
                at[others[0]] = r + 1
                at[others[1]] = q + 1
                here = cell(*at)
                for i in range(2):
                    for j in range(2):
                        pos = [0, 0, 0]
                        pos[axis] = edge - 1 if high else 0
                        pos[others[0]] = 2 * r + i
                        pos[others[1]] = 2 * q + j
                        spread[here, (pos[0] * edge + pos[1]) * edge + pos[2]] = 1.0
                if number < 4:
                    for box in range(boxes):
                        place[((box * 4 + number) * half + r) * half + q, here] = 1.0
    for x in range(edge):
        for y in range(edge):
            for z in range(edge):
                average[(x * edge + y) * edge + z, cell(x // 2 + 1, y // 2 + 1, z // 2 + 1)] = 0.125
    return dict(spread=spread, average=average, place=place, ghost=place @ spread)


def column(diffusion, stack):
    species = diffusion.shape[1]
    row = lax.broadcasted_iota(jnp.int32, (stack, species), 0)
    lane = lax.broadcasted_iota(jnp.int32, (stack, species), 1)
    return jnp.sum(jnp.where(row == lane, diffusion[...], 0.0), axis=1, keepdims=True)


def split(value):
    high = value.astype(BF16).astype(F32)
    return high, value - high


def parts(value):
    return jnp.concatenate(split(value), axis=0).astype(BF16)


def dot(a, b):
    return jnp.dot(a, b, preferred_element_type=F32)


def rows_dot(value, table):
    rows = value.shape[0]
    both = dot(parts(value), table)
    return both[:rows] + both[rows:]


GROUP = 5


def mixing(rate, scratch, stack, group):
    species = rate.shape[0]
    size = group * stack
    scratch[...] = jnp.zeros_like(scratch)
    high, low = split(rate[...])
    for b in range(group):
        at = b * stack
        for row, lane, part in ((at, at, high), (at, size + at, high), (size + at, at, low)):
            scratch[row : row + species, lane : lane + species] = part
    return scratch[: 2 * size, : 2 * size].astype(BF16)


def react(mix, fields):
    size = fields.shape[0]
    both = dot(mix, parts(fields))
    return both[:size] + both[size:]


def react_all(mix, fields):
    stack, depth = fields[0].shape
    made = [[] for _ in fields]

    def product(blocks):
        size = len(blocks[0])
        blank = [jnp.zeros_like(blocks[0][0])] * (GROUP - size)
        columns = [jnp.concatenate(block + blank, axis=0) for block in blocks]
        out = react(mix, jnp.concatenate(columns, axis=1))
        lanes = out.shape[1] // len(blocks)
        return [
            [out[b * stack : (b + 1) * stack, n * lanes : (n + 1) * lanes] for b in range(size)]
            for n in range(len(blocks))
        ]

    for lane in range(0, depth, 256):
        if lane + 256 <= depth:
            for at in range(0, len(fields), GROUP):
                block = [f[:, lane : lane + 256] for f in fields[at : at + GROUP]]
                for b, value in enumerate(product([block])[0]):
                    made[at + b].append(value)
        else:
            half = -(-len(fields) // 2)
            blocks = [[f[:, lane:] for f in part] for part in (fields[:half], fields[half:])]
            blocks[1] += [jnp.zeros_like(blocks[0][0])] * (half - len(blocks[1]))
            for n, values in enumerate(product(blocks)):
                for b, value in enumerate(values):
                    if n * half + b < len(fields):
                        made[n * half + b].append(value)
    return [jnp.concatenate(value, axis=1) for value in made]


def lanes_of(stack, lanes=128):
    return lax.broadcasted_iota(jnp.int32, (stack, lanes), 1)


def tiles_of(stack, depth, start, width):
    lane = lanes_of(stack)
    masks = []
    for t in range(depth // 128):
        along = lane + (t * 128 - start)
        masks.append((along >= 0) & (along < width))
    return masks


def fold(value, masks):
    out = value[:, :128]
    for t in range(1, len(masks)):
        out = jnp.where(masks[t], value[:, t * 128 : (t + 1) * 128], out)
    return out


def turn(value, by):
    return pltpu.roll(value, by & 127, 1)


def neighbour(me, count, even_up):
    step = jnp.where((me % 2 == 0) == even_up, 1, count - 1)
    return lax.rem(me + step, count)


def layer_rows(width, species, groups=0):
    return padded((width + groups) * species, 16)


def blocks_of(width, species, nz, pieces, slot=0):
    across = nz // 128
    numbers = range(slot * pieces, (slot + 1) * pieces)
    return [((width + n // across) * species, n % across * 128) for n in numbers]


def pack_layer(columns, tmp, species):
    for r, value in enumerate(columns):
        tmp[r * species : (r + 1) * species] = value
    below = len(columns) * species
    tmp[below:] = jnp.zeros((tmp.shape[0] - below, tmp.shape[1]), F32)


def pack_y_kernel(c, fine, near, far, own, *refs):
    others, (layer, tmp, held, rows, sems, fine_sem) = refs[:-6], refs[-6:]
    nx, ny, species, nz = c.shape
    count = fine.shape[1]
    stack = padded(species, 8)
    me = lax.axis_index("yz")
    slots = pltpu.make_async_copy(fine, held, fine_sem)
    slots.start()
    copies = []
    for n, y in enumerate((jnp.where(me % 2 == 0, ny - 1, 0), jnp.where(me % 2 == 0, 0, ny - 1))):
        copies.append(pltpu.make_async_copy(c.at[:, y], layer.at[n], sems.at[n]))
        copies[-1].start()
    slots.wait()
    step = rows.shape[1] // stack
    pieces = rows.shape[0]
    for s in range(species):
        value = held[s].astype(F32)
        for q in range(pieces):
            rows[q, s * step : s * step + count] = value[:, q * 128 : (q + 1) * 128]

    def slot(at):
        return [rows[q, pl.ds(at, species, stride=step), :] for q in range(pieces)]

    own[...] = jnp.concatenate(slot(me), axis=1).astype(BF16)
    for k, out in enumerate(others):
        out[...] = jnp.concatenate(slot(lax.rem(me + 2 + k, count)), axis=1).astype(BF16)
    for n, out in enumerate((far, near)):
        n = 1 - n
        copies[n].wait()
        pack_layer([layer[n, r] for r in range(nx)], tmp, species)
        sent = [slot(neighbour(me, count, n == 0))]
        if n == 0 and relays(count):
            sent.append(slot(lax.rem(me + 2, count)))
        for m, value in enumerate(sent):
            for (row, lane), piece in zip(blocks_of(nx, species, nz, pieces, m), value):
                tmp[row : row + species, lane : lane + 128] = piece
        out[...] = tmp[: out.shape[0]].astype(BF16)


def pack_y(c, fine):
    nx, ny, species, nz = c.shape
    count, cells = fine.shape[1:]
    stack = padded(species, 8)
    vmem = pl.BlockSpec(memory_space=pltpu.VMEM)
    far_rows = layer_rows(nx, species, -(-cells // nz))
    rows = layer_rows(nx, species, -(-2 * cells // nz)) if relays(count) else far_rows
    outs = [jax.ShapeDtypeStruct((n, nz), BF16) for n in (rows, far_rows)]
    direct = 0 if relays(count) else max(count - 3, 0)
    outs += [jax.ShapeDtypeStruct((species, cells), BF16)] * (1 + direct)
    return pl.pallas_call(
        pack_y_kernel,
        in_specs=[pl.BlockSpec(memory_space=pltpu.HBM)] * 2,
        out_specs=[vmem] * len(outs),
        out_shape=outs,
        scratch_shapes=[
            pltpu.VMEM((2, nx, species, nz), F32),
            pltpu.VMEM((rows, nz), F32),
            pltpu.VMEM(fine.shape, BF16),
            pltpu.VMEM((cells // 128, stack * padded(count, 8), 128), F32),
            pltpu.SemaphoreType.DMA((2,)),
            pltpu.SemaphoreType.DMA,
        ],
        compiler_params=pltpu.CompilerParams(vmem_limit_bytes=LIMIT),
        name="pack_y",
    )(
        pltpu.with_memory_space_constraint(c, pltpu.HBM),
        pltpu.with_memory_space_constraint(fine, pltpu.HBM),
    )


def relays(count):
    return count == 4


def relay_kernel(near, after, out, wide, width):
    species, cells = out.shape
    wide[...] = near[...].astype(F32)
    places = blocks_of(width, species, near.shape[1], cells // 128, 1)
    pieces = [wide[row : row + species, lane : lane + 128] for row, lane in places]
    out[...] = jnp.concatenate(pieces, axis=1).astype(BF16)


def relay(near, after, width, species, cells):
    vmem = pl.BlockSpec(memory_space=pltpu.VMEM)
    return pl.pallas_call(
        functools.partial(relay_kernel, width=width),
        in_specs=[vmem, pl.BlockSpec(memory_space=pl.ANY)],
        out_specs=vmem,
        out_shape=jax.ShapeDtypeStruct((species, cells), BF16),
        scratch_shapes=[pltpu.VMEM(near.shape, F32)],
        compiler_params=pltpu.CompilerParams(vmem_limit_bytes=LIMIT),
        name="relay",
    )(near, after)


def pack_x_kernel(c, after, out, tmp, x):
    nx, ny, species, _ = c.shape
    pack_layer([c[x, r] for r in range(ny)], tmp, species)
    out[...] = tmp[...].astype(BF16)


def pack_x(c, after, x):
    nx, ny, species, nz = c.shape
    vmem = pl.BlockSpec(memory_space=pltpu.VMEM)
    shape = (layer_rows(ny, species), nz)
    return pl.pallas_call(
        functools.partial(pack_x_kernel, x=x),
        in_specs=[vmem, pl.BlockSpec(memory_space=pl.ANY)],
        out_specs=vmem,
        out_shape=jax.ShapeDtypeStruct(shape, BF16),
        scratch_shapes=[pltpu.VMEM(shape, F32)],
        compiler_params=pltpu.CompilerParams(vmem_limit_bytes=LIMIT),
        name="pack_x",
    )(c, after)


def coarse_kernel(
    pos, c, rate, coef, spread, ghost, after, adv, old, new, mix, spread16, ghost16, columns, scratch
):
    count, stack, nz = adv.shape
    boxes = pos.shape[1]
    width = c.shape[0]
    mix[...] = mixing(rate, scratch, stack, 2)
    mixed = mixing(rate, scratch, stack, GROUP)
    spread16[...] = spread[...].astype(BF16)
    ghost16[...] = ghost[...].astype(BF16)
    for k in range(count):
        columns[k, c.shape[2] :] = jnp.zeros((stack - c.shape[2], nz), F32)
        columns[k, : c.shape[2]] = c[k // width, k % width]
    diff = column(coef, stack)
    for first in range(0, count, 2 * GROUP):
        some = range(first, min(first + 2 * GROUP, count))
        made = react_all(mixed, [columns[k] for k in some])
        for k in some:
            x, y = k // width, k % width
            mine = columns[k]
            lap = pltpu.roll(mine, 1, 1) + pltpu.roll(mine, nz - 1, 1) - 6.0 * mine
            if x > 0:
                lap = lap + columns[k - width]
            if x < width - 1:
                lap = lap + columns[k + width]
            if y > 0:
                lap = lap + columns[k - 1]
            if y < width - 1:
                lap = lap + columns[k + 1]
            value = mine + diff * lap + made[k - first]
            adv[k] = value
    lanes = old.shape[1]
    cell = lanes_of(stack, lanes) // width
    for i in range(boxes):
        lane = pos[0, i] * width
        start = pl.multiple_of(jnp.minimum(lane // 128, nz // 128 - 2) * 128, 128)
        offset = lane - start
        for source, out in ((columns, old), (adv, new)):
            total = jnp.zeros((stack, lanes), F32)
            for k in range(count):
                if k // width in (0, width - 1) and k % width in (0, width - 1):
                    continue
                part = source[k, :, pl.ds(start, PATCH)]
                moved = pltpu.roll(part, (k * width - offset) & (PATCH - 1), 1)
                total = jnp.where(cell == k, moved, total)
            out[i * stack : (i + 1) * stack] = total


def coarse_part(pos, c, rate, coef, table, stack, after):
    nx, ny, species, nz = c.shape
    boxes = pos.shape[1]
    lanes = padded(nx**3, PATCH)
    vmem = pl.BlockSpec(memory_space=pltpu.VMEM)
    small = jax.ShapeDtypeStruct((boxes * stack, lanes), F32)
    size = padded(2 * GROUP * stack, 128)
    return pl.pallas_call(
        coarse_kernel,
        in_specs=[vmem] * 6 + [pl.BlockSpec(memory_space=pl.ANY)],
        out_specs=[vmem] * 6,
        out_shape=[
            jax.ShapeDtypeStruct((nx * ny, stack, nz), F32),
            small,
            small,
            jax.ShapeDtypeStruct((4 * stack, 4 * stack), BF16),
            jax.ShapeDtypeStruct(table["spread"].shape, BF16),
            jax.ShapeDtypeStruct(table["ghost"].shape, BF16),
        ],
        scratch_shapes=[
            pltpu.VMEM((nx * ny, stack, nz), F32),
            pltpu.VMEM((size, size), F32),
        ],
        compiler_params=pltpu.CompilerParams(vmem_limit_bytes=LIMIT),
        cost_estimate=pl.CostEstimate(
            flops=800 * c.size, bytes_accessed=12 * c.size, transcendentals=0
        ),
        name="coarse_part",
    )(pos, c, rate, coef, jnp.asarray(table["spread"]), jnp.asarray(table["ghost"]), after)


def by_box(total, boxes, half):
    each = 4 * half * half
    lane = lax.broadcasted_iota(jnp.int32, total.shape, 1)
    rows = [
        jnp.where((lane >= i * each) & (lane < (i + 1) * each), total, 0.0) for i in range(boxes)
    ]
    return jnp.concatenate(rows, axis=0)


def gather_faces(pos, layers, faces, half, stack, species, nz, total):
    lane = lanes_of(stack)
    for ref, face in zip(layers, faces):
        for i in range(pos.shape[1]):
            start = pos[0, i] * (half + 2) + 1
            masks = tiles_of(stack, nz, start, half)
            for r in range(half):
                base = ((i * 4 + face) * half + r) * half
                at = (r + 1) * species
                moved = turn(fold(ref[at : at + stack], masks), base - start)
                tiles = []
                for t in range(total.shape[1] // 128):
                    along = lane + (t * 128 - base)
                    here = (along >= 0) & (along < half)
                    tiles.append(jnp.where(here, moved, total[:, t * 128 : (t + 1) * 128]))
                total = tiles[0] if len(tiles) == 1 else jnp.concatenate(tiles, axis=1)
    return total


def y_faces_kernel(pos, owner, near, far, own, after, from_y, start, wide):
    stack = from_y.shape[0]
    species, cells = own.shape
    nz = near.shape[1]
    boxes = pos.shape[1]
    width = far.shape[0] // species - -(-cells // nz)
    half = width - 2
    wide[0] = near[...].astype(F32)
    wide[1, : far.shape[0]] = far[...].astype(F32)
    me, count = lax.axis_index("yz"), lax.axis_size("yz")
    odd = me % 2
    zero = jnp.zeros(from_y.shape, F32)
    layers = (wide.at[0], wide.at[1])
    from_y[...] = gather_faces(pos, layers, (3 - odd, 2 + odd), half, stack, species, nz, zero)
    direct = own[...].astype(F32)
    places = blocks_of(width, species, nz, cells // 128)
    edge = species // 8 * 8
    for i in range(boxes):
        by_near = owner[0, i] == neighbour(me, count, True)
        by_far = owner[0, i] == neighbour(me, count, False)
        at = i * stack
        start[at + edge : at + stack] = jnp.zeros((stack - edge, cells), F32)
        for q, (row, lane) in enumerate(places):
            part = direct[:, q * 128 : (q + 1) * 128]
            sent = [wide[n, row : row + species, lane : lane + 128] for n in range(2)]
            part = jnp.where(by_far, sent[1], jnp.where(by_near, sent[0], part))
            start[at : at + species, q * 128 : (q + 1) * 128] = part


def y_faces(pos, owner, near, far, own, after, half, stack):
    vmem = pl.BlockSpec(memory_space=pltpu.VMEM)
    boxes = pos.shape[1]
    lanes = padded(boxes * 4 * half * half, 128)
    return pl.pallas_call(
        y_faces_kernel,
        in_specs=[vmem] * 5 + [pl.BlockSpec(memory_space=pl.ANY)],
        out_specs=[vmem] * 2,
        out_shape=[
            jax.ShapeDtypeStruct((stack, lanes), F32),
            jax.ShapeDtypeStruct((boxes * stack, own.shape[1]), F32),
        ],
        scratch_shapes=[pltpu.VMEM((2, *near.shape), F32)],
        compiler_params=pltpu.CompilerParams(vmem_limit_bytes=LIMIT),
        cost_estimate=pl.CostEstimate(flops=10**9, bytes_accessed=ORDER, transcendentals=0),
        name="y_faces",
    )(pos, owner, near, far, own, after)


def fine_base_kernel(pos, owner, x_low, start, *refs, count, edge):
    others, refs = refs[: count - 3], refs[count - 3 :]
    old, new, mix, coef, spread, from_y, base, fix, gathered, field, wide = refs
    species = coef.shape[1]
    stack = from_y.shape[0]
    boxes, cells = base.shape[0] // stack, base.shape[1]
    me = lax.axis_index("yz")
    mixed = mix[...]

    def reaction(value):
        pairs = [value[at : at + 2 * stack] for at in range(0, boxes * stack, 2 * stack)]
        return jnp.concatenate([react(mixed, pair) for pair in pairs], axis=0)

    nz = x_low.shape[1]
    half = edge // 2
    wide[...] = x_low[...].astype(F32)
    gathered[...] = gather_faces(pos, [wide], [0], half, stack, species, nz, from_y[...])
    sent = [ref[...].astype(F32) for ref in others]
    for i in range(boxes):
        at = i * stack
        field[at : at + stack] = start[at : at + stack]
        back = lax.rem(me - owner[0, i] + count, count)
        value = start[at : at + species]
        for k in range(len(sent)):
            value = jnp.where(back == k + 2, sent[k], value)
        field[at : at + species] = value
    diff = jnp.concatenate([column(coef, stack)] * boxes, axis=0)
    old_v, new_v = old[...], new[...]
    sums = old_v + new_v
    spread_v = spread[...]
    both = rows_dot(jnp.concatenate([old_v, sums], axis=0), spread_v)
    ghost0, ghost1 = both[: boxes * stack], both[boxes * stack :]
    index = lax.broadcasted_iota(jnp.int32, (1, cells), 1)
    at = (index // (edge * edge), index // edge % edge, index % edge)
    step = (edge * edge, edge, 1)

    def inside(value):
        lap = -6.0 * value
        for axis in range(3):
            before = pltpu.roll(value, step[axis], 1)
            after = pltpu.roll(value, cells - step[axis], 1)
            lap = lap + jnp.where(at[axis] == 0, 0.0, before)
            lap = lap + jnp.where(at[axis] == edge - 1, 0.0, after)
        return lap

    first = field[...]
    second = first + 2.0 * diff * (inside(first) + ghost0) + 0.5 * reaction(first)
    base[...] = second + diff * (2.0 * inside(second) + ghost1) + 0.5 * reaction(second)
    pooled = lax.dot_general(
        parts(first + second), spread_v, (((1,), (1,)), ((), ())), preferred_element_type=F32
    )
    pooled = 0.25 * (pooled[: boxes * stack] + pooled[boxes * stack :])
    width = edge // 2 + 2
    lanes = old.shape[1]
    lane = lax.broadcasted_iota(jnp.int32, (1, lanes), 1)
    at = (lane // (width * width), lane // width % width, lane % width)
    step = (width * width, width, 1)
    inner = [(a >= 1) & (a <= width - 2) for a in at]
    rest = pooled - 0.5 * sums
    result = jnp.zeros_like(old_v)
    for axis in range(3):
        sides = inner[(axis + 1) % 3] & inner[(axis + 2) % 3]
        for edge_at, shift in ((0, lanes - step[axis]), (width - 1, step[axis])):
            mask = sides & (at[axis] == edge_at)
            fixed = rest - pltpu.roll(old_v, shift, 1)
            result = jnp.where(mask, fixed, result)
    fix[...] = diff * result


def fine_base(pos, owner, low, start, others, old, new, mix, coef, spread, from_y, edge):
    count = len(others) + 3
    vmem = pl.BlockSpec(memory_space=pltpu.VMEM)
    return pl.pallas_call(
        functools.partial(fine_base_kernel, count=count, edge=edge),
        in_specs=[vmem] * (count + 7),
        out_specs=[vmem] * 3,
        out_shape=[jax.ShapeDtypeStruct(a.shape, F32) for a in (start, old, from_y)],
        scratch_shapes=[pltpu.VMEM(start.shape, F32), pltpu.VMEM(low.shape, F32)],
        compiler_params=pltpu.CompilerParams(vmem_limit_bytes=LIMIT),
        name="fine_base",
    )(pos, owner, low, start, *others, old, new, mix, coef, spread, from_y)


def fine_finish_kernel(pos, owner, x_high, base, coef, ghost, gathered, *refs, half):
    packets, (kept, final, wide) = refs[:-3], refs[-3:]
    species, cells = packets[0].shape
    count = len(packets)
    stack = kept.shape[0]
    boxes = base.shape[0] // stack
    me = lax.axis_index("yz")
    wide[...] = x_high[...].astype(F32)
    total = gathered[...]
    total = gather_faces(pos, [wide], [1], half, stack, species, wide.shape[1], total)
    kept[...] = total
    diff = jnp.concatenate([column(coef, stack)] * boxes, axis=0)
    stacked = by_box(total, boxes, half).astype(BF16)
    value = base[...] + diff * diff * dot(stacked, ghost[...])
    final[...] = value
    for k, out in enumerate(packets):
        dest = partner(me, k, count)
        packet = jnp.zeros((species, cells), F32)
        for i in range(boxes):
            packet = jnp.where(owner[0, i] == dest, value[i * stack : i * stack + species], packet)
        out[...] = packet.astype(BF16)


def fine_finish(pos, owner, high, base, coef, ghost, gathered, count, half):
    vmem = pl.BlockSpec(memory_space=pltpu.VMEM)
    packet = jax.ShapeDtypeStruct((coef.shape[1], base.shape[1]), BF16)
    return pl.pallas_call(
        functools.partial(fine_finish_kernel, half=half),
        in_specs=[vmem] * 7,
        out_specs=[vmem] * (count + 2),
        out_shape=[packet] * count
        + [jax.ShapeDtypeStruct(a.shape, F32) for a in (gathered, base)],
        scratch_shapes=[pltpu.VMEM(high.shape, F32)],
        compiler_params=pltpu.CompilerParams(vmem_limit_bytes=LIMIT),
        name="fine_finish",
    )(pos, owner, high, base, coef, ghost, gathered)


def delta_of(field, kept, fix, coef, average, place, half, stack):
    boxes = field.shape[0] // stack
    diffs = jnp.concatenate([column(coef, stack)] * boxes, axis=0)
    stacked = by_box(kept[...], boxes, half).astype(BF16)
    halo = dot(stacked, place[...].astype(BF16))
    means = rows_dot(field[...], average[...].astype(BF16))
    return fix[...] - 0.5 * diffs * diffs * halo + means


def correct_kernel(
    pos, adv, x_first, x_second, near, far, coef, field, kept, fix, average, place, out, block, wide, sems, half
):
    count, stack, nz = adv.shape
    species = block.shape[2]
    width = half + 2
    delta = delta_of(field, kept, fix, coef, average, place, half, stack)
    diff = column(coef, stack)
    even = lax.axis_index("yz") % 2 == 0
    rows = x_first.shape[0]
    near_v, far_v = near[:rows].astype(F32), far[:rows].astype(F32)
    wide[0, :rows] = x_first[...].astype(F32)
    wide[1, : x_second.shape[0]] = x_second[...].astype(F32)
    wide[2, :rows] = jnp.where(even, far_v, near_v)
    wide[3, :rows] = jnp.where(even, near_v, far_v)
    boxes = delta.shape[0] // stack
    starts = [pos[0, i] * width for i in range(boxes)]
    cycle = [tiles_of(stack, nz, start, width) for start in starts]
    inside = [tiles_of(stack, nz, start + 1, half) for start in starts]
    lane = lanes_of(stack)
    copies = []
    for k in range(count):
        x, y = k // width, k % width
        value = adv[k]
        for there, at, n in (
            (x == 0, y, 0),
            (x == width - 1, y, 1),
            (y == 0, x, 2),
            (y == width - 1, x, 3),
        ):
            if there:
                value = value + diff * wide[n, at * species : at * species + stack]
        if x not in (0, width - 1) or y not in (0, width - 1):
            tiles = [value[:, t * 128 : (t + 1) * 128] for t in range(nz // 128)]
            covers = 0 < x < width - 1 and 0 < y < width - 1
            for i in range(boxes):
                mine = delta[i * stack : (i + 1) * stack]
                t = k * width // 128
                part = mine[:, t * 128 : (t + 1) * 128]
                if (k + 1) * width > (t + 1) * 128:
                    after = mine[:, (t + 1) * 128 : (t + 2) * 128]
                    part = jnp.where(lane < (k + 1) * width - (t + 1) * 128, after, part)
                moved = turn(part, starts[i] - k * width)
                for t in range(nz // 128):
                    if covers:
                        tiles[t] = jnp.where(inside[i][t], 0.0, tiles[t])
                    tiles[t] = tiles[t] + jnp.where(cycle[i][t], moved, 0.0)
            value = jnp.concatenate(tiles, axis=1)
        block[x, y] = value[:species]
        if y == width - 1:
            copies.append(pltpu.make_async_copy(block.at[x], out.at[x], sems.at[x]))
            copies[-1].start()
    for copy in copies:
        copy.wait()


def correct(pos, adv, halos, coef, field, kept, fix, table, half):
    _, stack, nz = adv.shape
    width = half + 2
    species = coef.shape[1]
    vmem = pl.BlockSpec(memory_space=pltpu.VMEM)
    return pl.pallas_call(
        functools.partial(correct_kernel, half=half),
        in_specs=[vmem] * 12,
        out_specs=pl.BlockSpec(memory_space=pltpu.HBM),
        out_shape=jax.ShapeDtypeStruct((width, width, species, nz), F32),
        scratch_shapes=[
            pltpu.VMEM((width, width, species, nz), F32),
            pltpu.VMEM((4, halos[0].shape[0] + stack, nz), F32),
            pltpu.SemaphoreType.DMA((width,)),
        ],
        compiler_params=pltpu.CompilerParams(vmem_limit_bytes=LIMIT),
        cost_estimate=pl.CostEstimate(
            flops=20 * adv.size, bytes_accessed=12 * adv.size, transcendentals=0
        ),
        name="coarse_correct",
    )(
        pos,
        adv,
        *halos,
        coef,
        field,
        kept,
        fix,
        jnp.asarray(table["average"]),
        jnp.asarray(table["place"]),
    )


def return_order(count):
    return [0, 2, 3, 1] if count == 4 else list(range(count))


def unpack_kernel(*refs):
    packets, (out, rows) = refs[:-2], refs[-2:]
    species, cells = packets[0].shape
    count = len(packets)
    step = rows.shape[1] // padded(species, 8)
    me = lax.axis_index("yz")
    for k, packet in zip(return_order(count), packets):
        source = origin(me, k, count)
        value = packet[...].astype(F32)
        for q in range(cells // 128):
            rows[q, pl.ds(source, species, stride=step), :] = value[:, q * 128 : (q + 1) * 128]
    for s in range(species):
        pieces = [rows[q, s * step : s * step + count] for q in range(cells // 128)]
        out[s] = jnp.concatenate(pieces, axis=1).astype(BF16)


def unpack(packets):
    species, cells = packets[0].shape
    count = len(packets)
    vmem = pl.BlockSpec(memory_space=pltpu.VMEM)
    rows = padded(species, 8) * padded(count, 8)
    return pl.pallas_call(
        unpack_kernel,
        in_specs=[vmem] * count,
        out_specs=vmem,
        out_shape=jax.ShapeDtypeStruct((species, count, cells), BF16),
        scratch_shapes=[pltpu.VMEM((cells // 128, rows, 128), F32)],
        compiler_params=pltpu.CompilerParams(vmem_limit_bytes=LIMIT),
        name="unpack",
    )(*[packets[k] for k in return_order(count)])


def ring(axis, by):
    count = lax.axis_size(axis)
    return [(i, (i + by) % count) for i in range(count)]


def mutual(axis, by):
    count = lax.axis_size(axis)
    one_way = [(i, (i + by) % count) for i in range(0, count, 2)]
    return one_way + [(j, i) for i, j in one_way]


def partner(me, k, count):
    return me ^ k if count & (count - 1) == 0 else lax.rem(me + k, count)


def origin(me, source, count):
    return me ^ source if count & (count - 1) == 0 else lax.rem(me - source + count, count)


def local(coarse_state, fine_state, diffusion, rate, box_pos, box_owner):
    species, width = coarse_state.shape[:2]
    half = width - 2
    stack = padded(species, 8)
    count = lax.axis_size("yz")
    me = lax.axis_index("yz")
    pos, owner = box_pos[0], box_owner[0]
    table = tables(width, pos.shape[1])
    coef = diffusion[None]
    c = jnp.transpose(coarse_state, (1, 2, 0, 3))

    fine = jnp.transpose(fine_state, (1, 0, 2))
    near, far, own, *others = pack_y(c, fine)
    x_high = pack_x(c, own, c.shape[0] - 1)
    x_low = pack_x(c, x_high, 0)
    halos = [
        lax.ppermute(x_high, "gx", ring("gx", 1)),
        lax.ppermute(x_low, "gx", ring("gx", -1)),
        lax.ppermute(near, "yz", mutual("yz", 1)),
        lax.ppermute(far, "yz", mutual("yz", -1)),
    ]
    if relays(count):
        after = passed = relay(halos[2], x_low, width, *own.shape)
        others = [lax.ppermute(passed, "yz", mutual("yz", -1))]
    else:
        after = x_low
        others = [lax.ppermute(slot, "yz", ring("yz", 2 + k)) for k, slot in enumerate(others)]

    adv, old, new, mix, spread, ghost = coarse_part(
        pos, c, rate, coef, table, stack, after
    )
    from_y, start = y_faces(pos, owner, *halos[2:], own, old, half, stack)
    base, fix, gathered = fine_base(
        pos, owner, halos[0], start, others, old, new, mix, coef, spread, from_y, 2 * half
    )
    made = fine_finish(pos, owner, halos[1], base, coef, ghost, gathered, count, half)
    packets, (kept, field) = made[:count], made[count:]

    def swap(value, k):
        even = count & (count - 1) == 0
        pairs = [(i, i ^ k if even else (i + k) % count) for i in range(count)]
        return lax.ppermute(value, "yz", pairs)

    back = [packets[0]] + [swap(packets[k], k) for k in range(1, count)]
    coarse_next = correct(pos, adv, halos, coef, field, kept, fix, table, half)

    fine_next = jnp.transpose(unpack(back), (1, 0, 2))
    return jnp.transpose(coarse_next, (2, 0, 1, 3)), fine_next


def solution(mesh):
    in_specs = (
        P(None, "gx", "yz", None),
        P(("gx", "yz"), None, None),
        P(),
        P(),
        P("gx", "yz", None),
        P("gx", "yz", None),
    )
    out_specs = (P(None, "gx", "yz", None), P(("gx", "yz"), None, None))
    return jax.shard_map(local, mesh=mesh, in_specs=in_specs, out_specs=out_specs, check_vma=False)
```

```python
import functools

import jax
import jax.numpy as jnp
import numpy as np
from jax import lax
from jax.experimental import pallas as pl
from jax.experimental.pallas import tpu as pltpu
from jax.sharding import PartitionSpec as P

F32 = jnp.float32
BF16 = jnp.bfloat16
LIMIT = 12 * 1024 * 1024
PATCH = 256
ORDER = 20_000_000


def padded(count, unit):
    return -(-count // unit) * unit


@functools.lru_cache(maxsize=None)
def tables(width, boxes):
    half = width - 2
    edge = 2 * half
    cells = width**3
    lanes = padded(cells, PATCH)
    fine = edge**3
    spread = np.zeros((lanes, fine), np.float32)
    average = np.zeros((fine, lanes), np.float32)
    halo = padded(boxes * 4 * half * half, 128)
    place = np.zeros((halo, lanes), np.float32)

    def cell(x, y, z):
        return (x * width + y) * width + z

    for number in range(6):
        axis, high = divmod(number, 2)
        others = [a for a in range(3) if a != axis]
        for r in range(half):
            for q in range(half):
                at = [0, 0, 0]
                at[axis] = width - 1 if high else 0
                at[others[0]] = r + 1
                at[others[1]] = q + 1
                here = cell(*at)
                for i in range(2):
                    for j in range(2):
                        pos = [0, 0, 0]
                        pos[axis] = edge - 1 if high else 0
                        pos[others[0]] = 2 * r + i
                        pos[others[1]] = 2 * q + j
                        spread[here, (pos[0] * edge + pos[1]) * edge + pos[2]] = 1.0
                if number < 4:
                    for box in range(boxes):
                        place[((box * 4 + number) * half + r) * half + q, here] = 1.0
    for x in range(edge):
        for y in range(edge):
            for z in range(edge):
                average[(x * edge + y) * edge + z, cell(x // 2 + 1, y // 2 + 1, z // 2 + 1)] = 0.125
    return dict(spread=spread, average=average, place=place, ghost=place @ spread)


def column(diffusion, stack):
    species = diffusion.shape[1]
    row = lax.broadcasted_iota(jnp.int32, (stack, species), 0)
    lane = lax.broadcasted_iota(jnp.int32, (stack, species), 1)
    return jnp.sum(jnp.where(row == lane, diffusion[...], 0.0), axis=1, keepdims=True)


def split(value):
    high = value.astype(BF16).astype(F32)
    return high, value - high


def parts(value):
    return jnp.concatenate(split(value), axis=0).astype(BF16)


def dot(a, b):
    return jnp.dot(a, b, preferred_element_type=F32)


def rows_dot(value, table):
    rows = value.shape[0]
    both = dot(parts(value), table)
    return both[:rows] + both[rows:]


GROUP = 5


def mixing(rate, scratch, stack, group):
    species = rate.shape[0]
    size = group * stack
    scratch[...] = jnp.zeros_like(scratch)
    high, low = split(rate[...])
    for b in range(group):
        at = b * stack
        for row, lane, part in ((at, at, high), (at, size + at, high), (size + at, at, low)):
            scratch[row : row + species, lane : lane + species] = part
    return scratch[: 2 * size, : 2 * size].astype(BF16)


def react(mix, fields):
    size = fields.shape[0]
    both = dot(mix, parts(fields))
    return both[:size] + both[size:]


def react_all(mix, fields):
    stack, depth = fields[0].shape
    made = [[] for _ in fields]

    def product(blocks):
        size = len(blocks[0])
        blank = [jnp.zeros_like(blocks[0][0])] * (GROUP - size)
        columns = [jnp.concatenate(block + blank, axis=0) for block in blocks]
        out = react(mix, jnp.concatenate(columns, axis=1))
        lanes = out.shape[1] // len(blocks)
        return [
            [out[b * stack : (b + 1) * stack, n * lanes : (n + 1) * lanes] for b in range(size)]
            for n in range(len(blocks))
        ]

    for lane in range(0, depth, 256):
        if lane + 256 <= depth:
            for at in range(0, len(fields), GROUP):
                block = [f[:, lane : lane + 256] for f in fields[at : at + GROUP]]
                for b, value in enumerate(product([block])[0]):
                    made[at + b].append(value)
        else:
            half = -(-len(fields) // 2)
            blocks = [[f[:, lane:] for f in part] for part in (fields[:half], fields[half:])]
            blocks[1] += [jnp.zeros_like(blocks[0][0])] * (half - len(blocks[1]))
            for n, values in enumerate(product(blocks)):
                for b, value in enumerate(values):
                    if n * half + b < len(fields):
                        made[n * half + b].append(value)
    return [jnp.concatenate(value, axis=1) for value in made]


def lanes_of(stack, lanes=128):
    return lax.broadcasted_iota(jnp.int32, (stack, lanes), 1)


def tiles_of(stack, depth, start, width):
    lane = lanes_of(stack)
    masks = []
    for t in range(depth // 128):
        along = lane + (t * 128 - start)
        masks.append((along >= 0) & (along < width))
    return masks


def fold(value, masks):
    out = value[:, :128]
    for t in range(1, len(masks)):
        out = jnp.where(masks[t], value[:, t * 128 : (t + 1) * 128], out)
    return out


def turn(value, by):
    return pltpu.roll(value, by & 127, 1)


def neighbour(me, count, even_up):
    step = jnp.where((me % 2 == 0) == even_up, 1, count - 1)
    return lax.rem(me + step, count)


def layer_rows(width, species, groups=0):
    return padded((width + groups) * species, 16)


def blocks_of(width, species, nz, pieces, slot=0):
    across = nz // 128
    numbers = range(slot * pieces, (slot + 1) * pieces)
    return [((width + n // across) * species, n % across * 128) for n in numbers]


def pack_layer(columns, tmp, species):
    for r, value in enumerate(columns):
        tmp[r * species : (r + 1) * species] = value
    below = len(columns) * species
    tmp[below:] = jnp.zeros((tmp.shape[0] - below, tmp.shape[1]), F32)


def pack_y_kernel(c, fine, near, far, own, *refs):
    others, (layer, tmp, held, rows, sems, fine_sem) = refs[:-6], refs[-6:]
    nx, ny, species, nz = c.shape
    count = fine.shape[1]
    stack = padded(species, 8)
    me = lax.axis_index("yz")
    slots = pltpu.make_async_copy(fine, held, fine_sem)
    slots.start()
    ends = (jnp.where(me % 2 == 0, ny - 1, 0), jnp.where(me % 2 == 0, 0, ny - 1))
    copies = {}
    for n in (1, 0):
        for r in range(nx):
            copies[n, r] = pltpu.make_async_copy(c.at[r, ends[n]], layer.at[n, r], sems.at[n, r])
            copies[n, r].start()
    slots.wait()
    step = rows.shape[1] // stack
    pieces = rows.shape[0]
    for s in range(species):
        value = held[s].astype(F32)
        for q in range(pieces):
            rows[q, s * step : s * step + count] = value[:, q * 128 : (q + 1) * 128]

    def slot(at):
        return [rows[q, pl.ds(at, species, stride=step), :] for q in range(pieces)]

    own[...] = jnp.concatenate(slot(me), axis=1).astype(BF16)
    for k, out in enumerate(others):
        out[...] = jnp.concatenate(slot(lax.rem(me + 2 + k, count)), axis=1).astype(BF16)
    for n, out in enumerate((far, near)):
        n = 1 - n
        for r in range(nx):
            copies[n, r].wait()
        pack_layer([layer[n, r] for r in range(nx)], tmp, species)
        sent = [slot(neighbour(me, count, n == 0))]
        if n == 0 and relays(count):
            sent.append(slot(lax.rem(me + 2, count)))
        for m, value in enumerate(sent):
            for (row, lane), piece in zip(blocks_of(nx, species, nz, pieces, m), value):
                tmp[row : row + species, lane : lane + 128] = piece
        out[...] = tmp[: out.shape[0]].astype(BF16)


def pack_y(c, fine):
    nx, ny, species, nz = c.shape
    count, cells = fine.shape[1:]
    stack = padded(species, 8)
    vmem = pl.BlockSpec(memory_space=pltpu.VMEM)
    far_rows = layer_rows(nx, species, -(-cells // nz))
    rows = layer_rows(nx, species, -(-2 * cells // nz)) if relays(count) else far_rows
    outs = [jax.ShapeDtypeStruct((n, nz), BF16) for n in (rows, far_rows)]
    direct = 0 if relays(count) else max(count - 3, 0)
    outs += [jax.ShapeDtypeStruct((species, cells), BF16)] * (1 + direct)
    return pl.pallas_call(
        pack_y_kernel,
        in_specs=[pl.BlockSpec(memory_space=pltpu.HBM)] * 2,
        out_specs=[vmem] * len(outs),
        out_shape=outs,
        scratch_shapes=[
            pltpu.VMEM((2, nx, species, nz), F32),
            pltpu.VMEM((rows, nz), F32),
            pltpu.VMEM(fine.shape, BF16),
            pltpu.VMEM((cells // 128, stack * padded(count, 8), 128), F32),
            pltpu.SemaphoreType.DMA((2, nx)),
            pltpu.SemaphoreType.DMA,
        ],
        compiler_params=pltpu.CompilerParams(vmem_limit_bytes=LIMIT),
        name="pack_y",
    )(
        pltpu.with_memory_space_constraint(c, pltpu.HBM),
        pltpu.with_memory_space_constraint(fine, pltpu.HBM),
    )


def relays(count):
    return count == 4


def relay_kernel(near, after, out, wide, width):
    species, cells = out.shape
    wide[...] = near[...].astype(F32)
    places = blocks_of(width, species, near.shape[1], cells // 128, 1)
    pieces = [wide[row : row + species, lane : lane + 128] for row, lane in places]
    out[...] = jnp.concatenate(pieces, axis=1).astype(BF16)


def relay(near, after, width, species, cells):
    vmem = pl.BlockSpec(memory_space=pltpu.VMEM)
    return pl.pallas_call(
        functools.partial(relay_kernel, width=width),
        in_specs=[vmem, pl.BlockSpec(memory_space=pl.ANY)],
        out_specs=vmem,
        out_shape=jax.ShapeDtypeStruct((species, cells), BF16),
        scratch_shapes=[pltpu.VMEM(near.shape, F32)],
        compiler_params=pltpu.CompilerParams(vmem_limit_bytes=LIMIT),
        name="relay",
    )(near, after)


def pack_x_kernel(c, after, out, tmp, x):
    nx, ny, species, _ = c.shape
    pack_layer([c[x, r] for r in range(ny)], tmp, species)
    out[...] = tmp[...].astype(BF16)


def pack_x(c, after, x):
    nx, ny, species, nz = c.shape
    vmem = pl.BlockSpec(memory_space=pltpu.VMEM)
    shape = (layer_rows(ny, species), nz)
    return pl.pallas_call(
        functools.partial(pack_x_kernel, x=x),
        in_specs=[vmem, pl.BlockSpec(memory_space=pl.ANY)],
        out_specs=vmem,
        out_shape=jax.ShapeDtypeStruct(shape, BF16),
        scratch_shapes=[pltpu.VMEM(shape, F32)],
        compiler_params=pltpu.CompilerParams(vmem_limit_bytes=LIMIT),
        name="pack_x",
    )(c, after)


def coarse_kernel(
    pos, c, rate, coef, spread, ghost, after, adv, old, new, mix, spread16, ghost16, columns, scratch
):
    count, stack, nz = adv.shape
    boxes = pos.shape[1]
    width = c.shape[0]
    mix[...] = mixing(rate, scratch, stack, 2)
    mixed = mixing(rate, scratch, stack, GROUP)
    spread16[...] = spread[...].astype(BF16)
    ghost16[...] = ghost[...].astype(BF16)
    for k in range(count):
        columns[k, c.shape[2] :] = jnp.zeros((stack - c.shape[2], nz), F32)
        columns[k, : c.shape[2]] = c[k // width, k % width]
    diff = column(coef, stack)
    for first in range(0, count, 2 * GROUP):
        some = range(first, min(first + 2 * GROUP, count))
        made = react_all(mixed, [columns[k] for k in some])
        for k in some:
            x, y = k // width, k % width
            mine = columns[k]
            lap = pltpu.roll(mine, 1, 1) + pltpu.roll(mine, nz - 1, 1) - 6.0 * mine
            if x > 0:
                lap = lap + columns[k - width]
            if x < width - 1:
                lap = lap + columns[k + width]
            if y > 0:
                lap = lap + columns[k - 1]
            if y < width - 1:
                lap = lap + columns[k + 1]
            value = mine + diff * lap + made[k - first]
            adv[k] = value
    lanes = old.shape[1]
    cell = lanes_of(stack, lanes) // width
    for i in range(boxes):
        lane = pos[0, i] * width
        start = pl.multiple_of(jnp.minimum(lane // 128, nz // 128 - 2) * 128, 128)
        offset = lane - start
        for source, out in ((columns, old), (adv, new)):
            total = jnp.zeros((stack, lanes), F32)
            for k in range(count):
                if k // width in (0, width - 1) and k % width in (0, width - 1):
                    continue
                part = source[k, :, pl.ds(start, PATCH)]
                moved = pltpu.roll(part, (k * width - offset) & (PATCH - 1), 1)
                total = jnp.where(cell == k, moved, total)
            out[i * stack : (i + 1) * stack] = total


def coarse_part(pos, c, rate, coef, table, stack, after):
    nx, ny, species, nz = c.shape
    boxes = pos.shape[1]
    lanes = padded(nx**3, PATCH)
    vmem = pl.BlockSpec(memory_space=pltpu.VMEM)
    small = jax.ShapeDtypeStruct((boxes * stack, lanes), F32)
    size = padded(2 * GROUP * stack, 128)
    return pl.pallas_call(
        coarse_kernel,
        in_specs=[vmem] * 6 + [pl.BlockSpec(memory_space=pl.ANY)],
        out_specs=[vmem] * 6,
        out_shape=[
            jax.ShapeDtypeStruct((nx * ny, stack, nz), F32),
            small,
            small,
            jax.ShapeDtypeStruct((4 * stack, 4 * stack), BF16),
            jax.ShapeDtypeStruct(table["spread"].shape, BF16),
            jax.ShapeDtypeStruct(table["ghost"].shape, BF16),
        ],
        scratch_shapes=[
            pltpu.VMEM((nx * ny, stack, nz), F32),
            pltpu.VMEM((size, size), F32),
        ],
        compiler_params=pltpu.CompilerParams(vmem_limit_bytes=LIMIT),
        cost_estimate=pl.CostEstimate(
            flops=800 * c.size, bytes_accessed=12 * c.size, transcendentals=0
        ),
        name="coarse_part",
    )(pos, c, rate, coef, jnp.asarray(table["spread"]), jnp.asarray(table["ghost"]), after)


def by_box(total, boxes, half):
    each = 4 * half * half
    lane = lax.broadcasted_iota(jnp.int32, total.shape, 1)
    rows = [
        jnp.where((lane >= i * each) & (lane < (i + 1) * each), total, 0.0) for i in range(boxes)
    ]
    return jnp.concatenate(rows, axis=0)


def gather_faces(pos, layers, faces, half, stack, species, nz, total):
    lane = lanes_of(stack)
    for ref, face in zip(layers, faces):
        for i in range(pos.shape[1]):
            start = pos[0, i] * (half + 2) + 1
            masks = tiles_of(stack, nz, start, half)
            for r in range(half):
                base = ((i * 4 + face) * half + r) * half
                at = (r + 1) * species
                moved = turn(fold(ref[at : at + stack], masks), base - start)
                tiles = []
                for t in range(total.shape[1] // 128):
                    along = lane + (t * 128 - base)
                    here = (along >= 0) & (along < half)
                    tiles.append(jnp.where(here, moved, total[:, t * 128 : (t + 1) * 128]))
                total = tiles[0] if len(tiles) == 1 else jnp.concatenate(tiles, axis=1)
    return total


def y_faces_kernel(pos, owner, near, far, own, after, from_y, start, wide):
    stack = from_y.shape[0]
    species, cells = own.shape
    nz = near.shape[1]
    boxes = pos.shape[1]
    width = far.shape[0] // species - -(-cells // nz)
    half = width - 2
    wide[0] = near[...].astype(F32)
    wide[1, : far.shape[0]] = far[...].astype(F32)
    me, count = lax.axis_index("yz"), lax.axis_size("yz")
    odd = me % 2
    zero = jnp.zeros(from_y.shape, F32)
    layers = (wide.at[0], wide.at[1])
    from_y[...] = gather_faces(pos, layers, (3 - odd, 2 + odd), half, stack, species, nz, zero)
    direct = own[...].astype(F32)
    places = blocks_of(width, species, nz, cells // 128)
    edge = species // 8 * 8
    for i in range(boxes):
        by_near = owner[0, i] == neighbour(me, count, True)
        by_far = owner[0, i] == neighbour(me, count, False)
        at = i * stack
        start[at + edge : at + stack] = jnp.zeros((stack - edge, cells), F32)
        for q, (row, lane) in enumerate(places):
            part = direct[:, q * 128 : (q + 1) * 128]
            sent = [wide[n, row : row + species, lane : lane + 128] for n in range(2)]
            part = jnp.where(by_far, sent[1], jnp.where(by_near, sent[0], part))
            start[at : at + species, q * 128 : (q + 1) * 128] = part


def y_faces(pos, owner, near, far, own, after, half, stack):
    vmem = pl.BlockSpec(memory_space=pltpu.VMEM)
    boxes = pos.shape[1]
    lanes = padded(boxes * 4 * half * half, 128)
    return pl.pallas_call(
        y_faces_kernel,
        in_specs=[vmem] * 5 + [pl.BlockSpec(memory_space=pl.ANY)],
        out_specs=[vmem] * 2,
        out_shape=[
            jax.ShapeDtypeStruct((stack, lanes), F32),
            jax.ShapeDtypeStruct((boxes * stack, own.shape[1]), F32),
        ],
        scratch_shapes=[pltpu.VMEM((2, *near.shape), F32)],
        compiler_params=pltpu.CompilerParams(vmem_limit_bytes=LIMIT),
        cost_estimate=pl.CostEstimate(flops=10**9, bytes_accessed=ORDER, transcendentals=0),
        name="y_faces",
    )(pos, owner, near, far, own, after)


def fine_kernel(pos, owner, x_low, x_high, start, *refs, count, edge):
    others, refs = refs[: count - 3], refs[count - 3 :]
    old, new, mix, coef, spread, ghost, from_y = refs[:7]
    packets = refs[7 : 7 + count]
    fix, kept, final, field, wide = refs[7 + count :]
    species = packets[0].shape[0]
    stack = from_y.shape[0]
    boxes = final.shape[0] // stack
    cells = final.shape[1]
    me = lax.axis_index("yz")
    mixed = mix[...]

    def reaction(value):
        pairs = [value[at : at + 2 * stack] for at in range(0, boxes * stack, 2 * stack)]
        return jnp.concatenate([react(mixed, pair) for pair in pairs], axis=0)

    nz = x_low.shape[1]
    half = edge // 2
    wide[0, : x_low.shape[0]] = x_low[...].astype(F32)
    wide[1, : x_high.shape[0]] = x_high[...].astype(F32)
    sent = [ref[...].astype(F32) for ref in others]
    for i in range(boxes):
        at = i * stack
        field[at : at + stack] = start[at : at + stack]
        back = lax.rem(me - owner[0, i] + count, count)
        value = start[at : at + species]
        for k in range(len(sent)):
            value = jnp.where(back == k + 2, sent[k], value)
        field[at : at + species] = value
    diff = jnp.concatenate([column(coef, stack)] * boxes, axis=0)
    old_v, new_v = old[...], new[...]
    sums = old_v + new_v
    spread_v = spread[...]
    both = rows_dot(jnp.concatenate([old_v, sums], axis=0), spread_v)
    ghost0, ghost1 = both[: boxes * stack], both[boxes * stack :]
    index = lax.broadcasted_iota(jnp.int32, (1, cells), 1)
    at = (index // (edge * edge), index // edge % edge, index % edge)
    step = (edge * edge, edge, 1)

    def inside(value):
        lap = -6.0 * value
        for axis in range(3):
            before = pltpu.roll(value, step[axis], 1)
            after = pltpu.roll(value, cells - step[axis], 1)
            lap = lap + jnp.where(at[axis] == 0, 0.0, before)
            lap = lap + jnp.where(at[axis] == edge - 1, 0.0, after)
        return lap

    first = field[...]
    second = first + 2.0 * diff * (inside(first) + ghost0) + 0.5 * reaction(first)
    base = second + diff * (2.0 * inside(second) + ghost1) + 0.5 * reaction(second)
    layers = (wide.at[0], wide.at[1])
    total = gather_faces(pos, layers, (0, 1), half, stack, species, nz, from_y[...])
    kept[...] = total
    stacked = by_box(total, boxes, half).astype(BF16)
    value = base + diff * diff * dot(stacked, ghost[...])
    final[...] = value
    for k, out in enumerate(packets):
        dest = partner(me, k, count)
        packet = jnp.zeros((species, cells), F32)
        for i in range(boxes):
            packet = jnp.where(owner[0, i] == dest, value[i * stack : i * stack + species], packet)
        out[...] = packet.astype(BF16)
    pooled = lax.dot_general(
        parts(first + second), spread_v, (((1,), (1,)), ((), ())), preferred_element_type=F32
    )
    pooled = 0.25 * (pooled[: boxes * stack] + pooled[boxes * stack :])
    width = edge // 2 + 2
    lanes = old.shape[1]
    lane = lax.broadcasted_iota(jnp.int32, (1, lanes), 1)
    at = (lane // (width * width), lane // width % width, lane % width)
    step = (width * width, width, 1)
    inner = [(a >= 1) & (a <= width - 2) for a in at]
    rest = pooled - 0.5 * sums
    result = jnp.zeros_like(old_v)
    for axis in range(3):
        sides = inner[(axis + 1) % 3] & inner[(axis + 2) % 3]
        for edge_at, shift in ((0, lanes - step[axis]), (width - 1, step[axis])):
            mask = sides & (at[axis] == edge_at)
            fixed = rest - pltpu.roll(old_v, shift, 1)
            result = jnp.where(mask, fixed, result)
    fix[...] = diff * result


def fine_part(pos, owner, low, high, start, others, old, new, mix, coef, spread, ghost, from_y, edge):
    boxes = owner.shape[1]
    count = len(others) + 3
    stack = from_y.shape[0]
    cells = start.shape[1]
    vmem = pl.BlockSpec(memory_space=pltpu.VMEM)
    return pl.pallas_call(
        functools.partial(fine_kernel, count=count, edge=edge),
        in_specs=[vmem] * (count + 9),
        out_specs=[vmem] * (count + 3),
        out_shape=[jax.ShapeDtypeStruct((coef.shape[1], cells), BF16)] * count
        + [
            jax.ShapeDtypeStruct((boxes * stack, old.shape[1]), F32),
            jax.ShapeDtypeStruct(from_y.shape, F32),
            jax.ShapeDtypeStruct((boxes * stack, cells), F32),
        ],
        scratch_shapes=[
            pltpu.VMEM((boxes * stack, cells), F32),
            pltpu.VMEM((2, *low.shape), F32),
        ],
        compiler_params=pltpu.CompilerParams(vmem_limit_bytes=LIMIT),
        name="fine_part",
    )(pos, owner, low, high, start, *others, old, new, mix, coef, spread, ghost, from_y)


def delta_of(field, kept, fix, coef, average, place, half, stack):
    boxes = field.shape[0] // stack
    diffs = jnp.concatenate([column(coef, stack)] * boxes, axis=0)
    stacked = by_box(kept[...], boxes, half).astype(BF16)
    halo = dot(stacked, place[...].astype(BF16))
    means = rows_dot(field[...], average[...].astype(BF16))
    return fix[...] - 0.5 * diffs * diffs * halo + means


def correct_kernel(
    pos, adv, x_first, x_second, near, far, coef, field, kept, fix, average, place, out, block, wide, sems, half
):
    count, stack, nz = adv.shape
    species = block.shape[2]
    width = half + 2
    delta = delta_of(field, kept, fix, coef, average, place, half, stack)
    diff = column(coef, stack)
    even = lax.axis_index("yz") % 2 == 0
    rows = x_first.shape[0]
    near_v, far_v = near[:rows].astype(F32), far[:rows].astype(F32)
    wide[0, :rows] = x_first[...].astype(F32)
    wide[1, : x_second.shape[0]] = x_second[...].astype(F32)
    wide[2, :rows] = jnp.where(even, far_v, near_v)
    wide[3, :rows] = jnp.where(even, near_v, far_v)
    boxes = delta.shape[0] // stack
    starts = [pos[0, i] * width for i in range(boxes)]
    cycle = [tiles_of(stack, nz, start, width) for start in starts]
    inside = [tiles_of(stack, nz, start + 1, half) for start in starts]
    lane = lanes_of(stack)
    copies = []
    for k in range(count):
        x, y = k // width, k % width
        value = adv[k]
        for there, at, n in (
            (x == 0, y, 0),
            (x == width - 1, y, 1),
            (y == 0, x, 2),
            (y == width - 1, x, 3),
        ):
            if there:
                value = value + diff * wide[n, at * species : at * species + stack]
        if x not in (0, width - 1) or y not in (0, width - 1):
            tiles = [value[:, t * 128 : (t + 1) * 128] for t in range(nz // 128)]
            covers = 0 < x < width - 1 and 0 < y < width - 1
            for i in range(boxes):
                mine = delta[i * stack : (i + 1) * stack]
                t = k * width // 128
                part = mine[:, t * 128 : (t + 1) * 128]
                if (k + 1) * width > (t + 1) * 128:
                    after = mine[:, (t + 1) * 128 : (t + 2) * 128]
                    part = jnp.where(lane < (k + 1) * width - (t + 1) * 128, after, part)
                moved = turn(part, starts[i] - k * width)
                for t in range(nz // 128):
                    if covers:
                        tiles[t] = jnp.where(inside[i][t], 0.0, tiles[t])
                    tiles[t] = tiles[t] + jnp.where(cycle[i][t], moved, 0.0)
            value = jnp.concatenate(tiles, axis=1)
        block[x, y] = value[:species]
        if y == width - 1:
            copies.append(pltpu.make_async_copy(block.at[x], out.at[x], sems.at[x]))
            copies[-1].start()
    for copy in copies:
        copy.wait()


def correct(pos, adv, halos, coef, field, kept, fix, table, half):
    _, stack, nz = adv.shape
    width = half + 2
    species = coef.shape[1]
    vmem = pl.BlockSpec(memory_space=pltpu.VMEM)
    return pl.pallas_call(
        functools.partial(correct_kernel, half=half),
        in_specs=[vmem] * 12,
        out_specs=pl.BlockSpec(memory_space=pltpu.HBM),
        out_shape=jax.ShapeDtypeStruct((width, width, species, nz), F32),
        scratch_shapes=[
            pltpu.VMEM((width, width, species, nz), F32),
            pltpu.VMEM((4, halos[0].shape[0] + stack, nz), F32),
            pltpu.SemaphoreType.DMA((width,)),
        ],
        compiler_params=pltpu.CompilerParams(vmem_limit_bytes=LIMIT),
        cost_estimate=pl.CostEstimate(
            flops=20 * adv.size, bytes_accessed=12 * adv.size, transcendentals=0
        ),
        name="coarse_correct",
    )(
        pos,
        adv,
        *halos,
        coef,
        field,
        kept,
        fix,
        jnp.asarray(table["average"]),
        jnp.asarray(table["place"]),
    )


def return_order(count):
    return [0, 2, 3, 1] if count == 4 else list(range(count))


def unpack_kernel(*refs):
    packets, (out, rows) = refs[:-2], refs[-2:]
    species, cells = packets[0].shape
    count = len(packets)
    step = rows.shape[1] // padded(species, 8)
    me = lax.axis_index("yz")
    for k, packet in zip(return_order(count), packets):
        source = origin(me, k, count)
        value = packet[...].astype(F32)
        for q in range(cells // 128):
            rows[q, pl.ds(source, species, stride=step), :] = value[:, q * 128 : (q + 1) * 128]
    for s in range(species):
        pieces = [rows[q, s * step : s * step + count] for q in range(cells // 128)]
        out[s] = jnp.concatenate(pieces, axis=1).astype(BF16)


def unpack(packets):
    species, cells = packets[0].shape
    count = len(packets)
    vmem = pl.BlockSpec(memory_space=pltpu.VMEM)
    rows = padded(species, 8) * padded(count, 8)
    return pl.pallas_call(
        unpack_kernel,
        in_specs=[vmem] * count,
        out_specs=vmem,
        out_shape=jax.ShapeDtypeStruct((species, count, cells), BF16),
        scratch_shapes=[pltpu.VMEM((cells // 128, rows, 128), F32)],
        compiler_params=pltpu.CompilerParams(vmem_limit_bytes=LIMIT),
        name="unpack",
    )(*[packets[k] for k in return_order(count)])


def ring(axis, by):
    count = lax.axis_size(axis)
    return [(i, (i + by) % count) for i in range(count)]


def mutual(axis, by):
    count = lax.axis_size(axis)
    one_way = [(i, (i + by) % count) for i in range(0, count, 2)]
    return one_way + [(j, i) for i, j in one_way]


def partner(me, k, count):
    return me ^ k if count & (count - 1) == 0 else lax.rem(me + k, count)


def origin(me, source, count):
    return me ^ source if count & (count - 1) == 0 else lax.rem(me - source + count, count)


def local(coarse_state, fine_state, diffusion, rate, box_pos, box_owner):
    species, width = coarse_state.shape[:2]
    half = width - 2
    stack = padded(species, 8)
    count = lax.axis_size("yz")
    me = lax.axis_index("yz")
    pos, owner = box_pos[0], box_owner[0]
    table = tables(width, pos.shape[1])
    coef = diffusion[None]
    c = jnp.transpose(coarse_state, (1, 2, 0, 3))

    fine = jnp.transpose(fine_state, (1, 0, 2))
    near, far, own, *others = pack_y(c, fine)
    x_high = pack_x(c, own, c.shape[0] - 1)
    x_low = pack_x(c, x_high, 0)
    halos = [
        lax.ppermute(x_high, "gx", ring("gx", 1)),
        lax.ppermute(x_low, "gx", ring("gx", -1)),
        lax.ppermute(near, "yz", mutual("yz", 1)),
        lax.ppermute(far, "yz", mutual("yz", -1)),
    ]
    if relays(count):
        after = passed = relay(halos[2], x_low, width, *own.shape)
        others = [lax.ppermute(passed, "yz", mutual("yz", -1))]
    else:
        after = x_low
        others = [lax.ppermute(slot, "yz", ring("yz", 2 + k)) for k, slot in enumerate(others)]

    adv, old, new, mix, spread, ghost = coarse_part(
        pos, c, rate, coef, table, stack, after
    )
    from_y, start = y_faces(pos, owner, *halos[2:], own, old, half, stack)
    made = fine_part(
        pos, owner, *halos[:2], start, others, old, new, mix, coef, spread, ghost, from_y, 2 * half
    )
    packets, (fix, kept, field) = made[:count], made[count:]

    def swap(value, k):
        even = count & (count - 1) == 0
        pairs = [(i, i ^ k if even else (i + k) % count) for i in range(count)]
        return lax.ppermute(value, "yz", pairs)

    back = [packets[0]] + [swap(packets[k], k) for k in range(1, count)]
    coarse_next = correct(pos, adv, halos, coef, field, kept, fix, table, half)

    fine_next = jnp.transpose(unpack(back), (1, 0, 2))
    return jnp.transpose(coarse_next, (2, 0, 1, 3)), fine_next


def solution(mesh):
    in_specs = (
        P(None, "gx", "yz", None),
        P(("gx", "yz"), None, None),
        P(),
        P(),
        P("gx", "yz", None),
        P("gx", "yz", None),
    )
    out_specs = (P(None, "gx", "yz", None), P(("gx", "yz"), None, None))
    return jax.shard_map(local, mesh=mesh, in_specs=in_specs, out_specs=out_specs, check_vma=False)
```

```python
import functools

import jax
import jax.numpy as jnp
import numpy as np
from jax import lax
from jax.experimental import pallas as pl
from jax.experimental.pallas import tpu as pltpu
from jax.sharding import PartitionSpec as P

F32 = jnp.float32
BF16 = jnp.bfloat16
LIMIT = 12 * 1024 * 1024
PATCH = 256
ORDER = 20_000_000


def padded(count, unit):
    return -(-count // unit) * unit


@functools.lru_cache(maxsize=None)
def tables(width, boxes):
    half = width - 2
    edge = 2 * half
    cells = width**3
    lanes = padded(cells, PATCH)
    fine = edge**3
    spread = np.zeros((lanes, fine), np.float32)
    average = np.zeros((fine, lanes), np.float32)
    halo = padded(boxes * 4 * half * half, 128)
    place = np.zeros((halo, lanes), np.float32)

    def cell(x, y, z):
        return (x * width + y) * width + z

    for number in range(6):
        axis, high = divmod(number, 2)
        others = [a for a in range(3) if a != axis]
        for r in range(half):
            for q in range(half):
                at = [0, 0, 0]
                at[axis] = width - 1 if high else 0
                at[others[0]] = r + 1
                at[others[1]] = q + 1
                here = cell(*at)
                for i in range(2):
                    for j in range(2):
                        pos = [0, 0, 0]
                        pos[axis] = edge - 1 if high else 0
                        pos[others[0]] = 2 * r + i
                        pos[others[1]] = 2 * q + j
                        spread[here, (pos[0] * edge + pos[1]) * edge + pos[2]] = 1.0
                if number < 4:
                    for box in range(boxes):
                        place[((box * 4 + number) * half + r) * half + q, here] = 1.0
    for x in range(edge):
        for y in range(edge):
            for z in range(edge):
                average[(x * edge + y) * edge + z, cell(x // 2 + 1, y // 2 + 1, z // 2 + 1)] = 0.125
    return dict(spread=spread, average=average, place=place, ghost=place @ spread)


def column(diffusion, stack):
    species = diffusion.shape[1]
    row = lax.broadcasted_iota(jnp.int32, (stack, species), 0)
    lane = lax.broadcasted_iota(jnp.int32, (stack, species), 1)
    return jnp.sum(jnp.where(row == lane, diffusion[...], 0.0), axis=1, keepdims=True)


def split(value):
    high = value.astype(BF16).astype(F32)
    return high, value - high


def parts(value):
    return jnp.concatenate(split(value), axis=0).astype(BF16)


def dot(a, b):
    return jnp.dot(a, b, preferred_element_type=F32)


def rows_dot(value, table):
    rows = value.shape[0]
    both = dot(parts(value), table)
    return both[:rows] + both[rows:]


GROUP = 5


def mixing(rate, scratch, stack, group):
    species = rate.shape[0]
    size = group * stack
    scratch[...] = jnp.zeros_like(scratch)
    high, low = split(rate[...])
    for b in range(group):
        at = b * stack
        for row, lane, part in ((at, at, high), (at, size + at, high), (size + at, at, low)):
            scratch[row : row + species, lane : lane + species] = part
    return scratch[: 2 * size, : 2 * size].astype(BF16)


def react(mix, fields):
    size = fields.shape[0]
    both = dot(mix, parts(fields))
    return both[:size] + both[size:]


def react_all(mix, fields):
    stack, depth = fields[0].shape
    made = [[] for _ in fields]

    def product(blocks):
        size = len(blocks[0])
        blank = [jnp.zeros_like(blocks[0][0])] * (GROUP - size)
        columns = [jnp.concatenate(block + blank, axis=0) for block in blocks]
        out = react(mix, jnp.concatenate(columns, axis=1))
        lanes = out.shape[1] // len(blocks)
        return [
            [out[b * stack : (b + 1) * stack, n * lanes : (n + 1) * lanes] for b in range(size)]
            for n in range(len(blocks))
        ]

    for lane in range(0, depth, 256):
        if lane + 256 <= depth:
            for at in range(0, len(fields), GROUP):
                block = [f[:, lane : lane + 256] for f in fields[at : at + GROUP]]
                for b, value in enumerate(product([block])[0]):
                    made[at + b].append(value)
        else:
            half = -(-len(fields) // 2)
            blocks = [[f[:, lane:] for f in part] for part in (fields[:half], fields[half:])]
            blocks[1] += [jnp.zeros_like(blocks[0][0])] * (half - len(blocks[1]))
            for n, values in enumerate(product(blocks)):
                for b, value in enumerate(values):
                    if n * half + b < len(fields):
                        made[n * half + b].append(value)
    return [jnp.concatenate(value, axis=1) for value in made]


def lanes_of(stack, lanes=128):
    return lax.broadcasted_iota(jnp.int32, (stack, lanes), 1)


def tiles_of(stack, depth, start, width):
    lane = lanes_of(stack)
    masks = []
    for t in range(depth // 128):
        along = lane + (t * 128 - start)
        masks.append((along >= 0) & (along < width))
    return masks


def fold(value, masks):
    out = value[:, :128]
    for t in range(1, len(masks)):
        out = jnp.where(masks[t], value[:, t * 128 : (t + 1) * 128], out)
    return out


def turn(value, by):
    return pltpu.roll(value, by & 127, 1)


def neighbour(me, count, even_up):
    step = jnp.where((me % 2 == 0) == even_up, 1, count - 1)
    return lax.rem(me + step, count)


def layer_rows(width, species, groups=0):
    return padded((width + groups) * species, 16)


def blocks_of(width, species, nz, pieces, slot=0):
    across = nz // 128
    numbers = range(slot * pieces, (slot + 1) * pieces)
    return [((width + n // across) * species, n % across * 128) for n in numbers]


def pack_layer(columns, tmp, species):
    for r, value in enumerate(columns):
        tmp[r * species : (r + 1) * species] = value
    below = len(columns) * species
    tmp[below:] = jnp.zeros((tmp.shape[0] - below, tmp.shape[1]), F32)


def pack_y_kernel(c, fine, near, far, own, *refs):
    others, (layer, tmp, held, rows, sems, fine_sem) = refs[:-6], refs[-6:]
    nx, ny, species, nz = c.shape
    count = fine.shape[1]
    stack = padded(species, 8)
    me = lax.axis_index("yz")
    slots = pltpu.make_async_copy(fine, held, fine_sem)
    slots.start()
    copies = []
    for n, y in enumerate((jnp.where(me % 2 == 0, ny - 1, 0), jnp.where(me % 2 == 0, 0, ny - 1))):
        copies.append(pltpu.make_async_copy(c.at[:, y], layer.at[n], sems.at[n]))
        copies[-1].start()
    slots.wait()
    step = rows.shape[1] // stack
    pieces = rows.shape[0]
    for s in range(species):
        value = held[s].astype(F32)
        for q in range(pieces):
            rows[q, s * step : s * step + count] = value[:, q * 128 : (q + 1) * 128]

    def slot(at):
        return [rows[q, pl.ds(at, species, stride=step), :] for q in range(pieces)]

    own[...] = jnp.concatenate(slot(me), axis=1).astype(BF16)
    for k, out in enumerate(others):
        out[...] = jnp.concatenate(slot(lax.rem(me + 2 + k, count)), axis=1).astype(BF16)
    for n, out in enumerate((far, near)):
        n = 1 - n
        copies[n].wait()
        pack_layer([layer[n, r] for r in range(nx)], tmp, species)
        sent = [slot(neighbour(me, count, n == 0))]
        if n == 0 and relays(count):
            sent.append(slot(lax.rem(me + 2, count)))
        for m, value in enumerate(sent):
            for (row, lane), piece in zip(blocks_of(nx, species, nz, pieces, m), value):
                tmp[row : row + species, lane : lane + 128] = piece
        out[...] = tmp[: out.shape[0]].astype(BF16)


def pack_y(c, fine):
    nx, ny, species, nz = c.shape
    count, cells = fine.shape[1:]
    stack = padded(species, 8)
    vmem = pl.BlockSpec(memory_space=pltpu.VMEM)
    far_rows = layer_rows(nx, species, -(-cells // nz))
    rows = layer_rows(nx, species, -(-2 * cells // nz)) if relays(count) else far_rows
    outs = [jax.ShapeDtypeStruct((n, nz), BF16) for n in (rows, far_rows)]
    direct = 0 if relays(count) else max(count - 3, 0)
    outs += [jax.ShapeDtypeStruct((species, cells), BF16)] * (1 + direct)
    return pl.pallas_call(
        pack_y_kernel,
        in_specs=[pl.BlockSpec(memory_space=pltpu.HBM)] * 2,
        out_specs=[vmem] * len(outs),
        out_shape=outs,
        scratch_shapes=[
            pltpu.VMEM((2, nx, species, nz), F32),
            pltpu.VMEM((rows, nz), F32),
            pltpu.VMEM(fine.shape, BF16),
            pltpu.VMEM((cells // 128, stack * padded(count, 8), 128), F32),
            pltpu.SemaphoreType.DMA((2,)),
            pltpu.SemaphoreType.DMA,
        ],
        compiler_params=pltpu.CompilerParams(vmem_limit_bytes=LIMIT),
        name="pack_y",
    )(
        pltpu.with_memory_space_constraint(c, pltpu.HBM),
        pltpu.with_memory_space_constraint(fine, pltpu.HBM),
    )


def relays(count):
    return count == 4


def relay_kernel(near, after, out, wide, width):
    species, cells = out.shape
    wide[...] = near[...].astype(F32)
    places = blocks_of(width, species, near.shape[1], cells // 128, 1)
    pieces = [wide[row : row + species, lane : lane + 128] for row, lane in places]
    out[...] = jnp.concatenate(pieces, axis=1).astype(BF16)


def relay(near, after, width, species, cells):
    vmem = pl.BlockSpec(memory_space=pltpu.VMEM)
    return pl.pallas_call(
        functools.partial(relay_kernel, width=width),
        in_specs=[vmem, pl.BlockSpec(memory_space=pl.ANY)],
        out_specs=vmem,
        out_shape=jax.ShapeDtypeStruct((species, cells), BF16),
        scratch_shapes=[pltpu.VMEM(near.shape, F32)],
        compiler_params=pltpu.CompilerParams(vmem_limit_bytes=LIMIT),
        name="relay",
    )(near, after)


def pack_x_kernel(c, after, out, tmp, x):
    nx, ny, species, _ = c.shape
    pack_layer([c[x, r] for r in range(ny)], tmp, species)
    out[...] = tmp[...].astype(BF16)


def pack_x(c, after, x):
    nx, ny, species, nz = c.shape
    vmem = pl.BlockSpec(memory_space=pltpu.VMEM)
    shape = (layer_rows(ny, species), nz)
    return pl.pallas_call(
        functools.partial(pack_x_kernel, x=x),
        in_specs=[vmem, pl.BlockSpec(memory_space=pl.ANY)],
        out_specs=vmem,
        out_shape=jax.ShapeDtypeStruct(shape, BF16),
        scratch_shapes=[pltpu.VMEM(shape, F32)],
        compiler_params=pltpu.CompilerParams(vmem_limit_bytes=LIMIT),
        name="pack_x",
    )(c, after)


def coarse_kernel(
    pos, c, rate, coef, spread, ghost, after, adv, old, new, mix, spread16, ghost16, columns, scratch
):
    count, stack, nz = adv.shape
    boxes = pos.shape[1]
    width = c.shape[0]
    mix[...] = mixing(rate, scratch, stack, 2)
    mixed = mixing(rate, scratch, stack, GROUP)
    spread16[...] = spread[...].astype(BF16)
    ghost16[...] = ghost[...].astype(BF16)
    for k in range(count):
        columns[k, c.shape[2] :] = jnp.zeros((stack - c.shape[2], nz), F32)
        columns[k, : c.shape[2]] = c[k // width, k % width]
    diff = column(coef, stack)
    for first in range(0, count, 2 * GROUP):
        some = range(first, min(first + 2 * GROUP, count))
        made = react_all(mixed, [columns[k] for k in some])
        for k in some:
            x, y = k // width, k % width
            mine = columns[k]
            lap = pltpu.roll(mine, 1, 1) + pltpu.roll(mine, nz - 1, 1) - 6.0 * mine
            if x > 0:
                lap = lap + columns[k - width]
            if x < width - 1:
                lap = lap + columns[k + width]
            if y > 0:
                lap = lap + columns[k - 1]
            if y < width - 1:
                lap = lap + columns[k + 1]
            value = mine + diff * lap + made[k - first]
            adv[k] = value
    lanes = old.shape[1]
    cell = lanes_of(stack, lanes) // width
    for i in range(boxes):
        lane = pos[0, i] * width
        start = pl.multiple_of(jnp.minimum(lane // 128, nz // 128 - 2) * 128, 128)
        offset = lane - start
        for source, out in ((columns, old), (adv, new)):
            total = jnp.zeros((stack, lanes), F32)
            for k in range(count):
                if k // width in (0, width - 1) and k % width in (0, width - 1):
                    continue
                part = source[k, :, pl.ds(start, PATCH)]
                moved = pltpu.roll(part, (k * width - offset) & (PATCH - 1), 1)
                total = jnp.where(cell == k, moved, total)
            out[i * stack : (i + 1) * stack] = total


def coarse_part(pos, c, rate, coef, table, stack, after):
    nx, ny, species, nz = c.shape
    boxes = pos.shape[1]
    lanes = padded(nx**3, PATCH)
    vmem = pl.BlockSpec(memory_space=pltpu.VMEM)
    small = jax.ShapeDtypeStruct((boxes * stack, lanes), F32)
    size = padded(2 * GROUP * stack, 128)
    return pl.pallas_call(
        coarse_kernel,
        in_specs=[vmem] * 6 + [pl.BlockSpec(memory_space=pl.ANY)],
        out_specs=[vmem] * 6,
        out_shape=[
            jax.ShapeDtypeStruct((nx * ny, stack, nz), F32),
            small,
            small,
            jax.ShapeDtypeStruct((4 * stack, 4 * stack), BF16),
            jax.ShapeDtypeStruct(table["spread"].shape, BF16),
            jax.ShapeDtypeStruct(table["ghost"].shape, BF16),
        ],
        scratch_shapes=[
            pltpu.VMEM((nx * ny, stack, nz), F32),
            pltpu.VMEM((size, size), F32),
        ],
        compiler_params=pltpu.CompilerParams(vmem_limit_bytes=LIMIT),
        cost_estimate=pl.CostEstimate(
            flops=800 * c.size, bytes_accessed=12 * c.size, transcendentals=0
        ),
        name="coarse_part",
    )(pos, c, rate, coef, jnp.asarray(table["spread"]), jnp.asarray(table["ghost"]), after)


def by_box(total, boxes, half):
    each = 4 * half * half
    lane = lax.broadcasted_iota(jnp.int32, total.shape, 1)
    rows = [
        jnp.where((lane >= i * each) & (lane < (i + 1) * each), total, 0.0) for i in range(boxes)
    ]
    return jnp.concatenate(rows, axis=0)


def gather_faces(pos, layers, faces, half, stack, species, nz, total):
    lane = lanes_of(stack)
    for ref, face in zip(layers, faces):
        for i in range(pos.shape[1]):
            start = pos[0, i] * (half + 2) + 1
            masks = tiles_of(stack, nz, start, half)
            for r in range(half):
                base = ((i * 4 + face) * half + r) * half
                at = (r + 1) * species
                moved = turn(fold(ref[at : at + stack], masks), base - start)
                tiles = []
                for t in range(total.shape[1] // 128):
                    along = lane + (t * 128 - base)
                    here = (along >= 0) & (along < half)
                    tiles.append(jnp.where(here, moved, total[:, t * 128 : (t + 1) * 128]))
                total = tiles[0] if len(tiles) == 1 else jnp.concatenate(tiles, axis=1)
    return total


def y_faces_kernel(pos, owner, near, far, own, old, new, spread, from_y, start, ghosts, wide):
    stack = from_y.shape[0]
    species, cells = own.shape
    nz = near.shape[1]
    boxes = pos.shape[1]
    width = far.shape[0] // species - -(-cells // nz)
    half = width - 2
    wide[0] = near[...].astype(F32)
    wide[1, : far.shape[0]] = far[...].astype(F32)
    me, count = lax.axis_index("yz"), lax.axis_size("yz")
    odd = me % 2
    zero = jnp.zeros(from_y.shape, F32)
    layers = (wide.at[0], wide.at[1])
    from_y[...] = gather_faces(pos, layers, (3 - odd, 2 + odd), half, stack, species, nz, zero)
    old_v = old[...]
    ghosts[...] = rows_dot(jnp.concatenate([old_v, old_v + new[...]], axis=0), spread[...])
    direct = own[...].astype(F32)
    places = blocks_of(width, species, nz, cells // 128)
    edge = species // 8 * 8
    for i in range(boxes):
        by_near = owner[0, i] == neighbour(me, count, True)
        by_far = owner[0, i] == neighbour(me, count, False)
        at = i * stack
        start[at + edge : at + stack] = jnp.zeros((stack - edge, cells), F32)
        for q, (row, lane) in enumerate(places):
            part = direct[:, q * 128 : (q + 1) * 128]
            sent = [wide[n, row : row + species, lane : lane + 128] for n in range(2)]
            part = jnp.where(by_far, sent[1], jnp.where(by_near, sent[0], part))
            start[at : at + species, q * 128 : (q + 1) * 128] = part


def y_faces(pos, owner, near, far, own, old, new, spread, half, stack):
    vmem = pl.BlockSpec(memory_space=pltpu.VMEM)
    boxes = pos.shape[1]
    lanes = padded(boxes * 4 * half * half, 128)
    return pl.pallas_call(
        y_faces_kernel,
        in_specs=[vmem] * 8,
        out_specs=[vmem] * 3,
        out_shape=[
            jax.ShapeDtypeStruct((stack, lanes), F32),
            jax.ShapeDtypeStruct((boxes * stack, own.shape[1]), F32),
            jax.ShapeDtypeStruct((2 * boxes * stack, own.shape[1]), F32),
        ],
        scratch_shapes=[pltpu.VMEM((2, *near.shape), F32)],
        compiler_params=pltpu.CompilerParams(vmem_limit_bytes=LIMIT),
        cost_estimate=pl.CostEstimate(flops=10**9, bytes_accessed=ORDER, transcendentals=0),
        name="y_faces",
    )(pos, owner, near, far, own, old, new, spread)


def fine_kernel(pos, owner, x_low, x_high, start, *refs, count, edge):
    others, refs = refs[: count - 3], refs[count - 3 :]
    mix, coef, ghosts, ghost, from_y = refs[:5]
    packets = refs[5 : 5 + count]
    mid, kept, final, field, wide = refs[5 + count :]
    species = packets[0].shape[0]
    stack = from_y.shape[0]
    boxes = final.shape[0] // stack
    cells = final.shape[1]
    me = lax.axis_index("yz")
    mixed = mix[...]

    def reaction(value):
        pairs = [value[at : at + 2 * stack] for at in range(0, boxes * stack, 2 * stack)]
        return jnp.concatenate([react(mixed, pair) for pair in pairs], axis=0)

    nz = x_low.shape[1]
    half = edge // 2
    wide[0, : x_low.shape[0]] = x_low[...].astype(F32)
    wide[1, : x_high.shape[0]] = x_high[...].astype(F32)
    sent = [ref[...].astype(F32) for ref in others]
    for i in range(boxes):
        at = i * stack
        field[at : at + stack] = start[at : at + stack]
        back = lax.rem(me - owner[0, i] + count, count)
        value = start[at : at + species]
        for k in range(len(sent)):
            value = jnp.where(back == k + 2, sent[k], value)
        field[at : at + species] = value
    diff = jnp.concatenate([column(coef, stack)] * boxes, axis=0)
    ghost0, ghost1 = ghosts[: boxes * stack], ghosts[boxes * stack :]
    index = lax.broadcasted_iota(jnp.int32, (1, cells), 1)
    at = (index // (edge * edge), index // edge % edge, index % edge)
    step = (edge * edge, edge, 1)

    def inside(value):
        lap = -6.0 * value
        for axis in range(3):
            before = pltpu.roll(value, step[axis], 1)
            after = pltpu.roll(value, cells - step[axis], 1)
            lap = lap + jnp.where(at[axis] == 0, 0.0, before)
            lap = lap + jnp.where(at[axis] == edge - 1, 0.0, after)
        return lap

    first = field[...]
    second = first + 2.0 * diff * (inside(first) + ghost0) + 0.5 * reaction(first)
    base = second + diff * (2.0 * inside(second) + ghost1) + 0.5 * reaction(second)
    layers = (wide.at[0], wide.at[1])
    total = gather_faces(pos, layers, (0, 1), half, stack, species, nz, from_y[...])
    kept[...] = total
    stacked = by_box(total, boxes, half).astype(BF16)
    value = base + diff * diff * dot(stacked, ghost[...])
    final[...] = value
    for k, out in enumerate(packets):
        dest = partner(me, k, count)
        packet = jnp.zeros((species, cells), F32)
        for i in range(boxes):
            packet = jnp.where(owner[0, i] == dest, value[i * stack : i * stack + species], packet)
        out[...] = packet.astype(BF16)
    mid[...] = first + second


def fine_part(pos, owner, low, high, start, others, mix, coef, ghosts, ghost, from_y, edge):
    boxes = owner.shape[1]
    count = len(others) + 3
    stack = from_y.shape[0]
    cells = start.shape[1]
    vmem = pl.BlockSpec(memory_space=pltpu.VMEM)
    return pl.pallas_call(
        functools.partial(fine_kernel, count=count, edge=edge),
        in_specs=[vmem] * (count + 7),
        out_specs=[vmem] * (count + 3),
        out_shape=[jax.ShapeDtypeStruct((coef.shape[1], cells), BF16)] * count
        + [
            jax.ShapeDtypeStruct((boxes * stack, cells), F32),
            jax.ShapeDtypeStruct(from_y.shape, F32),
            jax.ShapeDtypeStruct((boxes * stack, cells), F32),
        ],
        scratch_shapes=[
            pltpu.VMEM((boxes * stack, cells), F32),
            pltpu.VMEM((2, *low.shape), F32),
        ],
        compiler_params=pltpu.CompilerParams(vmem_limit_bytes=LIMIT),
        name="fine_part",
    )(pos, owner, low, high, start, *others, mix, coef, ghosts, ghost, from_y)


def fix_of(mid, old, new, spread, diffs, width):
    old_v = old[...]
    size = old_v.shape[0]
    pooled = lax.dot_general(
        parts(mid[...]), spread[...], (((1,), (1,)), ((), ())), preferred_element_type=F32
    )
    rest = 0.25 * (pooled[:size] + pooled[size:]) - 0.5 * (old_v + new[...])
    lanes = old_v.shape[1]
    lane = lax.broadcasted_iota(jnp.int32, (1, lanes), 1)
    at = (lane // (width * width), lane // width % width, lane % width)
    step = (width * width, width, 1)
    inner = [(a >= 1) & (a <= width - 2) for a in at]
    result = jnp.zeros_like(old_v)
    for axis in range(3):
        sides = inner[(axis + 1) % 3] & inner[(axis + 2) % 3]
        for edge_at, shift in ((0, lanes - step[axis]), (width - 1, step[axis])):
            mask = sides & (at[axis] == edge_at)
            result = jnp.where(mask, rest - pltpu.roll(old_v, shift, 1), result)
    return diffs * result


def delta_of(field, kept, mid, old, new, spread, coef, average, place, half, stack):
    boxes = field.shape[0] // stack
    diffs = jnp.concatenate([column(coef, stack)] * boxes, axis=0)
    halo = dot(by_box(kept[...], boxes, half).astype(BF16), place[...].astype(BF16))
    means = rows_dot(field[...], average[...].astype(BF16))
    fix = fix_of(mid, old, new, spread, diffs, half + 2)
    return fix - 0.5 * diffs * diffs * halo + means


def correct_kernel(
    pos,
    adv,
    x_first,
    x_second,
    near,
    far,
    coef,
    field,
    kept,
    mid,
    old,
    new,
    spread,
    average,
    place,
    out,
    block,
    wide,
    sems,
    half,
):
    count, stack, nz = adv.shape
    species = block.shape[2]
    width = half + 2
    delta = delta_of(field, kept, mid, old, new, spread, coef, average, place, half, stack)
    diff = column(coef, stack)
    even = lax.axis_index("yz") % 2 == 0
    rows = x_first.shape[0]
    near_v, far_v = near[:rows].astype(F32), far[:rows].astype(F32)
    wide[0, :rows] = x_first[...].astype(F32)
    wide[1, : x_second.shape[0]] = x_second[...].astype(F32)
    wide[2, :rows] = jnp.where(even, far_v, near_v)
    wide[3, :rows] = jnp.where(even, near_v, far_v)
    boxes = delta.shape[0] // stack
    starts = [pos[0, i] * width for i in range(boxes)]
    cycle = [tiles_of(stack, nz, start, width) for start in starts]
    inside = [tiles_of(stack, nz, start + 1, half) for start in starts]
    lane = lanes_of(stack)
    copies = []
    for k in range(count):
        x, y = k // width, k % width
        value = adv[k]
        for there, at, n in (
            (x == 0, y, 0),
            (x == width - 1, y, 1),
            (y == 0, x, 2),
            (y == width - 1, x, 3),
        ):
            if there:
                value = value + diff * wide[n, at * species : at * species + stack]
        if x not in (0, width - 1) or y not in (0, width - 1):
            tiles = [value[:, t * 128 : (t + 1) * 128] for t in range(nz // 128)]
            covers = 0 < x < width - 1 and 0 < y < width - 1
            for i in range(boxes):
                mine = delta[i * stack : (i + 1) * stack]
                t = k * width // 128
                part = mine[:, t * 128 : (t + 1) * 128]
                if (k + 1) * width > (t + 1) * 128:
                    after = mine[:, (t + 1) * 128 : (t + 2) * 128]
                    part = jnp.where(lane < (k + 1) * width - (t + 1) * 128, after, part)
                moved = turn(part, starts[i] - k * width)
                for t in range(nz // 128):
                    if covers:
                        tiles[t] = jnp.where(inside[i][t], 0.0, tiles[t])
                    tiles[t] = tiles[t] + jnp.where(cycle[i][t], moved, 0.0)
            value = jnp.concatenate(tiles, axis=1)
        block[x, y] = value[:species]
        if y == width - 1:
            copies.append(pltpu.make_async_copy(block.at[x], out.at[x], sems.at[x]))
            copies[-1].start()
    for copy in copies:
        copy.wait()


def correct(pos, adv, halos, coef, field, kept, mid, old, new, spread, table, half):
    _, stack, nz = adv.shape
    width = half + 2
    species = coef.shape[1]
    vmem = pl.BlockSpec(memory_space=pltpu.VMEM)
    return pl.pallas_call(
        functools.partial(correct_kernel, half=half),
        in_specs=[vmem] * 15,
        out_specs=pl.BlockSpec(memory_space=pltpu.HBM),
        out_shape=jax.ShapeDtypeStruct((width, width, species, nz), F32),
        scratch_shapes=[
            pltpu.VMEM((width, width, species, nz), F32),
            pltpu.VMEM((4, halos[0].shape[0] + stack, nz), F32),
            pltpu.SemaphoreType.DMA((width,)),
        ],
        compiler_params=pltpu.CompilerParams(vmem_limit_bytes=LIMIT),
        cost_estimate=pl.CostEstimate(
            flops=20 * adv.size, bytes_accessed=12 * adv.size, transcendentals=0
        ),
        name="coarse_correct",
    )(
        pos,
        adv,
        *halos,
        coef,
        field,
        kept,
        mid,
        old,
        new,
        spread,
        jnp.asarray(table["average"]),
        jnp.asarray(table["place"]),
    )


def return_order(count):
    return [0, 2, 3, 1] if count == 4 else list(range(count))


def unpack_kernel(*refs):
    packets, (out, rows) = refs[:-2], refs[-2:]
    species, cells = packets[0].shape
    count = len(packets)
    step = rows.shape[1] // padded(species, 8)
    me = lax.axis_index("yz")
    for k, packet in zip(return_order(count), packets):
        source = origin(me, k, count)
        value = packet[...].astype(F32)
        for q in range(cells // 128):
            rows[q, pl.ds(source, species, stride=step), :] = value[:, q * 128 : (q + 1) * 128]
    for s in range(species):
        pieces = [rows[q, s * step : s * step + count] for q in range(cells // 128)]
        out[s] = jnp.concatenate(pieces, axis=1).astype(BF16)


def unpack(packets):
    species, cells = packets[0].shape
    count = len(packets)
    vmem = pl.BlockSpec(memory_space=pltpu.VMEM)
    rows = padded(species, 8) * padded(count, 8)
    return pl.pallas_call(
        unpack_kernel,
        in_specs=[vmem] * count,
        out_specs=vmem,
        out_shape=jax.ShapeDtypeStruct((species, count, cells), BF16),
        scratch_shapes=[pltpu.VMEM((cells // 128, rows, 128), F32)],
        compiler_params=pltpu.CompilerParams(vmem_limit_bytes=LIMIT),
        name="unpack",
    )(*[packets[k] for k in return_order(count)])


def ring(axis, by):
    count = lax.axis_size(axis)
    return [(i, (i + by) % count) for i in range(count)]


def mutual(axis, by):
    count = lax.axis_size(axis)
    one_way = [(i, (i + by) % count) for i in range(0, count, 2)]
    return one_way + [(j, i) for i, j in one_way]


def partner(me, k, count):
    return me ^ k if count & (count - 1) == 0 else lax.rem(me + k, count)


def origin(me, source, count):
    return me ^ source if count & (count - 1) == 0 else lax.rem(me - source + count, count)


def local(coarse_state, fine_state, diffusion, rate, box_pos, box_owner):
    species, width = coarse_state.shape[:2]
    half = width - 2
    stack = padded(species, 8)
    count = lax.axis_size("yz")
    me = lax.axis_index("yz")
    pos, owner = box_pos[0], box_owner[0]
    table = tables(width, pos.shape[1])
    coef = diffusion[None]
    c = jnp.transpose(coarse_state, (1, 2, 0, 3))

    fine = jnp.transpose(fine_state, (1, 0, 2))
    near, far, own, *others = pack_y(c, fine)
    x_high = pack_x(c, own, c.shape[0] - 1)
    x_low = pack_x(c, x_high, 0)
    halos = [
        lax.ppermute(x_high, "gx", ring("gx", 1)),
        lax.ppermute(x_low, "gx", ring("gx", -1)),
        lax.ppermute(near, "yz", mutual("yz", 1)),
        lax.ppermute(far, "yz", mutual("yz", -1)),
    ]
    if relays(count):
        after = passed = relay(halos[2], x_low, width, *own.shape)
        others = [lax.ppermute(passed, "yz", mutual("yz", -1))]
    else:
        after = x_low
        others = [lax.ppermute(slot, "yz", ring("yz", 2 + k)) for k, slot in enumerate(others)]

    adv, old, new, mix, spread, ghost = coarse_part(
        pos, c, rate, coef, table, stack, after
    )
    from_y, start, ghosts = y_faces(pos, owner, *halos[2:], own, old, new, spread, half, stack)
    made = fine_part(
        pos, owner, *halos[:2], start, others, mix, coef, ghosts, ghost, from_y, 2 * half
    )
    packets, (mid, kept, field) = made[:count], made[count:]

    def swap(value, k):
        even = count & (count - 1) == 0
        pairs = [(i, i ^ k if even else (i + k) % count) for i in range(count)]
        return lax.ppermute(value, "yz", pairs)

    back = [packets[0]] + [swap(packets[k], k) for k in range(1, count)]
    coarse_next = correct(pos, adv, halos, coef, field, kept, mid, old, new, spread, table, half)

    fine_next = jnp.transpose(unpack(back), (1, 0, 2))
    return jnp.transpose(coarse_next, (2, 0, 1, 3)), fine_next


def solution(mesh):
    in_specs = (
        P(None, "gx", "yz", None),
        P(("gx", "yz"), None, None),
        P(),
        P(),
        P("gx", "yz", None),
        P("gx", "yz", None),
    )
    out_specs = (P(None, "gx", "yz", None), P(("gx", "yz"), None, None))
    return jax.shard_map(local, mesh=mesh, in_specs=in_specs, out_specs=out_specs, check_vma=False)
```

```python
import functools

import jax
import jax.numpy as jnp
import numpy as np
from jax import lax
from jax.experimental import pallas as pl
from jax.experimental.pallas import tpu as pltpu
from jax.sharding import PartitionSpec as P

F32 = jnp.float32
BF16 = jnp.bfloat16
LIMIT = 12 * 1024 * 1024
PATCH = 256
ORDER = 20_000_000


def padded(count, unit):
    return -(-count // unit) * unit


@functools.lru_cache(maxsize=None)
def tables(width, boxes):
    half = width - 2
    edge = 2 * half
    cells = width**3
    lanes = padded(cells, PATCH)
    fine = edge**3
    spread = np.zeros((lanes, fine), np.float32)
    average = np.zeros((fine, lanes), np.float32)
    halo = padded(boxes * 4 * half * half, 128)
    place = np.zeros((halo, lanes), np.float32)

    def cell(x, y, z):
        return (x * width + y) * width + z

    for number in range(6):
        axis, high = divmod(number, 2)
        others = [a for a in range(3) if a != axis]
        for r in range(half):
            for q in range(half):
                at = [0, 0, 0]
                at[axis] = width - 1 if high else 0
                at[others[0]] = r + 1
                at[others[1]] = q + 1
                here = cell(*at)
                for i in range(2):
                    for j in range(2):
                        pos = [0, 0, 0]
                        pos[axis] = edge - 1 if high else 0
                        pos[others[0]] = 2 * r + i
                        pos[others[1]] = 2 * q + j
                        spread[here, (pos[0] * edge + pos[1]) * edge + pos[2]] = 1.0
                if number < 4:
                    for box in range(boxes):
                        place[((box * 4 + number) * half + r) * half + q, here] = 1.0
    for x in range(edge):
        for y in range(edge):
            for z in range(edge):
                average[(x * edge + y) * edge + z, cell(x // 2 + 1, y // 2 + 1, z // 2 + 1)] = 0.125
    return dict(spread=spread, average=average, place=place, ghost=place @ spread)


def column(diffusion, stack):
    species = diffusion.shape[1]
    row = lax.broadcasted_iota(jnp.int32, (stack, species), 0)
    lane = lax.broadcasted_iota(jnp.int32, (stack, species), 1)
    return jnp.sum(jnp.where(row == lane, diffusion[...], 0.0), axis=1, keepdims=True)


def split(value):
    high = value.astype(BF16).astype(F32)
    return high, value - high


def parts(value):
    return jnp.concatenate(split(value), axis=0).astype(BF16)


def dot(a, b):
    return jnp.dot(a, b, preferred_element_type=F32)


def rows_dot(value, table):
    rows = value.shape[0]
    both = dot(parts(value), table)
    return both[:rows] + both[rows:]


GROUP = 5


def mixing(rate, scratch, stack, group):
    species = rate.shape[0]
    size = group * stack
    scratch[...] = jnp.zeros_like(scratch)
    high, low = split(rate[...])
    for b in range(group):
        at = b * stack
        for row, lane, part in ((at, at, high), (at, size + at, high), (size + at, at, low)):
            scratch[row : row + species, lane : lane + species] = part
    return scratch[: 2 * size, : 2 * size].astype(BF16)


def react(mix, fields):
    size = fields.shape[0]
    both = dot(mix, parts(fields))
    return both[:size] + both[size:]


def react_all(mix, fields):
    stack, depth = fields[0].shape
    made = [[] for _ in fields]

    def product(blocks):
        size = len(blocks[0])
        blank = [jnp.zeros_like(blocks[0][0])] * (GROUP - size)
        columns = [jnp.concatenate(block + blank, axis=0) for block in blocks]
        out = react(mix, jnp.concatenate(columns, axis=1))
        lanes = out.shape[1] // len(blocks)
        return [
            [out[b * stack : (b + 1) * stack, n * lanes : (n + 1) * lanes] for b in range(size)]
            for n in range(len(blocks))
        ]

    for lane in range(0, depth, 256):
        if lane + 256 <= depth:
            for at in range(0, len(fields), GROUP):
                block = [f[:, lane : lane + 256] for f in fields[at : at + GROUP]]
                for b, value in enumerate(product([block])[0]):
                    made[at + b].append(value)
        else:
            half = -(-len(fields) // 2)
            blocks = [[f[:, lane:] for f in part] for part in (fields[:half], fields[half:])]
            blocks[1] += [jnp.zeros_like(blocks[0][0])] * (half - len(blocks[1]))
            for n, values in enumerate(product(blocks)):
                for b, value in enumerate(values):
                    if n * half + b < len(fields):
                        made[n * half + b].append(value)
    return [jnp.concatenate(value, axis=1) for value in made]


def lanes_of(stack, lanes=128):
    return lax.broadcasted_iota(jnp.int32, (stack, lanes), 1)


def tiles_of(stack, depth, start, width):
    lane = lanes_of(stack)
    masks = []
    for t in range(depth // 128):
        along = lane + (t * 128 - start)
        masks.append((along >= 0) & (along < width))
    return masks


def fold(value, masks):
    out = value[:, :128]
    for t in range(1, len(masks)):
        out = jnp.where(masks[t], value[:, t * 128 : (t + 1) * 128], out)
    return out


def turn(value, by):
    return pltpu.roll(value, by & 127, 1)


def neighbour(me, count, even_up):
    step = jnp.where((me % 2 == 0) == even_up, 1, count - 1)
    return lax.rem(me + step, count)


def layer_rows(width, species, groups=0):
    return padded((width + groups) * species, 16)


def blocks_of(width, species, nz, pieces, slot=0):
    across = nz // 128
    numbers = range(slot * pieces, (slot + 1) * pieces)
    return [((width + n // across) * species, n % across * 128) for n in numbers]


def pack_layer(columns, tmp, species):
    for r, value in enumerate(columns):
        tmp[r * species : (r + 1) * species] = value
    below = len(columns) * species
    tmp[below:] = jnp.zeros((tmp.shape[0] - below, tmp.shape[1]), F32)


def pack_y_kernel(c, fine, near, far, own, *refs):
    others, (layer, tmp, held, rows, sems, fine_sem) = refs[:-6], refs[-6:]
    nx, ny, species, nz = c.shape
    count = fine.shape[1]
    stack = padded(species, 8)
    me = lax.axis_index("yz")
    slots = pltpu.make_async_copy(fine, held, fine_sem)
    slots.start()
    copies = []
    for n, y in enumerate((jnp.where(me % 2 == 0, ny - 1, 0), jnp.where(me % 2 == 0, 0, ny - 1))):
        copies.append(pltpu.make_async_copy(c.at[:, y], layer.at[n], sems.at[n]))
        copies[-1].start()
    slots.wait()
    step = rows.shape[1] // stack
    pieces = rows.shape[0]
    for s in range(species):
        value = held[s].astype(F32)
        for q in range(pieces):
            rows[q, s * step : s * step + count] = value[:, q * 128 : (q + 1) * 128]

    def slot(at):
        return [rows[q, pl.ds(at, species, stride=step), :] for q in range(pieces)]

    own[...] = jnp.concatenate(slot(me), axis=1).astype(BF16)
    for k, out in enumerate(others):
        out[...] = jnp.concatenate(slot(lax.rem(me + 2 + k, count)), axis=1).astype(BF16)
    for n, out in enumerate((far, near)):
        n = 1 - n
        copies[n].wait()
        pack_layer([layer[n, r] for r in range(nx)], tmp, species)
        sent = [slot(neighbour(me, count, n == 0))]
        if n == 0 and relays(count):
            sent.append(slot(lax.rem(me + 2, count)))
        for m, value in enumerate(sent):
            for (row, lane), piece in zip(blocks_of(nx, species, nz, pieces, m), value):
                tmp[row : row + species, lane : lane + 128] = piece
        out[...] = tmp[: out.shape[0]].astype(BF16)


def pack_y(c, fine):
    nx, ny, species, nz = c.shape
    count, cells = fine.shape[1:]
    stack = padded(species, 8)
    vmem = pl.BlockSpec(memory_space=pltpu.VMEM)
    far_rows = layer_rows(nx, species, -(-cells // nz))
    rows = layer_rows(nx, species, -(-2 * cells // nz)) if relays(count) else far_rows
    outs = [jax.ShapeDtypeStruct((n, nz), BF16) for n in (rows, far_rows)]
    direct = 0 if relays(count) else max(count - 3, 0)
    outs += [jax.ShapeDtypeStruct((species, cells), BF16)] * (1 + direct)
    return pl.pallas_call(
        pack_y_kernel,
        in_specs=[pl.BlockSpec(memory_space=pltpu.HBM)] * 2,
        out_specs=[vmem] * len(outs),
        out_shape=outs,
        scratch_shapes=[
            pltpu.VMEM((2, nx, species, nz), F32),
            pltpu.VMEM((rows, nz), F32),
            pltpu.VMEM(fine.shape, BF16),
            pltpu.VMEM((cells // 128, stack * padded(count, 8), 128), F32),
            pltpu.SemaphoreType.DMA((2,)),
            pltpu.SemaphoreType.DMA,
        ],
        compiler_params=pltpu.CompilerParams(vmem_limit_bytes=LIMIT),
        name="pack_y",
    )(
        pltpu.with_memory_space_constraint(c, pltpu.HBM),
        pltpu.with_memory_space_constraint(fine, pltpu.HBM),
    )


def relays(count):
    return count == 4


def relay_kernel(near, after, out, wide, width):
    species, cells = out.shape
    wide[...] = near[...].astype(F32)
    places = blocks_of(width, species, near.shape[1], cells // 128, 1)
    pieces = [wide[row : row + species, lane : lane + 128] for row, lane in places]
    out[...] = jnp.concatenate(pieces, axis=1).astype(BF16)


def relay(near, after, width, species, cells):
    vmem = pl.BlockSpec(memory_space=pltpu.VMEM)
    return pl.pallas_call(
        functools.partial(relay_kernel, width=width),
        in_specs=[vmem, pl.BlockSpec(memory_space=pl.ANY)],
        out_specs=vmem,
        out_shape=jax.ShapeDtypeStruct((species, cells), BF16),
        scratch_shapes=[pltpu.VMEM(near.shape, F32)],
        compiler_params=pltpu.CompilerParams(vmem_limit_bytes=LIMIT),
        name="relay",
    )(near, after)


def pack_x_kernel(c, after, out, tmp, x):
    nx, ny, species, _ = c.shape
    pack_layer([c[x, r] for r in range(ny)], tmp, species)
    out[...] = tmp[...].astype(BF16)


def pack_x(c, after, x):
    nx, ny, species, nz = c.shape
    vmem = pl.BlockSpec(memory_space=pltpu.VMEM)
    shape = (layer_rows(ny, species), nz)
    return pl.pallas_call(
        functools.partial(pack_x_kernel, x=x),
        in_specs=[vmem, pl.BlockSpec(memory_space=pl.ANY)],
        out_specs=vmem,
        out_shape=jax.ShapeDtypeStruct(shape, BF16),
        scratch_shapes=[pltpu.VMEM(shape, F32)],
        compiler_params=pltpu.CompilerParams(vmem_limit_bytes=LIMIT),
        name="pack_x",
    )(c, after)


def coarse_kernel(
    pos, c, rate, coef, spread, ghost, after, adv, old, new, mix, spread16, ghost16, columns, scratch
):
    count, stack, nz = adv.shape
    boxes = pos.shape[1]
    width = c.shape[0]
    mix[...] = mixing(rate, scratch, stack, 2)
    mixed = mixing(rate, scratch, stack, GROUP)
    spread16[...] = spread[...].astype(BF16)
    ghost16[...] = ghost[...].astype(BF16)
    for k in range(count):
        columns[k, c.shape[2] :] = jnp.zeros((stack - c.shape[2], nz), F32)
        columns[k, : c.shape[2]] = c[k // width, k % width]
    diff = column(coef, stack)
    for first in range(0, count, 2 * GROUP):
        some = range(first, min(first + 2 * GROUP, count))
        made = react_all(mixed, [columns[k] for k in some])
        for k in some:
            x, y = k // width, k % width
            mine = columns[k]
            lap = pltpu.roll(mine, 1, 1) + pltpu.roll(mine, nz - 1, 1) - 6.0 * mine
            if x > 0:
                lap = lap + columns[k - width]
            if x < width - 1:
                lap = lap + columns[k + width]
            if y > 0:
                lap = lap + columns[k - 1]
            if y < width - 1:
                lap = lap + columns[k + 1]
            value = mine + diff * lap + made[k - first]
            adv[k] = value
    lanes = old.shape[1]
    cell = lanes_of(stack, lanes) // width
    for i in range(boxes):
        lane = pos[0, i] * width
        start = pl.multiple_of(jnp.minimum(lane // 128, nz // 128 - 2) * 128, 128)
        offset = lane - start
        for source, out in ((columns, old), (adv, new)):
            total = jnp.zeros((stack, lanes), F32)
            for k in range(count):
                if k // width in (0, width - 1) and k % width in (0, width - 1):
                    continue
                part = source[k, :, pl.ds(start, PATCH)]
                moved = pltpu.roll(part, (k * width - offset) & (PATCH - 1), 1)
                total = jnp.where(cell == k, moved, total)
            out[i * stack : (i + 1) * stack] = total


def coarse_part(pos, c, rate, coef, table, stack, after):
    nx, ny, species, nz = c.shape
    boxes = pos.shape[1]
    lanes = padded(nx**3, PATCH)
    vmem = pl.BlockSpec(memory_space=pltpu.VMEM)
    small = jax.ShapeDtypeStruct((boxes * stack, lanes), F32)
    size = padded(2 * GROUP * stack, 128)
    return pl.pallas_call(
        coarse_kernel,
        in_specs=[vmem] * 6 + [pl.BlockSpec(memory_space=pl.ANY)],
        out_specs=[vmem] * 6,
        out_shape=[
            jax.ShapeDtypeStruct((nx * ny, stack, nz), F32),
            small,
            small,
            jax.ShapeDtypeStruct((4 * stack, 4 * stack), BF16),
            jax.ShapeDtypeStruct(table["spread"].shape, BF16),
            jax.ShapeDtypeStruct(table["ghost"].shape, BF16),
        ],
        scratch_shapes=[
            pltpu.VMEM((nx * ny, stack, nz), F32),
            pltpu.VMEM((size, size), F32),
        ],
        compiler_params=pltpu.CompilerParams(vmem_limit_bytes=LIMIT),
        cost_estimate=pl.CostEstimate(
            flops=800 * c.size, bytes_accessed=12 * c.size, transcendentals=0
        ),
        name="coarse_part",
    )(pos, c, rate, coef, jnp.asarray(table["spread"]), jnp.asarray(table["ghost"]), after)


def by_box(total, boxes, half):
    each = 4 * half * half
    lane = lax.broadcasted_iota(jnp.int32, total.shape, 1)
    rows = [
        jnp.where((lane >= i * each) & (lane < (i + 1) * each), total, 0.0) for i in range(boxes)
    ]
    return jnp.concatenate(rows, axis=0)


def gather_faces(pos, layers, faces, half, stack, species, nz, total):
    lane = lanes_of(stack)
    for ref, face in zip(layers, faces):
        for i in range(pos.shape[1]):
            start = pos[0, i] * (half + 2) + 1
            masks = tiles_of(stack, nz, start, half)
            for r in range(half):
                base = ((i * 4 + face) * half + r) * half
                at = (r + 1) * species
                moved = turn(fold(ref[at : at + stack], masks), base - start)
                tiles = []
                for t in range(total.shape[1] // 128):
                    along = lane + (t * 128 - base)
                    here = (along >= 0) & (along < half)
                    tiles.append(jnp.where(here, moved, total[:, t * 128 : (t + 1) * 128]))
                total = tiles[0] if len(tiles) == 1 else jnp.concatenate(tiles, axis=1)
    return total


def y_faces_kernel(
    pos, owner, near, far, x_low, own, old, new, spread, from_y, start, ghosts, wide, x_wide
):
    stack = from_y.shape[0]
    species, cells = own.shape
    nz = near.shape[1]
    boxes = pos.shape[1]
    width = far.shape[0] // species - -(-cells // nz)
    half = width - 2
    wide[0] = near[...].astype(F32)
    wide[1, : far.shape[0]] = far[...].astype(F32)
    x_wide[...] = x_low[...].astype(F32)
    me, count = lax.axis_index("yz"), lax.axis_size("yz")
    odd = me % 2
    zero = jnp.zeros(from_y.shape, F32)
    layers = (wide.at[0], wide.at[1], x_wide)
    faces = (3 - odd, 2 + odd, 0)
    from_y[...] = gather_faces(pos, layers, faces, half, stack, species, nz, zero)
    old_v = old[...]
    ghosts[...] = rows_dot(jnp.concatenate([old_v, old_v + new[...]], axis=0), spread[...])
    direct = own[...].astype(F32)
    places = blocks_of(width, species, nz, cells // 128)
    edge = species // 8 * 8
    for i in range(boxes):
        by_near = owner[0, i] == neighbour(me, count, True)
        by_far = owner[0, i] == neighbour(me, count, False)
        at = i * stack
        start[at + edge : at + stack] = jnp.zeros((stack - edge, cells), F32)
        for q, (row, lane) in enumerate(places):
            part = direct[:, q * 128 : (q + 1) * 128]
            sent = [wide[n, row : row + species, lane : lane + 128] for n in range(2)]
            part = jnp.where(by_far, sent[1], jnp.where(by_near, sent[0], part))
            start[at : at + species, q * 128 : (q + 1) * 128] = part


def y_faces(pos, owner, near, far, x_low, own, old, new, spread, half, stack):
    vmem = pl.BlockSpec(memory_space=pltpu.VMEM)
    boxes = pos.shape[1]
    lanes = padded(boxes * 4 * half * half, 128)
    return pl.pallas_call(
        y_faces_kernel,
        in_specs=[vmem] * 9,
        out_specs=[vmem] * 3,
        out_shape=[
            jax.ShapeDtypeStruct((stack, lanes), F32),
            jax.ShapeDtypeStruct((boxes * stack, own.shape[1]), F32),
            jax.ShapeDtypeStruct((2 * boxes * stack, own.shape[1]), F32),
        ],
        scratch_shapes=[pltpu.VMEM((2, *near.shape), F32), pltpu.VMEM(x_low.shape, F32)],
        compiler_params=pltpu.CompilerParams(vmem_limit_bytes=LIMIT),
        cost_estimate=pl.CostEstimate(flops=10**9, bytes_accessed=ORDER, transcendentals=0),
        name="y_faces",
    )(pos, owner, near, far, x_low, own, old, new, spread)


def fine_kernel(pos, owner, x_high, start, *refs, count, edge):
    others, refs = refs[: count - 3], refs[count - 3 :]
    mix, coef, ghosts, ghost, from_y = refs[:5]
    packets = refs[5 : 5 + count]
    mid, kept, final, field, wide = refs[5 + count :]
    species = packets[0].shape[0]
    stack = from_y.shape[0]
    boxes = final.shape[0] // stack
    cells = final.shape[1]
    me = lax.axis_index("yz")
    mixed = mix[...]

    def reaction(value):
        pairs = [value[at : at + 2 * stack] for at in range(0, boxes * stack, 2 * stack)]
        return jnp.concatenate([react(mixed, pair) for pair in pairs], axis=0)

    nz = x_high.shape[1]
    half = edge // 2
    wide[...] = x_high[...].astype(F32)
    sent = [ref[...].astype(F32) for ref in others]
    for i in range(boxes):
        at = i * stack
        field[at : at + stack] = start[at : at + stack]
        back = lax.rem(me - owner[0, i] + count, count)
        value = start[at : at + species]
        for k in range(len(sent)):
            value = jnp.where(back == k + 2, sent[k], value)
        field[at : at + species] = value
    diff = jnp.concatenate([column(coef, stack)] * boxes, axis=0)
    ghost0, ghost1 = ghosts[: boxes * stack], ghosts[boxes * stack :]
    index = lax.broadcasted_iota(jnp.int32, (1, cells), 1)
    at = (index // (edge * edge), index // edge % edge, index % edge)
    step = (edge * edge, edge, 1)

    def inside(value):
        lap = -6.0 * value
        for axis in range(3):
            before = pltpu.roll(value, step[axis], 1)
            after = pltpu.roll(value, cells - step[axis], 1)
            lap = lap + jnp.where(at[axis] == 0, 0.0, before)
            lap = lap + jnp.where(at[axis] == edge - 1, 0.0, after)
        return lap

    first = field[...]
    second = first + 2.0 * diff * (inside(first) + ghost0) + 0.5 * reaction(first)
    base = second + diff * (2.0 * inside(second) + ghost1) + 0.5 * reaction(second)
    total = gather_faces(pos, [wide], [1], half, stack, species, nz, from_y[...])
    kept[...] = total
    stacked = by_box(total, boxes, half).astype(BF16)
    value = base + diff * diff * dot(stacked, ghost[...])
    final[...] = value
    for k, out in enumerate(packets):
        dest = partner(me, k, count)
        packet = jnp.zeros((species, cells), F32)
        for i in range(boxes):
            packet = jnp.where(owner[0, i] == dest, value[i * stack : i * stack + species], packet)
        out[...] = packet.astype(BF16)
    mid[...] = first + second


def fine_part(pos, owner, high, start, others, mix, coef, ghosts, ghost, from_y, edge):
    boxes = owner.shape[1]
    count = len(others) + 3
    stack = from_y.shape[0]
    cells = start.shape[1]
    vmem = pl.BlockSpec(memory_space=pltpu.VMEM)
    return pl.pallas_call(
        functools.partial(fine_kernel, count=count, edge=edge),
        in_specs=[vmem] * (count + 6),
        out_specs=[vmem] * (count + 3),
        out_shape=[jax.ShapeDtypeStruct((coef.shape[1], cells), BF16)] * count
        + [
            jax.ShapeDtypeStruct((boxes * stack, cells), F32),
            jax.ShapeDtypeStruct(from_y.shape, F32),
            jax.ShapeDtypeStruct((boxes * stack, cells), F32),
        ],
        scratch_shapes=[
            pltpu.VMEM((boxes * stack, cells), F32),
            pltpu.VMEM(high.shape, F32),
        ],
        compiler_params=pltpu.CompilerParams(vmem_limit_bytes=LIMIT),
        name="fine_part",
    )(pos, owner, high, start, *others, mix, coef, ghosts, ghost, from_y)


def fix_of(mid, old, new, spread, diffs, width):
    old_v = old[...]
    size = old_v.shape[0]
    pooled = lax.dot_general(
        parts(mid[...]), spread[...], (((1,), (1,)), ((), ())), preferred_element_type=F32
    )
    rest = 0.25 * (pooled[:size] + pooled[size:]) - 0.5 * (old_v + new[...])
    lanes = old_v.shape[1]
    lane = lax.broadcasted_iota(jnp.int32, (1, lanes), 1)
    at = (lane // (width * width), lane // width % width, lane % width)
    step = (width * width, width, 1)
    inner = [(a >= 1) & (a <= width - 2) for a in at]
    result = jnp.zeros_like(old_v)
    for axis in range(3):
        sides = inner[(axis + 1) % 3] & inner[(axis + 2) % 3]
        for edge_at, shift in ((0, lanes - step[axis]), (width - 1, step[axis])):
            mask = sides & (at[axis] == edge_at)
            result = jnp.where(mask, rest - pltpu.roll(old_v, shift, 1), result)
    return diffs * result


def delta_of(field, kept, mid, old, new, spread, coef, average, place, half, stack):
    boxes = field.shape[0] // stack
    diffs = jnp.concatenate([column(coef, stack)] * boxes, axis=0)
    halo = dot(by_box(kept[...], boxes, half).astype(BF16), place[...].astype(BF16))
    means = rows_dot(field[...], average[...].astype(BF16))
    fix = fix_of(mid, old, new, spread, diffs, half + 2)
    return fix - 0.5 * diffs * diffs * halo + means


def correct_kernel(
    pos,
    adv,
    x_first,
    x_second,
    near,
    far,
    coef,
    field,
    kept,
    mid,
    old,
    new,
    spread,
    average,
    place,
    out,
    block,
    wide,
    sems,
    half,
):
    count, stack, nz = adv.shape
    species = block.shape[2]
    width = half + 2
    delta = delta_of(field, kept, mid, old, new, spread, coef, average, place, half, stack)
    diff = column(coef, stack)
    even = lax.axis_index("yz") % 2 == 0
    rows = x_first.shape[0]
    near_v, far_v = near[:rows].astype(F32), far[:rows].astype(F32)
    wide[0, :rows] = x_first[...].astype(F32)
    wide[1, : x_second.shape[0]] = x_second[...].astype(F32)
    wide[2, :rows] = jnp.where(even, far_v, near_v)
    wide[3, :rows] = jnp.where(even, near_v, far_v)
    boxes = delta.shape[0] // stack
    starts = [pos[0, i] * width for i in range(boxes)]
    cycle = [tiles_of(stack, nz, start, width) for start in starts]
    inside = [tiles_of(stack, nz, start + 1, half) for start in starts]
    lane = lanes_of(stack)
    copies = []
    for k in range(count):
        x, y = k // width, k % width
        value = adv[k]
        for there, at, n in (
            (x == 0, y, 0),
            (x == width - 1, y, 1),
            (y == 0, x, 2),
            (y == width - 1, x, 3),
        ):
            if there:
                value = value + diff * wide[n, at * species : at * species + stack]
        if x not in (0, width - 1) or y not in (0, width - 1):
            tiles = [value[:, t * 128 : (t + 1) * 128] for t in range(nz // 128)]
            covers = 0 < x < width - 1 and 0 < y < width - 1
            for i in range(boxes):
                mine = delta[i * stack : (i + 1) * stack]
                t = k * width // 128
                part = mine[:, t * 128 : (t + 1) * 128]
                if (k + 1) * width > (t + 1) * 128:
                    after = mine[:, (t + 1) * 128 : (t + 2) * 128]
                    part = jnp.where(lane < (k + 1) * width - (t + 1) * 128, after, part)
                moved = turn(part, starts[i] - k * width)
                for t in range(nz // 128):
                    if covers:
                        tiles[t] = jnp.where(inside[i][t], 0.0, tiles[t])
                    tiles[t] = tiles[t] + jnp.where(cycle[i][t], moved, 0.0)
            value = jnp.concatenate(tiles, axis=1)
        block[x, y] = value[:species]
        if y == width - 1:
            copies.append(pltpu.make_async_copy(block.at[x], out.at[x], sems.at[x]))
            copies[-1].start()
    for copy in copies:
        copy.wait()


def correct(pos, adv, halos, coef, field, kept, mid, old, new, spread, table, half):
    _, stack, nz = adv.shape
    width = half + 2
    species = coef.shape[1]
    vmem = pl.BlockSpec(memory_space=pltpu.VMEM)
    return pl.pallas_call(
        functools.partial(correct_kernel, half=half),
        in_specs=[vmem] * 15,
        out_specs=pl.BlockSpec(memory_space=pltpu.HBM),
        out_shape=jax.ShapeDtypeStruct((width, width, species, nz), F32),
        scratch_shapes=[
            pltpu.VMEM((width, width, species, nz), F32),
            pltpu.VMEM((4, halos[0].shape[0] + stack, nz), F32),
            pltpu.SemaphoreType.DMA((width,)),
        ],
        compiler_params=pltpu.CompilerParams(vmem_limit_bytes=LIMIT),
        cost_estimate=pl.CostEstimate(
            flops=20 * adv.size, bytes_accessed=12 * adv.size, transcendentals=0
        ),
        name="coarse_correct",
    )(
        pos,
        adv,
        *halos,
        coef,
        field,
        kept,
        mid,
        old,
        new,
        spread,
        jnp.asarray(table["average"]),
        jnp.asarray(table["place"]),
    )


def return_order(count):
    return [0, 2, 3, 1] if count == 4 else list(range(count))


def unpack_kernel(*refs):
    packets, (out, rows) = refs[:-2], refs[-2:]
    species, cells = packets[0].shape
    count = len(packets)
    step = rows.shape[1] // padded(species, 8)
    me = lax.axis_index("yz")
    for k, packet in zip(return_order(count), packets):
        source = origin(me, k, count)
        value = packet[...].astype(F32)
        for q in range(cells // 128):
            rows[q, pl.ds(source, species, stride=step), :] = value[:, q * 128 : (q + 1) * 128]
    for s in range(species):
        pieces = [rows[q, s * step : s * step + count] for q in range(cells // 128)]
        out[s] = jnp.concatenate(pieces, axis=1).astype(BF16)


def unpack(packets):
    species, cells = packets[0].shape
    count = len(packets)
    vmem = pl.BlockSpec(memory_space=pltpu.VMEM)
    rows = padded(species, 8) * padded(count, 8)
    return pl.pallas_call(
        unpack_kernel,
        in_specs=[vmem] * count,
        out_specs=vmem,
        out_shape=jax.ShapeDtypeStruct((species, count, cells), BF16),
        scratch_shapes=[pltpu.VMEM((cells // 128, rows, 128), F32)],
        compiler_params=pltpu.CompilerParams(vmem_limit_bytes=LIMIT),
        name="unpack",
    )(*[packets[k] for k in return_order(count)])


def ring(axis, by):
    count = lax.axis_size(axis)
    return [(i, (i + by) % count) for i in range(count)]


def mutual(axis, by):
    count = lax.axis_size(axis)
    one_way = [(i, (i + by) % count) for i in range(0, count, 2)]
    return one_way + [(j, i) for i, j in one_way]


def partner(me, k, count):
    return me ^ k if count & (count - 1) == 0 else lax.rem(me + k, count)


def origin(me, source, count):
    return me ^ source if count & (count - 1) == 0 else lax.rem(me - source + count, count)


def local(coarse_state, fine_state, diffusion, rate, box_pos, box_owner):
    species, width = coarse_state.shape[:2]
    half = width - 2
    stack = padded(species, 8)
    count = lax.axis_size("yz")
    me = lax.axis_index("yz")
    pos, owner = box_pos[0], box_owner[0]
    table = tables(width, pos.shape[1])
    coef = diffusion[None]
    c = jnp.transpose(coarse_state, (1, 2, 0, 3))

    fine = jnp.transpose(fine_state, (1, 0, 2))
    near, far, own, *others = pack_y(c, fine)
    x_high = pack_x(c, own, c.shape[0] - 1)
    x_low = pack_x(c, x_high, 0)
    halos = [
        lax.ppermute(x_high, "gx", ring("gx", 1)),
        lax.ppermute(x_low, "gx", ring("gx", -1)),
        lax.ppermute(near, "yz", mutual("yz", 1)),
        lax.ppermute(far, "yz", mutual("yz", -1)),
    ]
    if relays(count):
        after = passed = relay(halos[2], x_low, width, *own.shape)
        others = [lax.ppermute(passed, "yz", mutual("yz", -1))]
    else:
        after = x_low
        others = [lax.ppermute(slot, "yz", ring("yz", 2 + k)) for k, slot in enumerate(others)]

    adv, old, new, mix, spread, ghost = coarse_part(
        pos, c, rate, coef, table, stack, after
    )
    from_y, start, ghosts = y_faces(
        pos, owner, *halos[2:], halos[0], own, old, new, spread, half, stack
    )
    made = fine_part(
        pos, owner, halos[1], start, others, mix, coef, ghosts, ghost, from_y, 2 * half
    )
    packets, (mid, kept, field) = made[:count], made[count:]

    def swap(value, k):
        even = count & (count - 1) == 0
        pairs = [(i, i ^ k if even else (i + k) % count) for i in range(count)]
        return lax.ppermute(value, "yz", pairs)

    back = [packets[0]] + [swap(packets[k], k) for k in range(1, count)]
    coarse_next = correct(pos, adv, halos, coef, field, kept, mid, old, new, spread, table, half)

    fine_next = jnp.transpose(unpack(back), (1, 0, 2))
    return jnp.transpose(coarse_next, (2, 0, 1, 3)), fine_next


def solution(mesh):
    in_specs = (
        P(None, "gx", "yz", None),
        P(("gx", "yz"), None, None),
        P(),
        P(),
        P("gx", "yz", None),
        P("gx", "yz", None),
    )
    out_specs = (P(None, "gx", "yz", None), P(("gx", "yz"), None, None))
    return jax.shard_map(local, mesh=mesh, in_specs=in_specs, out_specs=out_specs, check_vma=False)
```

```python
import functools

import jax
import jax.numpy as jnp
import numpy as np
from jax import lax
from jax.experimental import pallas as pl
from jax.experimental.pallas import tpu as pltpu
from jax.sharding import PartitionSpec as P

F32 = jnp.float32
BF16 = jnp.bfloat16
LIMIT = 12 * 1024 * 1024
PATCH = 256
ORDER = 20_000_000


def padded(count, unit):
    return -(-count // unit) * unit


@functools.lru_cache(maxsize=None)
def tables(width, boxes):
    half = width - 2
    edge = 2 * half
    cells = width**3
    lanes = padded(cells, PATCH)
    fine = edge**3
    spread = np.zeros((lanes, fine), np.float32)
    average = np.zeros((fine, lanes), np.float32)
    halo = padded(boxes * 4 * half * half, 128)
    place = np.zeros((halo, lanes), np.float32)

    def cell(x, y, z):
        return (x * width + y) * width + z

    for number in range(6):
        axis, high = divmod(number, 2)
        others = [a for a in range(3) if a != axis]
        for r in range(half):
            for q in range(half):
                at = [0, 0, 0]
                at[axis] = width - 1 if high else 0
                at[others[0]] = r + 1
                at[others[1]] = q + 1
                here = cell(*at)
                for i in range(2):
                    for j in range(2):
                        pos = [0, 0, 0]
                        pos[axis] = edge - 1 if high else 0
                        pos[others[0]] = 2 * r + i
                        pos[others[1]] = 2 * q + j
                        spread[here, (pos[0] * edge + pos[1]) * edge + pos[2]] = 1.0
                if number < 4:
                    for box in range(boxes):
                        place[((box * 4 + number) * half + r) * half + q, here] = 1.0
    for x in range(edge):
        for y in range(edge):
            for z in range(edge):
                average[(x * edge + y) * edge + z, cell(x // 2 + 1, y // 2 + 1, z // 2 + 1)] = 0.125
    return dict(spread=spread, average=average, place=place, ghost=place @ spread)


def column(diffusion, stack):
    species = diffusion.shape[1]
    row = lax.broadcasted_iota(jnp.int32, (stack, species), 0)
    lane = lax.broadcasted_iota(jnp.int32, (stack, species), 1)
    return jnp.sum(jnp.where(row == lane, diffusion[...], 0.0), axis=1, keepdims=True)


def split(value):
    high = value.astype(BF16).astype(F32)
    return high, value - high


def parts(value):
    return jnp.concatenate(split(value), axis=0).astype(BF16)


def dot(a, b):
    return jnp.dot(a, b, preferred_element_type=F32)


def rows_dot(value, table):
    rows = value.shape[0]
    both = dot(parts(value), table)
    return both[:rows] + both[rows:]


GROUP = 5


def mixing(rate, scratch, stack, group):
    species = rate.shape[0]
    size = group * stack
    scratch[...] = jnp.zeros_like(scratch)
    high, low = split(rate[...])
    for b in range(group):
        at = b * stack
        for row, lane, part in ((at, at, high), (at, size + at, high), (size + at, at, low)):
            scratch[row : row + species, lane : lane + species] = part
    return scratch[: 2 * size, : 2 * size].astype(BF16)


def react(mix, fields):
    size = fields.shape[0]
    both = dot(mix, parts(fields))
    return both[:size] + both[size:]


def react_all(mix, fields):
    stack, depth = fields[0].shape
    made = [[] for _ in fields]

    def product(blocks):
        size = len(blocks[0])
        blank = [jnp.zeros_like(blocks[0][0])] * (GROUP - size)
        columns = [jnp.concatenate(block + blank, axis=0) for block in blocks]
        out = react(mix, jnp.concatenate(columns, axis=1))
        lanes = out.shape[1] // len(blocks)
        return [
            [out[b * stack : (b + 1) * stack, n * lanes : (n + 1) * lanes] for b in range(size)]
            for n in range(len(blocks))
        ]

    for lane in range(0, depth, 256):
        if lane + 256 <= depth:
            for at in range(0, len(fields), GROUP):
                block = [f[:, lane : lane + 256] for f in fields[at : at + GROUP]]
                for b, value in enumerate(product([block])[0]):
                    made[at + b].append(value)
        else:
            half = -(-len(fields) // 2)
            blocks = [[f[:, lane:] for f in part] for part in (fields[:half], fields[half:])]
            blocks[1] += [jnp.zeros_like(blocks[0][0])] * (half - len(blocks[1]))
            for n, values in enumerate(product(blocks)):
                for b, value in enumerate(values):
                    if n * half + b < len(fields):
                        made[n * half + b].append(value)
    return [jnp.concatenate(value, axis=1) for value in made]


def lanes_of(stack, lanes=128):
    return lax.broadcasted_iota(jnp.int32, (stack, lanes), 1)


def tiles_of(stack, depth, start, width):
    lane = lanes_of(stack)
    masks = []
    for t in range(depth // 128):
        along = lane + (t * 128 - start)
        masks.append((along >= 0) & (along < width))
    return masks


def fold(value, masks):
    out = value[:, :128]
    for t in range(1, len(masks)):
        out = jnp.where(masks[t], value[:, t * 128 : (t + 1) * 128], out)
    return out


def turn(value, by):
    return pltpu.roll(value, by & 127, 1)


def neighbour(me, count, even_up):
    step = jnp.where((me % 2 == 0) == even_up, 1, count - 1)
    return lax.rem(me + step, count)


def layer_rows(width, species, groups=0):
    return padded((width + groups) * species, 16)


def blocks_of(width, species, nz, pieces, slot=0):
    across = nz // 128
    numbers = range(slot * pieces, (slot + 1) * pieces)
    return [((width + n // across) * species, n % across * 128) for n in numbers]


def pack_layer(columns, tmp, species):
    for r, value in enumerate(columns):
        tmp[r * species : (r + 1) * species] = value
    below = len(columns) * species
    tmp[below:] = jnp.zeros((tmp.shape[0] - below, tmp.shape[1]), F32)


def pack_y_kernel(c, fine, near, far, own, *refs):
    others, (layer, tmp, held, rows, sems, fine_sem) = refs[:-6], refs[-6:]
    nx, ny, species, nz = c.shape
    count = fine.shape[1]
    stack = padded(species, 8)
    me = lax.axis_index("yz")
    slots = pltpu.make_async_copy(fine, held, fine_sem)
    slots.start()
    copies = []
    for n, y in enumerate((jnp.where(me % 2 == 0, ny - 1, 0), jnp.where(me % 2 == 0, 0, ny - 1))):
        copies.append(pltpu.make_async_copy(c.at[:, y], layer.at[n], sems.at[n]))
        copies[-1].start()
    slots.wait()
    step = rows.shape[1] // stack
    pieces = rows.shape[0]
    for s in range(species):
        value = held[s].astype(F32)
        for q in range(pieces):
            rows[q, s * step : s * step + count] = value[:, q * 128 : (q + 1) * 128]

    def slot(at):
        return [rows[q, pl.ds(at, species, stride=step), :] for q in range(pieces)]

    own[...] = jnp.concatenate(slot(me), axis=1).astype(BF16)
    for k, out in enumerate(others):
        out[...] = jnp.concatenate(slot(lax.rem(me + 2 + k, count)), axis=1).astype(BF16)
    for n, out in enumerate((far, near)):
        n = 1 - n
        copies[n].wait()
        pack_layer([layer[n, r] for r in range(nx)], tmp, species)
        sent = [slot(neighbour(me, count, n == 0))]
        if n == 0 and relays(count):
            sent.append(slot(lax.rem(me + 2, count)))
        for m, value in enumerate(sent):
            for (row, lane), piece in zip(blocks_of(nx, species, nz, pieces, m), value):
                tmp[row : row + species, lane : lane + 128] = piece
        out[...] = tmp[: out.shape[0]].astype(BF16)


def pack_y(c, fine):
    nx, ny, species, nz = c.shape
    count, cells = fine.shape[1:]
    stack = padded(species, 8)
    vmem = pl.BlockSpec(memory_space=pltpu.VMEM)
    far_rows = layer_rows(nx, species, -(-cells // nz))
    rows = layer_rows(nx, species, -(-2 * cells // nz)) if relays(count) else far_rows
    outs = [jax.ShapeDtypeStruct((n, nz), BF16) for n in (rows, far_rows)]
    direct = 0 if relays(count) else max(count - 3, 0)
    outs += [jax.ShapeDtypeStruct((species, cells), BF16)] * (1 + direct)
    return pl.pallas_call(
        pack_y_kernel,
        in_specs=[pl.BlockSpec(memory_space=pltpu.HBM)] * 2,
        out_specs=[vmem] * len(outs),
        out_shape=outs,
        scratch_shapes=[
            pltpu.VMEM((2, nx, species, nz), F32),
            pltpu.VMEM((rows, nz), F32),
            pltpu.VMEM(fine.shape, BF16),
            pltpu.VMEM((cells // 128, stack * padded(count, 8), 128), F32),
            pltpu.SemaphoreType.DMA((2,)),
            pltpu.SemaphoreType.DMA,
        ],
        compiler_params=pltpu.CompilerParams(vmem_limit_bytes=LIMIT),
        name="pack_y",
    )(
        pltpu.with_memory_space_constraint(c, pltpu.HBM),
        pltpu.with_memory_space_constraint(fine, pltpu.HBM),
    )


def relays(count):
    return count == 4


def relay_kernel(near, after, out, wide, width):
    species, cells = out.shape
    wide[...] = near[...].astype(F32)
    places = blocks_of(width, species, near.shape[1], cells // 128, 1)
    pieces = [wide[row : row + species, lane : lane + 128] for row, lane in places]
    out[...] = jnp.concatenate(pieces, axis=1).astype(BF16)


def relay(near, after, width, species, cells):
    vmem = pl.BlockSpec(memory_space=pltpu.VMEM)
    return pl.pallas_call(
        functools.partial(relay_kernel, width=width),
        in_specs=[vmem, pl.BlockSpec(memory_space=pl.ANY)],
        out_specs=vmem,
        out_shape=jax.ShapeDtypeStruct((species, cells), BF16),
        scratch_shapes=[pltpu.VMEM(near.shape, F32)],
        compiler_params=pltpu.CompilerParams(vmem_limit_bytes=LIMIT),
        name="relay",
    )(near, after)


def pack_x_kernel(c, after, out, tmp, x):
    nx, ny, species, _ = c.shape
    pack_layer([c[x, r] for r in range(ny)], tmp, species)
    out[...] = tmp[...].astype(BF16)


def pack_x(c, after, x):
    nx, ny, species, nz = c.shape
    vmem = pl.BlockSpec(memory_space=pltpu.VMEM)
    shape = (layer_rows(ny, species), nz)
    return pl.pallas_call(
        functools.partial(pack_x_kernel, x=x),
        in_specs=[vmem, pl.BlockSpec(memory_space=pl.ANY)],
        out_specs=vmem,
        out_shape=jax.ShapeDtypeStruct(shape, BF16),
        scratch_shapes=[pltpu.VMEM(shape, F32)],
        compiler_params=pltpu.CompilerParams(vmem_limit_bytes=LIMIT),
        name="pack_x",
    )(c, after)


def coarse_kernel(
    pos, c, rate, coef, spread, ghost, after, adv, old, new, mix, spread16, ghost16, columns, scratch
):
    count, stack, nz = adv.shape
    boxes = pos.shape[1]
    width = c.shape[0]
    mix[...] = mixing(rate, scratch, stack, 2)
    mixed = mixing(rate, scratch, stack, GROUP)
    spread16[...] = spread[...].astype(BF16)
    ghost16[...] = ghost[...].astype(BF16)
    for k in range(count):
        columns[k, c.shape[2] :] = jnp.zeros((stack - c.shape[2], nz), F32)
        columns[k, : c.shape[2]] = c[k // width, k % width]
    diff = column(coef, stack)
    for first in range(0, count, 2 * GROUP):
        some = range(first, min(first + 2 * GROUP, count))
        made = react_all(mixed, [columns[k] for k in some])
        for k in some:
            x, y = k // width, k % width
            mine = columns[k]
            lap = pltpu.roll(mine, 1, 1) + pltpu.roll(mine, nz - 1, 1) - 6.0 * mine
            if x > 0:
                lap = lap + columns[k - width]
            if x < width - 1:
                lap = lap + columns[k + width]
            if y > 0:
                lap = lap + columns[k - 1]
            if y < width - 1:
                lap = lap + columns[k + 1]
            value = mine + diff * lap + made[k - first]
            adv[k] = value
    lanes = old.shape[1]
    cell = lanes_of(stack, lanes) // width
    for i in range(boxes):
        lane = pos[0, i] * width
        start = pl.multiple_of(jnp.minimum(lane // 128, nz // 128 - 2) * 128, 128)
        offset = lane - start
        for source, out in ((columns, old), (adv, new)):
            total = jnp.zeros((stack, lanes), F32)
            for k in range(count):
                if k // width in (0, width - 1) and k % width in (0, width - 1):
                    continue
                part = source[k, :, pl.ds(start, PATCH)]
                moved = pltpu.roll(part, (k * width - offset) & (PATCH - 1), 1)
                total = jnp.where(cell == k, moved, total)
            out[i * stack : (i + 1) * stack] = total


def coarse_part(pos, c, rate, coef, table, stack, after):
    nx, ny, species, nz = c.shape
    boxes = pos.shape[1]
    lanes = padded(nx**3, PATCH)
    vmem = pl.BlockSpec(memory_space=pltpu.VMEM)
    small = jax.ShapeDtypeStruct((boxes * stack, lanes), F32)
    size = padded(2 * GROUP * stack, 128)
    return pl.pallas_call(
        coarse_kernel,
        in_specs=[vmem] * 6 + [pl.BlockSpec(memory_space=pl.ANY)],
        out_specs=[vmem] * 6,
        out_shape=[
            jax.ShapeDtypeStruct((nx * ny, stack, nz), F32),
            small,
            small,
            jax.ShapeDtypeStruct((4 * stack, 4 * stack), BF16),
            jax.ShapeDtypeStruct(table["spread"].shape, BF16),
            jax.ShapeDtypeStruct(table["ghost"].shape, BF16),
        ],
        scratch_shapes=[
            pltpu.VMEM((nx * ny, stack, nz), F32),
            pltpu.VMEM((size, size), F32),
        ],
        compiler_params=pltpu.CompilerParams(vmem_limit_bytes=LIMIT),
        cost_estimate=pl.CostEstimate(
            flops=800 * c.size, bytes_accessed=12 * c.size, transcendentals=0
        ),
        name="coarse_part",
    )(pos, c, rate, coef, jnp.asarray(table["spread"]), jnp.asarray(table["ghost"]), after)


def by_box(total, boxes, half):
    each = 4 * half * half
    lane = lax.broadcasted_iota(jnp.int32, total.shape, 1)
    rows = [
        jnp.where((lane >= i * each) & (lane < (i + 1) * each), total, 0.0) for i in range(boxes)
    ]
    return jnp.concatenate(rows, axis=0)


def gather_faces(pos, layers, faces, half, stack, species, nz, total):
    lane = lanes_of(stack)
    for ref, face in zip(layers, faces):
        for i in range(pos.shape[1]):
            start = pos[0, i] * (half + 2) + 1
            masks = tiles_of(stack, nz, start, half)
            for r in range(half):
                base = ((i * 4 + face) * half + r) * half
                at = (r + 1) * species
                moved = turn(fold(ref[at : at + stack], masks), base - start)
                tiles = []
                for t in range(total.shape[1] // 128):
                    along = lane + (t * 128 - base)
                    here = (along >= 0) & (along < half)
                    tiles.append(jnp.where(here, moved, total[:, t * 128 : (t + 1) * 128]))
                total = tiles[0] if len(tiles) == 1 else jnp.concatenate(tiles, axis=1)
    return total


def y_faces_kernel(pos, owner, near, far, own, old, new, spread, from_y, start, ghosts, wide):
    stack = from_y.shape[0]
    species, cells = own.shape
    nz = near.shape[1]
    boxes = pos.shape[1]
    width = far.shape[0] // species - -(-cells // nz)
    half = width - 2
    wide[0] = near[...].astype(F32)
    wide[1, : far.shape[0]] = far[...].astype(F32)
    me, count = lax.axis_index("yz"), lax.axis_size("yz")
    odd = me % 2
    zero = jnp.zeros(from_y.shape, F32)
    layers = (wide.at[0], wide.at[1])
    from_y[...] = gather_faces(pos, layers, (3 - odd, 2 + odd), half, stack, species, nz, zero)
    old_v = old[...]
    ghosts[...] = rows_dot(jnp.concatenate([old_v, old_v + new[...]], axis=0), spread[...])
    direct = own[...].astype(F32)
    places = blocks_of(width, species, nz, cells // 128)
    edge = species // 8 * 8
    for i in range(boxes):
        by_near = owner[0, i] == neighbour(me, count, True)
        by_far = owner[0, i] == neighbour(me, count, False)
        at = i * stack
        start[at + edge : at + stack] = jnp.zeros((stack - edge, cells), F32)
        for q, (row, lane) in enumerate(places):
            part = direct[:, q * 128 : (q + 1) * 128]
            sent = [wide[n, row : row + species, lane : lane + 128] for n in range(2)]
            part = jnp.where(by_far, sent[1], jnp.where(by_near, sent[0], part))
            start[at : at + species, q * 128 : (q + 1) * 128] = part


def y_faces(pos, owner, near, far, own, old, new, spread, half, stack):
    vmem = pl.BlockSpec(memory_space=pltpu.VMEM)
    boxes = pos.shape[1]
    lanes = padded(boxes * 4 * half * half, 128)
    return pl.pallas_call(
        y_faces_kernel,
        in_specs=[vmem] * 8,
        out_specs=[vmem] * 3,
        out_shape=[
            jax.ShapeDtypeStruct((stack, lanes), F32),
            jax.ShapeDtypeStruct((boxes * stack, own.shape[1]), F32),
            jax.ShapeDtypeStruct((2 * boxes * stack, own.shape[1]), F32),
        ],
        scratch_shapes=[pltpu.VMEM((2, *near.shape), F32)],
        compiler_params=pltpu.CompilerParams(vmem_limit_bytes=LIMIT),
        cost_estimate=pl.CostEstimate(flops=10**9, bytes_accessed=ORDER, transcendentals=0),
        name="y_faces",
    )(pos, owner, near, far, own, old, new, spread)


def fine_kernel(pos, owner, x_low, x_high, start, *refs, count, edge):
    others, refs = refs[: count - 3], refs[count - 3 :]
    mix, coef, ghosts, ghost, from_y = refs[:5]
    packets = refs[5 : 5 + count]
    mid, kept, final, field, wide = refs[5 + count :]
    species = packets[0].shape[0]
    stack = from_y.shape[0]
    boxes = final.shape[0] // stack
    cells = final.shape[1]
    me = lax.axis_index("yz")
    mixed = mix[...]

    def reaction(value):
        pairs = [value[at : at + 2 * stack] for at in range(0, boxes * stack, 2 * stack)]
        return jnp.concatenate([react(mixed, pair) for pair in pairs], axis=0)

    nz = x_low.shape[1]
    half = edge // 2
    wide[0, : x_low.shape[0]] = x_low[...].astype(F32)
    wide[1, : x_high.shape[0]] = x_high[...].astype(F32)
    sent = [ref[...].astype(F32) for ref in others]
    for i in range(boxes):
        at = i * stack
        field[at : at + stack] = start[at : at + stack]
        back = lax.rem(me - owner[0, i] + count, count)
        value = start[at : at + species]
        for k in range(len(sent)):
            value = jnp.where(back == k + 2, sent[k], value)
        field[at : at + species] = value
    diff = jnp.concatenate([column(coef, stack)] * boxes, axis=0)
    ghost0, ghost1 = ghosts[: boxes * stack], ghosts[boxes * stack :]
    index = lax.broadcasted_iota(jnp.int32, (1, cells), 1)
    at = (index // (edge * edge), index // edge % edge, index % edge)
    step = (edge * edge, edge, 1)

    def inside(value):
        lap = -6.0 * value
        for axis in range(3):
            before = pltpu.roll(value, step[axis], 1)
            after = pltpu.roll(value, cells - step[axis], 1)
            lap = lap + jnp.where(at[axis] == 0, 0.0, before)
            lap = lap + jnp.where(at[axis] == edge - 1, 0.0, after)
        return lap

    first = field[...]
    second = first + 2.0 * diff * (inside(first) + ghost0) + 0.5 * reaction(first)
    base = second + diff * (2.0 * inside(second) + ghost1) + 0.5 * reaction(second)
    layers = (wide.at[0], wide.at[1])
    total = gather_faces(pos, layers, (0, 1), half, stack, species, nz, from_y[...])
    kept[...] = total
    stacked = by_box(total, boxes, half).astype(BF16)
    value = base + diff * diff * dot(stacked, ghost[...])
    final[...] = value
    for k, out in enumerate(packets):
        dest = partner(me, k, count)
        packet = jnp.zeros((species, cells), F32)
        for i in range(boxes):
            packet = jnp.where(owner[0, i] == dest, value[i * stack : i * stack + species], packet)
        out[...] = packet.astype(BF16)
    mid[...] = first + second


def fine_part(pos, owner, low, high, start, others, mix, coef, ghosts, ghost, from_y, edge):
    boxes = owner.shape[1]
    count = len(others) + 3
    stack = from_y.shape[0]
    cells = start.shape[1]
    vmem = pl.BlockSpec(memory_space=pltpu.VMEM)
    return pl.pallas_call(
        functools.partial(fine_kernel, count=count, edge=edge),
        in_specs=[vmem] * (count + 7),
        out_specs=[vmem] * (count + 3),
        out_shape=[jax.ShapeDtypeStruct((coef.shape[1], cells), BF16)] * count
        + [
            jax.ShapeDtypeStruct((boxes * stack, cells), F32),
            jax.ShapeDtypeStruct(from_y.shape, F32),
            jax.ShapeDtypeStruct((boxes * stack, cells), F32),
        ],
        scratch_shapes=[
            pltpu.VMEM((boxes * stack, cells), F32),
            pltpu.VMEM((2, *low.shape), F32),
        ],
        compiler_params=pltpu.CompilerParams(vmem_limit_bytes=LIMIT),
        name="fine_part",
    )(pos, owner, low, high, start, *others, mix, coef, ghosts, ghost, from_y)


def fix_of(mid, old, new, spread, diffs, width):
    old_v = old[...]
    size = old_v.shape[0]
    pooled = lax.dot_general(
        parts(mid[...]), spread[...], (((1,), (1,)), ((), ())), preferred_element_type=F32
    )
    rest = 0.25 * (pooled[:size] + pooled[size:]) - 0.5 * (old_v + new[...])
    lanes = old_v.shape[1]
    lane = lax.broadcasted_iota(jnp.int32, (1, lanes), 1)
    at = (lane // (width * width), lane // width % width, lane % width)
    step = (width * width, width, 1)
    inner = [(a >= 1) & (a <= width - 2) for a in at]
    result = jnp.zeros_like(old_v)
    for axis in range(3):
        sides = inner[(axis + 1) % 3] & inner[(axis + 2) % 3]
        for edge_at, shift in ((0, lanes - step[axis]), (width - 1, step[axis])):
            mask = sides & (at[axis] == edge_at)
            result = jnp.where(mask, rest - pltpu.roll(old_v, shift, 1), result)
    return diffs * result


def delta_of(field, kept, mid, old, new, spread, coef, average, place, half, stack):
    boxes = field.shape[0] // stack
    diffs = jnp.concatenate([column(coef, stack)] * boxes, axis=0)
    halo = dot(by_box(kept[...], boxes, half).astype(BF16), place[...].astype(BF16))
    means = rows_dot(field[...], average[...].astype(BF16))
    fix = fix_of(mid, old, new, spread, diffs, half + 2)
    return fix - 0.5 * diffs * diffs * halo + means


def correct_kernel(
    pos,
    adv,
    x_first,
    x_second,
    near,
    far,
    coef,
    field,
    kept,
    mid,
    old,
    new,
    spread,
    average,
    place,
    out,
    block,
    wide,
    sems,
    half,
):
    count, stack, nz = adv.shape
    species = block.shape[2]
    width = half + 2
    delta = delta_of(field, kept, mid, old, new, spread, coef, average, place, half, stack)
    diff = column(coef, stack)
    even = lax.axis_index("yz") % 2 == 0
    rows = x_first.shape[0]
    near_v, far_v = near[:rows].astype(F32), far[:rows].astype(F32)
    wide[0, :rows] = x_first[...].astype(F32)
    wide[1, : x_second.shape[0]] = x_second[...].astype(F32)
    wide[2, :rows] = jnp.where(even, far_v, near_v)
    wide[3, :rows] = jnp.where(even, near_v, far_v)
    boxes = delta.shape[0] // stack
    starts = [pos[0, i] * width for i in range(boxes)]
    cycle = [tiles_of(stack, nz, start, width) for start in starts]
    inside = [tiles_of(stack, nz, start + 1, half) for start in starts]
    lane = lanes_of(stack)
    copies = []
    for k in range(count):
        x, y = k // width, k % width
        value = adv[k]
        for there, at, n in (
            (x == 0, y, 0),
            (x == width - 1, y, 1),
            (y == 0, x, 2),
            (y == width - 1, x, 3),
        ):
            if there:
                value = value + diff * wide[n, at * species : at * species + stack]
        if x not in (0, width - 1) or y not in (0, width - 1):
            tiles = [value[:, t * 128 : (t + 1) * 128] for t in range(nz // 128)]
            covers = 0 < x < width - 1 and 0 < y < width - 1
            for i in range(boxes):
                mine = delta[i * stack : (i + 1) * stack]
                t = k * width // 128
                part = mine[:, t * 128 : (t + 1) * 128]
                if (k + 1) * width > (t + 1) * 128:
                    after = mine[:, (t + 1) * 128 : (t + 2) * 128]
                    part = jnp.where(lane < (k + 1) * width - (t + 1) * 128, after, part)
                moved = turn(part, starts[i] - k * width)
                for t in range(nz // 128):
                    if covers:
                        tiles[t] = jnp.where(inside[i][t], 0.0, tiles[t])
                    tiles[t] = tiles[t] + jnp.where(cycle[i][t], moved, 0.0)
            value = jnp.concatenate(tiles, axis=1)
        block[x, y] = value[:species]
        if y == width - 1:
            copies.append(pltpu.make_async_copy(block.at[x], out.at[x], sems.at[x]))
            copies[-1].start()
    for copy in copies:
        copy.wait()


def correct(pos, adv, halos, coef, field, kept, mid, old, new, spread, table, half):
    _, stack, nz = adv.shape
    width = half + 2
    species = coef.shape[1]
    vmem = pl.BlockSpec(memory_space=pltpu.VMEM)
    return pl.pallas_call(
        functools.partial(correct_kernel, half=half),
        in_specs=[vmem] * 15,
        out_specs=pl.BlockSpec(memory_space=pltpu.HBM),
        out_shape=jax.ShapeDtypeStruct((width, width, species, nz), F32),
        scratch_shapes=[
            pltpu.VMEM((width, width, species, nz), F32),
            pltpu.VMEM((4, halos[0].shape[0] + stack, nz), F32),
            pltpu.SemaphoreType.DMA((width,)),
        ],
        compiler_params=pltpu.CompilerParams(vmem_limit_bytes=LIMIT),
        cost_estimate=pl.CostEstimate(
            flops=20 * adv.size, bytes_accessed=12 * adv.size, transcendentals=0
        ),
        name="coarse_correct",
    )(
        pos,
        adv,
        *halos,
        coef,
        field,
        kept,
        mid,
        old,
        new,
        spread,
        jnp.asarray(table["average"]),
        jnp.asarray(table["place"]),
    )


def return_order(count):
    return [0, 2, 1, 3] if count == 4 else list(range(count))


def unpack_kernel(*refs):
    packets, (out, rows) = refs[:-2], refs[-2:]
    species, cells = packets[0].shape
    count = len(packets)
    step = rows.shape[1] // padded(species, 8)
    me = lax.axis_index("yz")
    for k, packet in zip(return_order(count), packets):
        source = origin(me, k, count)
        value = packet[...].astype(F32)
        for q in range(cells // 128):
            rows[q, pl.ds(source, species, stride=step), :] = value[:, q * 128 : (q + 1) * 128]
    for s in range(species):
        pieces = [rows[q, s * step : s * step + count] for q in range(cells // 128)]
        out[s] = jnp.concatenate(pieces, axis=1).astype(BF16)


def unpack(packets):
    species, cells = packets[0].shape
    count = len(packets)
    vmem = pl.BlockSpec(memory_space=pltpu.VMEM)
    rows = padded(species, 8) * padded(count, 8)
    return pl.pallas_call(
        unpack_kernel,
        in_specs=[vmem] * count,
        out_specs=vmem,
        out_shape=jax.ShapeDtypeStruct((species, count, cells), BF16),
        scratch_shapes=[pltpu.VMEM((cells // 128, rows, 128), F32)],
        compiler_params=pltpu.CompilerParams(vmem_limit_bytes=LIMIT),
        name="unpack",
    )(*[packets[k] for k in return_order(count)])


def ring(axis, by):
    count = lax.axis_size(axis)
    return [(i, (i + by) % count) for i in range(count)]


def mutual(axis, by):
    count = lax.axis_size(axis)
    one_way = [(i, (i + by) % count) for i in range(0, count, 2)]
    return one_way + [(j, i) for i, j in one_way]


def partner(me, k, count):
    return me ^ k if count & (count - 1) == 0 else lax.rem(me + k, count)


def origin(me, source, count):
    return me ^ source if count & (count - 1) == 0 else lax.rem(me - source + count, count)


def local(coarse_state, fine_state, diffusion, rate, box_pos, box_owner):
    species, width = coarse_state.shape[:2]
    half = width - 2
    stack = padded(species, 8)
    count = lax.axis_size("yz")
    me = lax.axis_index("yz")
    pos, owner = box_pos[0], box_owner[0]
    table = tables(width, pos.shape[1])
    coef = diffusion[None]
    c = jnp.transpose(coarse_state, (1, 2, 0, 3))

    fine = jnp.transpose(fine_state, (1, 0, 2))
    near, far, own, *others = pack_y(c, fine)
    x_high = pack_x(c, own, c.shape[0] - 1)
    x_low = pack_x(c, x_high, 0)
    halos = [
        lax.ppermute(x_high, "gx", ring("gx", 1)),
        lax.ppermute(x_low, "gx", ring("gx", -1)),
        lax.ppermute(near, "yz", mutual("yz", 1)),
        lax.ppermute(far, "yz", mutual("yz", -1)),
    ]
    if relays(count):
        after = passed = relay(halos[2], x_low, width, *own.shape)
        others = [lax.ppermute(passed, "yz", mutual("yz", -1))]
    else:
        after = x_low
        others = [lax.ppermute(slot, "yz", ring("yz", 2 + k)) for k, slot in enumerate(others)]

    adv, old, new, mix, spread, ghost = coarse_part(
        pos, c, rate, coef, table, stack, after
    )
    from_y, start, ghosts = y_faces(pos, owner, *halos[2:], own, old, new, spread, half, stack)
    made = fine_part(
        pos, owner, *halos[:2], start, others, mix, coef, ghosts, ghost, from_y, 2 * half
    )
    packets, (mid, kept, field) = made[:count], made[count:]

    def swap(value, k):
        even = count & (count - 1) == 0
        pairs = [(i, i ^ k if even else (i + k) % count) for i in range(count)]
        return lax.ppermute(value, "yz", pairs)

    back = [packets[0]] + [swap(packets[k], k) for k in range(1, count)]
    coarse_next = correct(pos, adv, halos, coef, field, kept, mid, old, new, spread, table, half)

    fine_next = jnp.transpose(unpack(back), (1, 0, 2))
    return jnp.transpose(coarse_next, (2, 0, 1, 3)), fine_next


def solution(mesh):
    in_specs = (
        P(None, "gx", "yz", None),
        P(("gx", "yz"), None, None),
        P(),
        P(),
        P("gx", "yz", None),
        P("gx", "yz", None),
    )
    out_specs = (P(None, "gx", "yz", None), P(("gx", "yz"), None, None))
    return jax.shard_map(local, mesh=mesh, in_specs=in_specs, out_specs=out_specs, check_vma=False)
```
